32 devices in a mesh: freq: 2 (over y), tile: 8 (over z, x), src: 2 (over core).
Axes of the slice: x: 2, y: 2, z: 4, core: 2. Of those that a mesh axis runs over, the one named last changes fastest.
Arguments:
- green: bfloat16 [2, 4096, 1024], P(None, ('freq', 'tile'), 'src'), parts along dimension 1, may hold values from -0.1875 to 0.1875
- direction: bfloat16 [2, 2048, 1024], P(None, ('freq', 'src')), parts along dimension 1, may hold values from -6 to 6
- partners: int32 [32, 8], P(('freq', 'tile')), parts along dimension 0, may hold values from 0 to 15, as said below
- counts: int32 [32], P(('freq', 'tile')), parts along dimension 0, may hold values from 1 to 8, as said below
Outputs:
- hessian: float32 [2048, 2, 1024], P(('freq', 'tile'), None, 'src'), parts along dimension 0
The draws below stay inside these ranges and needn't reach their ends.
There are 2 independent parts, one for each index of `freq`. The reference program is written for one: setup_inputs(seed, part) draws one part's arguments, and reference() takes and returns one part's arrays. A program takes and returns all parts, laid end to end along the dimension named above; each array names one. Nothing has to cross between parts.
Inputs may be any that keep to these rules, and one draw needn't show every extreme that they name: The entries partners[t, k] of a row are distinct tile indices u with |u // 2 - t // 2| <= 3; only those with k < counts[t] are sampled. `counts`: some tile row has all 8 slots sampled, and some tile row has only one.
All inputs are finite; a program needn't handle non-finite values.
Results may differ from the reference program's by a relative error of at most 0.0016.
Values may be sent and summed in bfloat16 or wider, within the bound.
No kernel may reach another device: no remote copies, remote signals or barrier semaphores. Data moves between devices by JAX's collectives and lax.ppermute only.
A program may use at most 64 MiB of HBM per device.

```python
import jax
import jax.numpy as jnp
from jax import lax

TILE = 128
SRC = 1024
TILE_DEV = 2
BAND_DEV = 3
TILES = 16
SENSORS = 2048
KMAX = 8


def pattern_tables(key):
    base_key = jax.random.fold_in(key, 4711)
    key_score, key_left, key_right, key_top, key_bottom = jax.random.split(base_key, 5)
    width = (2 * BAND_DEV + 1) * TILE_DEV
    rows = jnp.arange(TILES, dtype=jnp.int32)
    first = (rows // TILE_DEV - BAND_DEV) * TILE_DEV
    candidate = first[:, None] + jnp.arange(width, dtype=jnp.int32)[None, :]
    inside = (candidate >= 0) & (candidate < TILES)
    score = jax.random.randint(key_score, (TILES, width), 0, 2 ** 20, dtype=jnp.int32) * width
    score = score + jnp.arange(width, dtype=jnp.int32)[None, :]
    score = jnp.where(inside, score, score + 2 ** 26)
    order = jnp.argsort(score, axis=1, stable=True)[:, :KMAX]
    partner_table = jnp.take_along_axis(candidate, order, axis=1).astype(jnp.int32)
    left = jax.random.randint(key_left, (TILES,), 0, KMAX, dtype=jnp.int32)
    right = jax.random.randint(key_right, (TILES,), 0, KMAX, dtype=jnp.int32)
    count_table = jnp.maximum(1, KMAX - left * right // (KMAX - 1))
    top = jax.random.randint(key_top, (), 0, TILES, dtype=jnp.int32)
    bottom = (top + 1 + jax.random.randint(key_bottom, (), 0, TILES - 1, dtype=jnp.int32)) % TILES
    count_table = jnp.where(rows == top, KMAX, count_table)
    count_table = jnp.where(rows == bottom, 1, count_table).astype(jnp.int32)
    return (partner_table, count_table)


def draw_partners(key, part):
    return pattern_tables(key)[0]


def draw_counts(key, part):
    return pattern_tables(key)[1]


def levels(rng, extent, cuts, smallest, largest):
    def one(dim, shards_of):
        draws = jax.random.uniform(jax.random.fold_in(jax.random.fold_in(rng, 6), dim), (shards_of,), jnp.float32, smallest / len(cuts), largest / len(cuts))
        return jnp.repeat(jnp.exp(draws), extent[dim] // shards_of).reshape((-1,) + (1,) * (len(extent) - dim - 1))

    loudness = one(*cuts[0])
    for cut in cuts[1:]:
        loudness = loudness * one(*cut)
    return loudness


def noise(key, dims, scale, reach, cuts=(), kind=jnp.bfloat16):
    loudness = levels(key, dims, cuts, -0.22, 0.18) if cuts else 1.0
    array = jax.random.normal(key, dims, jnp.float32) * scale * loudness
    return jnp.minimum(jnp.maximum(array, -reach), reach).astype(kind)


def setup_inputs(seed: int = 0, part: int = 0) -> dict:
    key_of = jax.random.split(jax.random.key(seed), 5)
    part_splits = jax.random.split(jax.random.fold_in(key_of[4], part), 5)
    green = noise(part_splits[0], (2, SENSORS, SRC), SRC ** -0.5, 0.1875, ((1, 8), (2, 2)))
    direction = noise(part_splits[1], (2, SRC, SRC), 1.0, 6.0, ((1, 2),))
    partners = draw_partners(jax.random.fold_in(jax.random.fold_in(key_of[4], part), 71), part)
    counts = draw_counts(jax.random.fold_in(jax.random.fold_in(key_of[4], part), 71), part)
    return {"green": green, "direction": direction, "partners": partners, "counts": counts}


def reference(green, direction, partners, counts):
    sources = green.shape[2]
    tiles = green.reshape(2, TILES, TILE, sources)
    live = (jnp.arange(KMAX, dtype=jnp.int32)[None, :] < counts[:, None]).astype(jnp.float32)

    def visit(total, index):
        own = lax.dynamic_index_in_dim(tiles, index, 1, keepdims=False)
        image_real = (jnp.dot(own[0], direction[0], preferred_element_type=jnp.float32)
                      - jnp.dot(own[1], direction[1], preferred_element_type=jnp.float32)).astype(jnp.bfloat16)
        image_imag = (jnp.dot(own[0], direction[1], preferred_element_type=jnp.float32)
                      + jnp.dot(own[1], direction[0], preferred_element_type=jnp.float32)).astype(jnp.bfloat16)
        stack = jnp.take(tiles, partners[index].astype(jnp.int32), axis=1).reshape(2, KMAX * TILE, sources)
        mask = jnp.repeat(live[index], TILE)[None, :]
        couple_real = (jnp.dot(image_real, stack[0].T, preferred_element_type=jnp.float32)
                       + jnp.dot(image_imag, stack[1].T, preferred_element_type=jnp.float32))
        couple_imag = (jnp.dot(image_imag, stack[0].T, preferred_element_type=jnp.float32)
                       - jnp.dot(image_real, stack[1].T, preferred_element_type=jnp.float32))
        couple_real = (couple_real * mask).astype(jnp.bfloat16)
        couple_imag = (couple_imag * mask).astype(jnp.bfloat16)
        weight_real = (jnp.dot(couple_real, stack[0], preferred_element_type=jnp.float32)
                       - jnp.dot(couple_imag, stack[1], preferred_element_type=jnp.float32)).astype(jnp.bfloat16)
        weight_imag = (jnp.dot(couple_real, stack[1], preferred_element_type=jnp.float32)
                       + jnp.dot(couple_imag, stack[0], preferred_element_type=jnp.float32)).astype(jnp.bfloat16)
        out_real = (jnp.dot(own[0].T, weight_real, preferred_element_type=jnp.float32)
                    + jnp.dot(own[1].T, weight_imag, preferred_element_type=jnp.float32))
        out_imag = (jnp.dot(own[0].T, weight_imag, preferred_element_type=jnp.float32)
                    - jnp.dot(own[1].T, weight_real, preferred_element_type=jnp.float32))
        return total + jnp.stack([out_real, out_imag], axis=1), None

    start = jnp.zeros((sources, 2, sources), jnp.float32)
    total, _ = lax.scan(visit, start, jnp.arange(TILES, dtype=jnp.int32))
    return total
```

```python
import functools

import jax
import jax.numpy as jnp
from jax import lax
from jax.experimental import pallas as pl
from jax.experimental.pallas import tpu as pltpu
from jax.sharding import PartitionSpec as P

F32 = jnp.float32
BF16 = jnp.bfloat16
NOWHERE = -1000
PAD_ROWS = 16
VMEM_LIMIT = 40 * 1024 * 1024


def move(value, target):
    count = lax.axis_size("tile")
    pairs = [(source, target(source)) for source in range(count) if 0 <= target(source) < count]
    return lax.ppermute(value, "tile", pairs)


def cores(value):
    return lax.ppermute(value, "src", [(0, 1), (1, 0)])


def dot(a, b):
    return jnp.dot(a, b, preferred_element_type=F32)


def dot_t(a, b):
    return lax.dot_general(a, b, (((1,), (1,)), ((), ())), preferred_element_type=F32)


def images_kernel(core_ref, a_own, a_other, v_own, v_other, left_own, left_other):
    rows = a_own.shape[1]
    half = a_own.shape[2]
    core = core_ref[0]
    for column, out in ((core, left_own), (1 - core, left_other)):
        cols = pl.ds(pl.multiple_of(column * half, half), half)
        real = jnp.zeros((rows, half), F32)
        imag = jnp.zeros((rows, half), F32)
        for a, v in ((a_own, v_own), (a_other, v_other)):
            v_real, v_imag = v[0, :, cols], v[1, :, cols]
            real += dot(a[0], v_real) - dot(a[1], v_imag)
            imag += dot(a[0], v_imag) + dot(a[1], v_real)
        real = real.astype(BF16)
        imag = imag.astype(BF16)
        out[:rows, :half] = real
        out[:rows, half:] = imag
        out[rows:, :half] = imag
        out[rows:, half:] = -real


def window_kernel(blocks, start, last, mask_ref, left_own, left_other, *refs):
    a_refs = refs[: 2 * blocks]
    refs = refs[2 * blocks :]
    rows2, half = left_own.shape[0], left_own.shape[1] // 2
    rows = rows2 // 2
    tiles = mask_ref.shape[2]
    tile = rows // tiles
    if start:
        sums = [None, None]
    else:
        sums = [refs[0][...], refs[1][...]]
        refs = refs[2:]
    for block in range(blocks):
        a_own, a_other = a_refs[2 * block], a_refs[2 * block + 1]
        couple = (
            dot_t(left_own[:, :half], a_own[0])
            + dot_t(left_own[:, half:], a_own[1])
            + dot_t(left_other[:, :half], a_other[0])
            + dot_t(left_other[:, half:], a_other[1])
        )
        row_tile = lax.broadcasted_iota(jnp.int32, couple.shape, 0) // tile % tiles
        col_tile = lax.broadcasted_iota(jnp.int32, couple.shape, 1) // tile
        keep = jnp.zeros(couple.shape, F32)
        for r in range(tiles):
            for c in range(tiles):
                keep = jnp.where(
                    jnp.logical_and(row_tile == r, col_tile == c), mask_ref[block, r, c], keep
                )
        couple = (couple * keep).astype(BF16)
        turned = jnp.concatenate([-couple[rows:], couple[:rows]], axis=0)
        for index, a in enumerate((a_own, a_other)):
            term = dot(couple, a[0]) + dot(turned, a[1])
            sums[index] = term if sums[index] is None else sums[index] + term
    for out, total in zip(refs, sums):
        out[...] = total.astype(BF16) if last else total


def window_call(mask, left, groups, sums, last):
    args = [mask, *left]
    for pair in groups:
        args.extend(pair)
    if sums is not None:
        args.extend(sums)
    rows2, half = left[0].shape[0], left[0].shape[1] // 2
    vmem = pl.BlockSpec(memory_space=pltpu.VMEM)
    specs = [pl.BlockSpec(memory_space=pltpu.SMEM)] + [vmem] * (len(args) - 1)
    out = jax.ShapeDtypeStruct((rows2, half), BF16 if last else F32)
    return pl.pallas_call(
        functools.partial(window_kernel, len(groups), sums is None, last),
        out_shape=(out, out),
        in_specs=specs,
        out_specs=(vmem, vmem),
        compiler_params=pltpu.CompilerParams(vmem_limit_bytes=VMEM_LIMIT),
        cost_estimate=pl.CostEstimate(
            flops=len(groups) * 2 * 2 * rows2 * half * rows2 * 2,
            bytes_accessed=sum(a.size * a.dtype.itemsize for a in args[1:]) + 2 * rows2 * half * 4,
            transcendentals=0,
        ),
    )(*args)


def outer_kernel(planes, a_ref, w_own, w_other, *outs):
    rows = w_own.shape[0] // 2
    half = w_own.shape[1]
    rows2 = 2 * rows
    block = a_ref.shape[0] // planes
    for plane in range(planes):
        a = a_ref[plane * block : (plane + 1) * block, :]
        real = dot(a[:, :rows2], w_own[...]) + dot(a[:, rows2:], w_other[...])
        imag = (
            dot(a[:, :rows], w_own[rows:, :])
            - dot(a[:, rows:rows2], w_own[:rows, :])
            + dot(a[:, rows2 : rows2 + rows], w_other[rows:, :])
            - dot(a[:, rows2 + rows :], w_other[:rows, :])
        )
        out = outs[plane]
        if plane:
            top = jnp.maximum(jnp.max(jnp.abs(real)), jnp.max(jnp.abs(imag)))
            power = 14.0 - jnp.ceil(jnp.log2(jnp.full((PAD_ROWS, half), jnp.maximum(top, 1e-30), F32)))
            power = jnp.clip(power, -110.0, 110.0)
            scale = jnp.exp2(power)[:1]
            out[: block, :] = real * scale
            out[block : 2 * block, :] = imag * scale
            out[2 * block :, :] = power
        else:
            out[: block, :] = real
            out[block :, :] = imag


def shards(green, direction, partners, counts):
    tile_dev, kmax = partners.shape
    rows, half = green.shape[1:]
    count = lax.axis_size("tile")
    planes = count // 2
    place = lax.axis_index("tile")
    side, plane = place % 2, place // 2
    core = lax.axis_index("src")
    left_side = side == 0

    swap = lambda index: index ^ 1
    down = lambda index: index - 2
    up = lambda index: index + 2

    green_other = cores(green)
    direction_other = cores(direction)
    table = jnp.concatenate([partners, counts[:, None]], axis=1)

    mate = move(green, swap)
    above = move(green, down)
    below = move(green, up)
    table_mate = move(table, swap)
    mate_other = cores(mate)
    above_other = cores(above)
    below_other = cores(below)

    down_two = move(
        jnp.where(left_side & (plane < planes - 1), above, mate), down
    )
    up_two = move(
        jnp.where((side == 1) & (plane > 0), below, mate), up
    )
    down_two_other = cores(down_two)
    up_two_other = cores(up_two)

    near_left = plane >= 2
    near_right = plane <= planes - 3
    group = lambda p, s: 2 * p + s
    first_groups = [
        group(plane, side),
        group(plane, 1 - side),
        group(plane + 1, side),
        group(plane - 1, side),
    ]
    second_groups = [
        jnp.where(
            left_side,
            jnp.where(plane + 1 == planes - 1, group(plane + 1, 1), group(plane + 2, 0)),
            group(plane + 1, 0),
        ),
        jnp.where(
            left_side,
            group(plane - 1, 1),
            jnp.where(plane == 1, group(0, 0), group(plane - 2, 1)),
        ),
    ]
    third = []
    third_groups = []
    if planes <= 4:
        send = jnp.where(
            left_side, jnp.where(near_left, below, down_two), jnp.where(near_right, above, up_two)
        )
        third.append(move(send, swap))
        third_groups.append(
            jnp.where(
                left_side,
                jnp.where(
                    near_right,
                    group(plane + 1, 1),
                    jnp.where(near_left, group(plane - 2, 1), NOWHERE),
                ),
                jnp.where(
                    near_left,
                    group(plane - 1, 0),
                    jnp.where(near_right, group(plane + 2, 0), NOWHERE),
                ),
            )
        )
    else:
        third.append(move(jnp.where(left_side, below, above), swap))
        third_groups.append(
            jnp.where(
                left_side,
                jnp.where(near_right, group(plane + 1, 1), NOWHERE),
                jnp.where(near_left, group(plane - 1, 0), NOWHERE),
            )
        )
        third.append(move(jnp.where(left_side, down_two, up_two), swap))
        third_groups.append(
            jnp.where(
                left_side,
                jnp.where(near_left, group(plane - 2, 1), NOWHERE),
                jnp.where(near_right, group(plane + 2, 0), NOWHERE),
            )
        )
    third_other = [cores(block) for block in third]

    mine = side == core
    table_here = jnp.where(mine, table, table_mate)
    slots = jnp.arange(kmax, dtype=jnp.int32)[None, :]
    sampled = jnp.where(slots < table_here[:, kmax:], table_here[:, :kmax], NOWHERE * 4)
    ids = jnp.stack(first_groups + second_groups + third_groups).astype(jnp.int32)
    ids = ids[:, None] * tile_dev + jnp.arange(tile_dev, dtype=jnp.int32)[None, :]
    mask = jnp.any(sampled[None, :, None, :] == ids[:, None, :, None], axis=3).astype(F32)

    rows_own = jnp.where(mine, green, mate)
    rows_other = jnp.where(mine, green_other, mate_other)
    vmem = pl.BlockSpec(memory_space=pltpu.VMEM)
    smem = pl.BlockSpec(memory_space=pltpu.SMEM)
    left_shape = jax.ShapeDtypeStruct((2 * rows, 2 * half), BF16)
    left = pl.pallas_call(
        images_kernel,
        out_shape=(left_shape, left_shape),
        in_specs=[smem, vmem, vmem, vmem, vmem],
        out_specs=(vmem, vmem),
        compiler_params=pltpu.CompilerParams(vmem_limit_bytes=VMEM_LIMIT),
        cost_estimate=pl.CostEstimate(
            flops=2 * 4 * rows * 4 * half * half, bytes_accessed=8 * 1024 * 1024, transcendentals=0
        ),
    )(core.reshape(1).astype(jnp.int32), rows_own, rows_other, direction, direction_other)

    here, far = len(first_groups), len(first_groups) + len(second_groups)
    sums = window_call(
        mask[:here],
        left,
        [(green, green_other), (mate, mate_other), (above, above_other), (below, below_other)],
        None,
        False,
    )
    sums = window_call(
        mask[here:far], left, [(down_two, down_two_other), (up_two, up_two_other)], sums, False
    )
    weighted = window_call(mask[far:], left, list(zip(third, third_other)), sums, True)
    weighted_mate = cores(weighted[1])

    def whole(own, other):
        return jnp.concatenate(
            [jnp.where(core == 0, own, other), jnp.where(core == 0, other, own)], axis=2
        )

    block = 2 * half // count
    columns = jnp.stack(
        [
            whole(rows_own, rows_other),
            whole(jnp.where(mine, mate, green), jnp.where(mine, mate_other, green_other)),
        ]
    ).reshape(2, 2, rows, planes, 2, block)
    columns = lax.dynamic_index_in_dim(columns, side, 4, keepdims=False)
    columns = jnp.concatenate([columns, columns], axis=3)
    columns = lax.dynamic_slice_in_dim(columns, plane, planes, axis=3)
    columns = columns.transpose(3, 4, 0, 1, 2).reshape(planes * block, 4 * rows)

    out_shapes = [jax.ShapeDtypeStruct((2 * block, half), F32)]
    out_shapes += [jax.ShapeDtypeStruct((2 * block + PAD_ROWS, half), F32)] * (planes - 1)
    terms = pl.pallas_call(
        functools.partial(outer_kernel, planes),
        out_shape=tuple(out_shapes),
        in_specs=[vmem, vmem, vmem],
        out_specs=(vmem,) * planes,
        compiler_params=pltpu.CompilerParams(vmem_limit_bytes=VMEM_LIMIT),
        cost_estimate=pl.CostEstimate(
            flops=2 * planes * block * 4 * rows * 2 * half,
            bytes_accessed=8 * 1024 * 1024,
            transcendentals=0,
        ),
    )(columns, weighted[0], weighted_mate)
    total = terms[0]
    for distance in range(1, planes):
        sent = terms[distance].astype(jnp.float16)
        got = move(sent, lambda index: (index + 2 * distance) % count).astype(F32)
        total = total + got[: 2 * block] * jnp.exp2(-got[2 * block : 2 * block + 1])
    return jnp.stack([total[:block], total[block:]], axis=1)


def solution(mesh):
    in_specs = (
        P(None, ("freq", "tile"), "src"),
        P(None, ("freq", "src"), None),
        P(("freq", "tile"), None),
        P(("freq", "tile")),
    )
    out_specs = P(("freq", "tile"), None, "src")
    return jax.shard_map(shards, mesh=mesh, in_specs=in_specs, out_specs=out_specs, check_vma=False)
```

```python
import functools

import jax
import jax.numpy as jnp
from jax import lax
from jax.experimental import pallas as pl
from jax.experimental.pallas import tpu as pltpu
from jax.sharding import PartitionSpec as P

F32 = jnp.float32
BF16 = jnp.bfloat16
NOWHERE = -1000
PAD_ROWS = 16
VMEM_LIMIT = 24 * 1024 * 1024


def move(value, target):
    count = lax.axis_size("tile")
    pairs = [(source, target(source)) for source in range(count) if 0 <= target(source) < count]
    return lax.ppermute(value, "tile", pairs)


def cores(value):
    return lax.ppermute(value, "src", [(0, 1), (1, 0)])


def dot(a, b):
    return jnp.dot(a, b, preferred_element_type=F32)


def dot_t(a, b):
    return lax.dot_general(a, b, (((1,), (1,)), ((), ())), preferred_element_type=F32)


def images_kernel(core_ref, a_own, a_other, v_own, v_other, left):
    rows, half = a_own.shape[1:]
    core = core_ref[0]
    real = [a_own[0], -a_own[1], a_other[0], -a_other[1]]
    imag = [a_own[1], a_own[0], a_other[1], a_other[0]]
    sensors = jnp.concatenate(
        [jnp.concatenate(real, axis=1), jnp.concatenate(imag, axis=1)], axis=0
    )
    for index, column in enumerate((core, 1 - core)):
        cols = pl.ds(pl.multiple_of(column * half, half), half)
        values = jnp.concatenate(
            [v_own[0, :, cols], v_own[1, :, cols], v_other[0, :, cols], v_other[1, :, cols]], axis=0
        )
        images = dot(sensors, values).astype(BF16)
        at = 2 * index * half
        left[:, at : at + half] = images
        left[:rows, at + half : at + 2 * half] = images[rows:]
        left[rows:, at + half : at + 2 * half] = -images[:rows]


def window_kernel(blocks, start, last, mask_ref, left, *refs):
    a_refs = refs[: 2 * blocks]
    refs = refs[2 * blocks :]
    rows, half = left.shape[0] // 2, left.shape[1] // 4
    tiles = mask_ref.shape[2]
    tile = rows // tiles
    couples = refs[-1]
    refs = refs[:-1]
    for block in range(blocks):
        a_own, a_other = a_refs[2 * block], a_refs[2 * block + 1]
        partner = jnp.concatenate([a_own[0], a_own[1], a_other[0], a_other[1]], axis=1)
        couple = dot_t(left[...], partner)
        at = 2 * block * rows
        for r in range(tiles):
            for c in range(tiles):
                keep = mask_ref[block, r, c]
                upper = slice(r * tile, (r + 1) * tile)
                lower = slice(rows + r * tile, rows + (r + 1) * tile)
                real = (couple[upper, c * tile : (c + 1) * tile] * keep).astype(BF16)
                imag = (couple[lower, c * tile : (c + 1) * tile] * keep).astype(BF16)
                first = slice(at + c * tile, at + (c + 1) * tile)
                second = slice(at + rows + c * tile, at + rows + (c + 1) * tile)
                couples[upper, first] = real
                couples[lower, first] = imag
                couples[upper, second] = -imag
                couples[lower, second] = real
    for index in range(2):
        values = jnp.concatenate(
            [a_refs[2 * block + index][part] for block in range(blocks) for part in range(2)], axis=0
        )
        total = dot(couples[...], values)
        if not start:
            total += refs[index][...]
        out = refs[index if start else index + 2]
        out[...] = total.astype(BF16) if last else total


def window_call(mask, left, groups, sums, last):
    args = [mask, left]
    for pair in groups:
        args.extend(pair)
    if sums is not None:
        args.extend(sums)
    rows2, half = left.shape[0], left.shape[1] // 4
    vmem = pl.BlockSpec(memory_space=pltpu.VMEM)
    specs = [pl.BlockSpec(memory_space=pltpu.SMEM)] + [vmem] * (len(args) - 1)
    out = jax.ShapeDtypeStruct((rows2, half), BF16 if last else F32)
    return pl.pallas_call(
        functools.partial(window_kernel, len(groups), sums is None, last),
        out_shape=(out, out),
        in_specs=specs,
        out_specs=(vmem, vmem),
        scratch_shapes=[pltpu.VMEM((rows2, len(groups) * rows2), BF16)],
        compiler_params=pltpu.CompilerParams(vmem_limit_bytes=VMEM_LIMIT),
        cost_estimate=pl.CostEstimate(
            flops=len(groups) * 2 * 2 * rows2 * half * rows2 * 2,
            bytes_accessed=sum(a.size * a.dtype.itemsize for a in args[1:]) + 2 * rows2 * half * 4,
            transcendentals=0,
        ),
    )(*args)


def pick_kernel(flag_ref, *refs):
    outs = refs[len(refs) * 2 // 3 :]
    for index, out in enumerate(outs):

        @pl.when(flag_ref[index] == 1)
        def _():
            out[...] = refs[2 * index][...]

        @pl.when(flag_ref[index] != 1)
        def _():
            out[...] = refs[2 * index + 1][...]


def pick(*choices):
    flags = jnp.stack([flag for flag, _, _ in choices]).astype(jnp.int32)
    args = [value for choice in choices for value in choice[1:]]
    vmem = pl.BlockSpec(memory_space=pltpu.VMEM)
    out = jax.ShapeDtypeStruct(args[0].shape, args[0].dtype)
    return pl.pallas_call(
        pick_kernel,
        out_shape=(out,) * len(choices),
        in_specs=[pl.BlockSpec(memory_space=pltpu.SMEM)] + [vmem] * len(args),
        out_specs=(vmem,) * len(choices),
        compiler_params=pltpu.CompilerParams(vmem_limit_bytes=VMEM_LIMIT),
    )(flags, *args)


def columns_kernel(planes, block, place_ref, *refs):
    out = refs[-1]
    plane, side, core = place_ref[0], place_ref[1], place_ref[2]
    rows, half = refs[0].shape[1:]
    for distance in range(planes):
        owner = 2 * lax.rem(plane + distance, planes) + side
        at = owner * block
        own = at // half == core
        cols = pl.ds(pl.multiple_of(lax.rem(at, half), block), block)
        for group in range(2):
            for part in range(2):
                value = jnp.where(own, refs[2 * group][part, :, cols], refs[2 * group + 1][part, :, cols])
                start = (2 * group + part) * rows
                out[distance * block : (distance + 1) * block, start : start + rows] = value.T


def outer_kernel(planes, a_ref, w_own, w_other, *outs):
    rows = w_own.shape[0] // 2
    half = w_own.shape[1]
    rows2 = 2 * rows
    block = a_ref.shape[0] // planes
    for plane in range(planes):
        a = a_ref[plane * block : (plane + 1) * block, :]
        real = dot(a[:, :rows2], w_own[...]) + dot(a[:, rows2:], w_other[...])
        imag = (
            dot(a[:, :rows], w_own[rows:, :])
            - dot(a[:, rows:rows2], w_own[:rows, :])
            + dot(a[:, rows2 : rows2 + rows], w_other[rows:, :])
            - dot(a[:, rows2 + rows :], w_other[:rows, :])
        )
        out = outs[plane]
        if plane:
            top = jnp.maximum(jnp.max(jnp.abs(real)), jnp.max(jnp.abs(imag)))
            power = 14.0 - jnp.ceil(jnp.log2(jnp.full((PAD_ROWS, half), jnp.maximum(top, 1e-30), F32)))
            power = jnp.clip(power, -110.0, 110.0)
            scale = jnp.exp2(power)[:1]
            out[: block, :] = real * scale
            out[block : 2 * block, :] = imag * scale
            out[2 * block :, :] = power
        else:
            out[: block, :] = real
            out[block :, :] = imag


def shards(green, direction, partners, counts):
    tile_dev, kmax = partners.shape
    rows, half = green.shape[1:]
    count = lax.axis_size("tile")
    planes = count // 2
    place = lax.axis_index("tile")
    side, plane = place % 2, place // 2
    core = lax.axis_index("src")
    left_side = side == 0
    vmem = pl.BlockSpec(memory_space=pltpu.VMEM)
    smem = pl.BlockSpec(memory_space=pltpu.SMEM)
    params = pltpu.CompilerParams(vmem_limit_bytes=VMEM_LIMIT)
    last_plane = planes - 1

    mate = move(green, lambda i: i ^ 1)
    above = move(green, lambda i: i - 2)
    below = move(green, lambda i: i + 2)
    green_other = cores(green)
    direction_other = cores(direction)
    table = jnp.concatenate([partners, counts[:, None]], axis=1)
    table_mate = move(table, lambda i: i ^ 1)
    mate_other = cores(mate)
    above_other = cores(above)
    below_other = cores(below)

    def from_above(index):
        return index - 2

    def from_below(index):
        return index + 2

    down_far, up_far = pick(
        (left_side & (plane < last_plane), above, mate), ((side == 1) & (plane > 0), below, mate)
    )
    down = move(down_far, from_above)
    up = move(up_far, from_below)

    near_left = plane >= 2
    near_right = plane <= planes - 3

    def group(p, s):
        return 2 * p + s

    first_groups = [
        group(plane, side),
        group(plane, 1 - side),
        group(plane + 1, side),
        group(plane - 1, side),
    ]
    second_groups = [
        jnp.where(
            left_side,
            jnp.where(plane + 1 == last_plane, group(plane + 1, 1), group(plane + 2, 0)),
            group(plane + 1, 0),
        ),
        jnp.where(
            left_side,
            group(plane - 1, 1),
            jnp.where(plane == 1, group(0, 0), group(plane - 2, 1)),
        ),
    ]
    far_groups = []
    near_group = jnp.where(
        left_side,
        jnp.where(near_right, group(plane + 1, 1), NOWHERE),
        jnp.where(near_left, group(plane - 1, 0), NOWHERE),
    )
    far_group = jnp.where(
        left_side,
        jnp.where(near_left, group(plane - 2, 1), NOWHERE),
        jnp.where(near_right, group(plane + 2, 0), NOWHERE),
    )

    mine = side == core
    table_here = jnp.where(mine, table, table_mate)
    slots = jnp.arange(kmax, dtype=jnp.int32)[None, :]
    sampled = jnp.where(slots < table_here[:, kmax:], table_here[:, :kmax], NOWHERE * 4)
    ids = jnp.stack(first_groups + second_groups + [near_group, far_group]).astype(jnp.int32)
    ids = ids[:, None] * tile_dev + jnp.arange(tile_dev, dtype=jnp.int32)[None, :]
    mask = jnp.any(sampled[None, :, None, :] == ids[:, None, :, None], axis=3).astype(F32)

    (near_sent,) = pick((left_side, below, above))
    near = move(near_sent, lambda i: i ^ 1)
    rows_own, rows_other, rest_own, rest_other = pick(
        (mine, green, mate), (mine, green_other, mate_other), (mine, mate, green), (mine, mate_other, green_other)
    )
    left = pl.pallas_call(
        images_kernel,
        out_shape=jax.ShapeDtypeStruct((2 * rows, 4 * half), BF16),
        in_specs=[smem, vmem, vmem, vmem, vmem],
        out_specs=vmem,
        compiler_params=params,
        cost_estimate=pl.CostEstimate(
            flops=2 * 4 * rows * 4 * half * half, bytes_accessed=8 * 1024 * 1024, transcendentals=0
        ),
    )(core.reshape(1).astype(jnp.int32), rows_own, rows_other, direction, direction_other)

    block = 2 * half // count
    if block % 128 == 0:
        columns = pl.pallas_call(
            functools.partial(columns_kernel, planes, block),
            out_shape=jax.ShapeDtypeStruct((planes * block, 4 * rows), BF16),
            in_specs=[smem, vmem, vmem, vmem, vmem],
            out_specs=vmem,
            compiler_params=params,
        )(jnp.stack([plane, side, core]).astype(jnp.int32), rows_own, rows_other, rest_own, rest_other)
    else:

        def whole(own, other):
            return jnp.concatenate(
                [jnp.where(core == 0, own, other), jnp.where(core == 0, other, own)], axis=2
            )

        columns = jnp.stack([whole(rows_own, rows_other), whole(rest_own, rest_other)])
        columns = columns.reshape(2, 2, rows, planes, 2, block)
        columns = lax.dynamic_index_in_dim(columns, side, 4, keepdims=False)
        columns = jnp.concatenate([columns, columns], axis=3)
        columns = lax.dynamic_slice_in_dim(columns, plane, planes, axis=3)
        columns = columns.transpose(3, 4, 0, 1, 2).reshape(planes * block, 4 * rows)

    sums = window_call(
        mask[:4],
        left,
        [(green, green_other), (mate, mate_other), (above, above_other), (below, below_other)],
        None,
        False,
    )
    down, up, near, sums, columns = lax.optimization_barrier((down, up, near, sums, columns))
    (far_sent,) = pick((left_side, down, up))
    far = move(far_sent, lambda i: i ^ 1)
    sums = window_call(
        mask[4:7], left, [(down, cores(down)), (up, cores(up)), (near, cores(near))], sums, False
    )
    far, sums = lax.optimization_barrier((far, sums))
    weighted = window_call(mask[7:], left, [(far, cores(far))], sums, True)
    weighted_mate = cores(weighted[1])

    out_shapes = [jax.ShapeDtypeStruct((2 * block, half), F32)]
    out_shapes += [jax.ShapeDtypeStruct((2 * block + PAD_ROWS, half), F32)] * (planes - 1)
    terms = pl.pallas_call(
        functools.partial(outer_kernel, planes),
        out_shape=tuple(out_shapes),
        in_specs=[vmem, vmem, vmem],
        out_specs=(vmem,) * planes,
        compiler_params=params,
        cost_estimate=pl.CostEstimate(
            flops=2 * planes * block * 4 * rows * 2 * half,
            bytes_accessed=8 * 1024 * 1024,
            transcendentals=0,
        ),
    )(columns, weighted[0], weighted_mate)
    total = terms[0]
    for distance in range(1, planes):
        sent = terms[distance].astype(jnp.float16)
        got = move(sent, lambda index: (index + 2 * distance) % count).astype(F32)
        total = total + got[: 2 * block] * jnp.exp2(-got[2 * block : 2 * block + 1])
    return jnp.stack([total[:block], total[block:]], axis=1)


def solution(mesh):
    in_specs = (
        P(None, ("freq", "tile"), "src"),
        P(None, ("freq", "src"), None),
        P(("freq", "tile"), None),
        P(("freq", "tile")),
    )
    out_specs = P(("freq", "tile"), None, "src")
    return jax.shard_map(shards, mesh=mesh, in_specs=in_specs, out_specs=out_specs, check_vma=False)
```

```python
import functools

import jax
import jax.numpy as jnp
from jax import lax
from jax.experimental import pallas as pl
from jax.experimental.pallas import tpu as pltpu
from jax.sharding import PartitionSpec as P

F32 = jnp.float32
BF16 = jnp.bfloat16
NOWHERE = -1000
PAD_ROWS = 16
VMEM_LIMIT = 24 * 1024 * 1024


def move(value, target):
    count = lax.axis_size("tile")
    pairs = [(source, target(source)) for source in range(count) if 0 <= target(source) < count]
    return lax.ppermute(value, "tile", pairs)


def cores(value):
    return lax.ppermute(value, "src", [(0, 1), (1, 0)])


def dot(a, b):
    return jnp.dot(a, b, preferred_element_type=F32)


def dot_t(a, b):
    return lax.dot_general(a, b, (((1,), (1,)), ((), ())), preferred_element_type=F32)


def images_kernel(core_ref, a_own, a_other, v_own, v_other, left):
    rows, half = a_own.shape[1:]
    core = core_ref[0]
    real = [a_own[0], -a_own[1], a_other[0], -a_other[1]]
    imag = [a_own[1], a_own[0], a_other[1], a_other[0]]
    sensors = jnp.concatenate(
        [jnp.concatenate(real, axis=1), jnp.concatenate(imag, axis=1)], axis=0
    )
    for index, column in enumerate((core, 1 - core)):
        cols = pl.ds(pl.multiple_of(column * half, half), half)
        values = jnp.concatenate(
            [v_own[0, :, cols], v_own[1, :, cols], v_other[0, :, cols], v_other[1, :, cols]], axis=0
        )
        images = dot(sensors, values).astype(BF16)
        at = 2 * index * half
        left[:, at : at + half] = images
        left[:rows, at + half : at + 2 * half] = images[rows:]
        left[rows:, at + half : at + 2 * half] = -images[:rows]


def window_kernel(blocks, start, last, mask_ref, left, *refs):
    a_refs = refs[: 2 * blocks]
    refs = refs[2 * blocks :]
    rows, half = left.shape[0] // 2, left.shape[1] // 4
    tiles = mask_ref.shape[2]
    tile = rows // tiles
    couples = refs[-1]
    refs = refs[:-1]
    for block in range(blocks):
        a_own, a_other = a_refs[2 * block], a_refs[2 * block + 1]
        partner = jnp.concatenate([a_own[0], a_own[1], a_other[0], a_other[1]], axis=1)
        couple = dot_t(left[...], partner)
        at = 2 * block * rows
        for r in range(tiles):
            for c in range(tiles):
                keep = mask_ref[block, r, c]
                upper = slice(r * tile, (r + 1) * tile)
                lower = slice(rows + r * tile, rows + (r + 1) * tile)
                real = (couple[upper, c * tile : (c + 1) * tile] * keep).astype(BF16)
                imag = (couple[lower, c * tile : (c + 1) * tile] * keep).astype(BF16)
                first = slice(at + c * tile, at + (c + 1) * tile)
                second = slice(at + rows + c * tile, at + rows + (c + 1) * tile)
                couples[upper, first] = real
                couples[lower, first] = imag
                couples[upper, second] = -imag
                couples[lower, second] = real
    for index in range(2):
        values = jnp.concatenate(
            [a_refs[2 * block + index][part] for block in range(blocks) for part in range(2)], axis=0
        )
        total = dot(couples[...], values)
        if not start:
            total += refs[index][...]
        out = refs[index if start else index + 2]
        out[...] = total.astype(BF16) if last else total


def window_call(mask, left, groups, sums, last):
    args = [mask, left]
    for pair in groups:
        args.extend(pair)
    if sums is not None:
        args.extend(sums)
    rows2, half = left.shape[0], left.shape[1] // 4
    vmem = pl.BlockSpec(memory_space=pltpu.VMEM)
    specs = [pl.BlockSpec(memory_space=pltpu.SMEM)] + [vmem] * (len(args) - 1)
    out = jax.ShapeDtypeStruct((rows2, half), BF16 if last else F32)
    return pl.pallas_call(
        functools.partial(window_kernel, len(groups), sums is None, last),
        out_shape=(out, out),
        in_specs=specs,
        out_specs=(vmem, vmem),
        scratch_shapes=[pltpu.VMEM((rows2, len(groups) * rows2), BF16)],
        compiler_params=pltpu.CompilerParams(vmem_limit_bytes=VMEM_LIMIT),
        cost_estimate=pl.CostEstimate(
            flops=len(groups) * 2 * 2 * rows2 * half * rows2 * 2,
            bytes_accessed=sum(a.size * a.dtype.itemsize for a in args[1:]) + 2 * rows2 * half * 4,
            transcendentals=0,
        ),
    )(*args)


def pick_kernel(flag_ref, *refs):
    outs = refs[len(refs) * 2 // 3 :]
    for index, out in enumerate(outs):

        @pl.when(flag_ref[index] == 1)
        def _():
            out[...] = refs[2 * index][...]

        @pl.when(flag_ref[index] != 1)
        def _():
            out[...] = refs[2 * index + 1][...]


def pick(*choices):
    flags = jnp.stack([flag for flag, _, _ in choices]).astype(jnp.int32)
    args = [value for choice in choices for value in choice[1:]]
    vmem = pl.BlockSpec(memory_space=pltpu.VMEM)
    out = jax.ShapeDtypeStruct(args[0].shape, args[0].dtype)
    return pl.pallas_call(
        pick_kernel,
        out_shape=(out,) * len(choices),
        in_specs=[pl.BlockSpec(memory_space=pltpu.SMEM)] + [vmem] * len(args),
        out_specs=(vmem,) * len(choices),
        compiler_params=pltpu.CompilerParams(vmem_limit_bytes=VMEM_LIMIT),
    )(flags, *args)


def columns_kernel(planes, block, place_ref, *refs):
    out = refs[-1]
    plane, side, core = place_ref[0], place_ref[1], place_ref[2]
    rows, half = refs[0].shape[1:]
    for distance in range(planes):
        owner = 2 * lax.rem(plane + distance, planes) + side
        at = owner * block
        own = at // half == core
        cols = pl.ds(pl.multiple_of(lax.rem(at, half), block), block)
        for group in range(2):
            for part in range(2):
                value = jnp.where(own, refs[2 * group][part, :, cols], refs[2 * group + 1][part, :, cols])
                start = (2 * group + part) * rows
                out[distance * block : (distance + 1) * block, start : start + rows] = value.T


def outer_kernel(planes, a_ref, w_own, w_other, *outs):
    rows = w_own.shape[0] // 2
    half = w_own.shape[1]
    rows2 = 2 * rows
    block = a_ref.shape[0] // planes
    for plane in range(planes):
        a = a_ref[plane * block : (plane + 1) * block, :]
        real = dot(a[:, :rows2], w_own[...]) + dot(a[:, rows2:], w_other[...])
        imag = (
            dot(a[:, :rows], w_own[rows:, :])
            - dot(a[:, rows:rows2], w_own[:rows, :])
            + dot(a[:, rows2 : rows2 + rows], w_other[rows:, :])
            - dot(a[:, rows2 + rows :], w_other[:rows, :])
        )
        out = outs[plane]
        if plane:
            top = jnp.maximum(jnp.max(jnp.abs(real)), jnp.max(jnp.abs(imag)))
            power = 14.0 - jnp.ceil(jnp.log2(jnp.full((PAD_ROWS, half), jnp.maximum(top, 1e-30), F32)))
            power = jnp.clip(power, -110.0, 110.0)
            scale = jnp.exp2(power)[:1]
            out[: block, :] = real * scale
            out[block : 2 * block, :] = imag * scale
            out[2 * block :, :] = power
        else:
            out[: block, :] = real
            out[block :, :] = imag


def shards(green, direction, partners, counts):
    tile_dev, kmax = partners.shape
    rows, half = green.shape[1:]
    count = lax.axis_size("tile")
    planes = count // 2
    place = lax.axis_index("tile")
    side, plane = place % 2, place // 2
    core = lax.axis_index("src")
    left_side = side == 0
    vmem = pl.BlockSpec(memory_space=pltpu.VMEM)
    smem = pl.BlockSpec(memory_space=pltpu.SMEM)
    params = pltpu.CompilerParams(vmem_limit_bytes=VMEM_LIMIT)
    last_plane = planes - 1

    def odd_pair(index):
        target = (index // 2 - 1 ^ 1) + 1
        return 2 * target + index % 2 if 0 <= target < planes else -1

    direction_other = cores(direction)
    mate = move(green, lambda i: i ^ 1)
    pair = move(green, lambda i: i ^ 2)
    next_pair = move(green, odd_pair)
    green_other = cores(green)
    table = jnp.concatenate([partners, counts[:, None]], axis=1)
    table_mate = move(table, lambda i: i ^ 1)
    mate, direction_other, green_other, table_mate = lax.optimization_barrier(
        (mate, direction_other, green_other, table_mate)
    )

    odd = plane % 2 == 1
    right_side = side == 1
    pair_sent, next_sent = pick(
        (jnp.where(odd, left_side & (plane < last_plane), right_side & (plane > 0)), next_pair, mate),
        (jnp.where(odd, right_side, left_side & (plane < last_plane)), pair, mate),
    )
    pair_two = move(pair_sent, lambda i: i ^ 2)
    next_two = move(next_sent, odd_pair)
    (near_sent,) = pick((side == plane % 2, next_pair, pair))
    near = move(near_sent, lambda i: i ^ 1)
    mate_other = cores(mate)
    pair_other = cores(pair)
    next_other = cores(next_pair)

    near_left = plane >= 2
    near_right = plane <= planes - 3

    def group(p, s):
        return 2 * p + s

    first_groups = [
        group(plane, side),
        group(plane, 1 - side),
        group(jnp.where(odd, plane - 1, plane + 1), side),
        group(jnp.where(odd, plane + 1, plane - 1), side),
    ]
    from_above = jnp.where(
        left_side,
        jnp.where(plane + 1 == last_plane, group(plane + 1, 1), group(plane + 2, 0)),
        group(plane + 1, 0),
    )
    from_below = jnp.where(
        left_side,
        group(plane - 1, 1),
        jnp.where(plane == 1, group(0, 0), group(plane - 2, 1)),
    )
    second_groups = [
        jnp.where(odd, from_below, from_above),
        jnp.where(odd, from_above, from_below),
    ]
    near_group = jnp.where(
        left_side,
        jnp.where(near_right, group(plane + 1, 1), NOWHERE),
        jnp.where(near_left, group(plane - 1, 0), NOWHERE),
    )
    far_group = jnp.where(
        left_side,
        jnp.where(near_left, group(plane - 2, 1), NOWHERE),
        jnp.where(near_right, group(plane + 2, 0), NOWHERE),
    )

    mine = side == core
    table_here = jnp.where(mine, table, table_mate)
    slots = jnp.arange(kmax, dtype=jnp.int32)[None, :]
    sampled = jnp.where(slots < table_here[:, kmax:], table_here[:, :kmax], NOWHERE * 4)
    ids = jnp.stack(first_groups + second_groups + [near_group, far_group]).astype(jnp.int32)
    ids = ids[:, None] * tile_dev + jnp.arange(tile_dev, dtype=jnp.int32)[None, :]
    mask = jnp.any(sampled[None, :, None, :] == ids[:, None, :, None], axis=3).astype(F32)

    rows_own, rows_other, rest_own, rest_other = pick(
        (mine, green, mate), (mine, green_other, mate_other), (mine, mate, green), (mine, mate_other, green_other)
    )
    left = pl.pallas_call(
        images_kernel,
        out_shape=jax.ShapeDtypeStruct((2 * rows, 4 * half), BF16),
        in_specs=[smem, vmem, vmem, vmem, vmem],
        out_specs=vmem,
        compiler_params=params,
        cost_estimate=pl.CostEstimate(
            flops=2 * 4 * rows * 4 * half * half, bytes_accessed=8 * 1024 * 1024, transcendentals=0
        ),
    )(core.reshape(1).astype(jnp.int32), rows_own, rows_other, direction, direction_other)

    block = 2 * half // count
    if block % 128 == 0:
        columns = pl.pallas_call(
            functools.partial(columns_kernel, planes, block),
            out_shape=jax.ShapeDtypeStruct((planes * block, 4 * rows), BF16),
            in_specs=[smem, vmem, vmem, vmem, vmem],
            out_specs=vmem,
            compiler_params=params,
        )(jnp.stack([plane, side, core]).astype(jnp.int32), rows_own, rows_other, rest_own, rest_other)
    else:

        def whole(own, other):
            return jnp.concatenate(
                [jnp.where(core == 0, own, other), jnp.where(core == 0, other, own)], axis=2
            )

        columns = jnp.stack([whole(rows_own, rows_other), whole(rest_own, rest_other)])
        columns = columns.reshape(2, 2, rows, planes, 2, block)
        columns = lax.dynamic_index_in_dim(columns, side, 4, keepdims=False)
        columns = jnp.concatenate([columns, columns], axis=3)
        columns = lax.dynamic_slice_in_dim(columns, plane, planes, axis=3)
        columns = columns.transpose(3, 4, 0, 1, 2).reshape(planes * block, 4 * rows)

    sums = window_call(
        mask[:4],
        left,
        [(green, green_other), (mate, mate_other), (pair, pair_other), (next_pair, next_other)],
        None,
        False,
    )
    pair_two, next_two, near, sums, columns = lax.optimization_barrier(
        (pair_two, next_two, near, sums, columns)
    )
    (far_sent,) = pick((side == plane % 2, pair_two, next_two))
    far = move(far_sent, lambda i: i ^ 1)
    sums = window_call(
        mask[4:7], left, [(pair_two, cores(pair_two)), (next_two, cores(next_two)), (near, cores(near))], sums, False
    )
    far, sums = lax.optimization_barrier((far, sums))
    weighted = window_call(mask[7:], left, [(far, cores(far))], sums, True)
    weighted_mate = cores(weighted[1])

    out_shapes = [jax.ShapeDtypeStruct((2 * block, half), F32)]
    out_shapes += [jax.ShapeDtypeStruct((2 * block + PAD_ROWS, half), F32)] * (planes - 1)
    terms = pl.pallas_call(
        functools.partial(outer_kernel, planes),
        out_shape=tuple(out_shapes),
        in_specs=[vmem, vmem, vmem],
        out_specs=(vmem,) * planes,
        compiler_params=params,
        cost_estimate=pl.CostEstimate(
            flops=2 * planes * block * 4 * rows * 2 * half,
            bytes_accessed=8 * 1024 * 1024,
            transcendentals=0,
        ),
    )(columns, weighted[0], weighted_mate)
    total = terms[0]
    for distance in range(1, planes):
        sent = terms[distance].astype(jnp.float16)
        got = move(sent, lambda index: (index + 2 * distance) % count).astype(F32)
        total = total + got[: 2 * block] * jnp.exp2(-got[2 * block : 2 * block + 1])
    return jnp.stack([total[:block], total[block:]], axis=1)


def solution(mesh):
    in_specs = (
        P(None, ("freq", "tile"), "src"),
        P(None, ("freq", "src"), None),
        P(("freq", "tile"), None),
        P(("freq", "tile")),
    )
    out_specs = P(("freq", "tile"), None, "src")
    return jax.shard_map(shards, mesh=mesh, in_specs=in_specs, out_specs=out_specs, check_vma=False)
```

```python
import functools

import jax
import jax.numpy as jnp
from jax import lax
from jax.experimental import pallas as pl
from jax.experimental.pallas import tpu as pltpu
from jax.sharding import PartitionSpec as P

F32 = jnp.float32
BF16 = jnp.bfloat16
NOWHERE = -1000
PAD_ROWS = 16
VMEM_LIMIT = 24 * 1024 * 1024


def move(value, target):
    count = lax.axis_size("tile")
    pairs = [(source, target(source)) for source in range(count) if 0 <= target(source) < count]
    return lax.ppermute(value, "tile", pairs)


def cores(value):
    return lax.ppermute(value, "src", [(0, 1), (1, 0)])


def dot(a, b):
    return jnp.dot(a, b, preferred_element_type=F32)


def dot_t(a, b):
    return lax.dot_general(a, b, (((1,), (1,)), ((), ())), preferred_element_type=F32)


def parts_of(refs):
    if len(refs) == 1:
        return refs[0][0], refs[0][1]
    return refs[0][...], refs[1][...]


def images_kernel(core_ref, a_own, a_other, v_own, v_other, left):
    rows, half = a_own.shape[1] // 2, a_own.shape[2]
    core = core_ref[0]
    here = pl.ds(pl.multiple_of(core * rows, rows), rows)
    own_real, own_imag = a_own[0, here, :], a_own[1, here, :]
    other_real, other_imag = a_other[0, here, :], a_other[1, here, :]
    sensors = jnp.concatenate(
        [
            jnp.concatenate([own_real, -own_imag, other_real, -other_imag], axis=1),
            jnp.concatenate([own_imag, own_real, other_imag, other_real], axis=1),
        ],
        axis=0,
    )
    for index, column in enumerate((core, 1 - core)):
        cols = pl.ds(pl.multiple_of(column * half, half), half)
        values = jnp.concatenate(
            [v_own[0, :, cols], v_own[1, :, cols], v_other[0, :, cols], v_other[1, :, cols]], axis=0
        )
        images = dot(sensors, values).astype(BF16)
        at = 2 * index * half
        left[:, at : at + half] = images
        left[:rows, at + half : at + 2 * half] = images[rows:]
        left[rows:, at + half : at + 2 * half] = -images[:rows]


def window_kernel(widths, start, last, mask_ref, left_own, left_mate, *refs):
    blocks = []
    for width in widths:
        blocks.append((parts_of(refs[:width]), parts_of(refs[width : 2 * width])))
        refs = refs[2 * width :]
    half_rows, half = left_own.shape[0] // 2, left_own.shape[1] // 4
    rows = 2 * half_rows
    row_tiles, tiles = mask_ref.shape[1:]
    tile = rows // tiles
    couples = refs[-1]
    refs = refs[:-1]
    left = jnp.concatenate([left_own[...], left_mate[...]], axis=0)
    for block, (own, other) in enumerate(blocks):
        couple = dot_t(left, jnp.concatenate([*own, *other], axis=1))
        at = 2 * block * rows
        for r in range(row_tiles):
            for c in range(tiles):
                keep = mask_ref[block, r, c]
                begin = r * tile // half_rows * rows + r * tile % half_rows
                upper = slice(begin, begin + tile)
                lower = slice(begin + half_rows, begin + half_rows + tile)
                real = (couple[upper, c * tile : (c + 1) * tile] * keep).astype(BF16)
                imag = (couple[lower, c * tile : (c + 1) * tile] * keep).astype(BF16)
                first = slice(at + c * tile, at + (c + 1) * tile)
                second = slice(at + rows + c * tile, at + rows + (c + 1) * tile)
                couples[upper, first] = real
                couples[lower, first] = imag
                couples[upper, second] = -imag
                couples[lower, second] = real
    for index in range(2):
        values = jnp.concatenate([part for block in blocks for part in block[index]], axis=0)
        total = dot(couples[...], values)
        if not start:
            total += refs[index][...]
        out = refs[index if start else index + 2]
        out[...] = total.astype(BF16) if last else total


def window_call(mask, left, groups, sums, last):
    args = [mask, *left]
    for own, other in groups:
        args.extend(own)
        args.extend(other)
    if sums is not None:
        args.extend(sums)
    rows2, half = 2 * left[0].shape[0], left[0].shape[1] // 4
    vmem = pl.BlockSpec(memory_space=pltpu.VMEM)
    specs = [pl.BlockSpec(memory_space=pltpu.SMEM)] + [vmem] * (len(args) - 1)
    out = jax.ShapeDtypeStruct((rows2, half), BF16 if last else F32)
    return pl.pallas_call(
        functools.partial(window_kernel, [len(own) for own, _ in groups], sums is None, last),
        out_shape=(out, out),
        in_specs=specs,
        out_specs=(vmem, vmem),
        scratch_shapes=[pltpu.VMEM((rows2, len(groups) * rows2), BF16)],
        compiler_params=pltpu.CompilerParams(vmem_limit_bytes=VMEM_LIMIT),
        cost_estimate=pl.CostEstimate(
            flops=len(groups) * 2 * 2 * rows2 * half * rows2 * 2,
            bytes_accessed=sum(a.size * a.dtype.itemsize for a in args[1:]) + 2 * rows2 * half * 4,
            transcendentals=0,
        ),
    )(*args)


def pick_kernel(parts, flag_ref, *refs):
    outs = refs[len(refs) - len(parts) :]
    for index, (part, out) in enumerate(zip(parts, outs)):

        @pl.when(flag_ref[index] == 1)
        def _():
            out[...] = refs[2 * index][...] if part is None else refs[2 * index][part]

        @pl.when(flag_ref[index] != 1)
        def _():
            out[...] = refs[2 * index + 1][...] if part is None else refs[2 * index + 1][part]


def pick(*choices):
    flags = jnp.stack([choice[0] for choice in choices]).astype(jnp.int32)
    args = [value for choice in choices for value in choice[1:3]]
    parts = [choice[3] for choice in choices]
    vmem = pl.BlockSpec(memory_space=pltpu.VMEM)
    shapes = [a.shape if part is None else a.shape[1:] for a, part in zip(args[::2], parts)]
    return pl.pallas_call(
        functools.partial(pick_kernel, parts),
        out_shape=tuple(jax.ShapeDtypeStruct(shape, args[0].dtype) for shape in shapes),
        in_specs=[pl.BlockSpec(memory_space=pltpu.SMEM)] + [vmem] * len(args),
        out_specs=(vmem,) * len(choices),
        compiler_params=pltpu.CompilerParams(vmem_limit_bytes=VMEM_LIMIT),
    )(flags, *args)


def columns_kernel(planes, block, place_ref, *refs):
    out = refs[-1]
    side, core = place_ref[0], place_ref[1]
    rows, half = refs[0].shape[1] // 2, refs[0].shape[2]
    for turn in range(planes):
        at = (2 * place_ref[2 + turn] + side) * block
        own = at // half == core
        cols = pl.ds(pl.multiple_of(lax.rem(at, half), block), block)
        start = 0
        for reader in (core, 1 - core):
            here = pl.ds(pl.multiple_of(reader * rows, rows), rows)
            for group in range(2):
                for part in range(2):
                    value = jnp.where(
                        own, refs[2 * group][part, here, cols], refs[2 * group + 1][part, here, cols]
                    )
                    out[turn * block : (turn + 1) * block, start : start + rows] = value.T
                    start += rows


def outer_kernel(planes, a_ref, w_own, w_other, *outs):
    rows = w_own.shape[0] // 4
    half = w_own.shape[1]
    block = a_ref.shape[0] // planes
    straight = jnp.concatenate([w_own[...], w_other[...]], axis=0)
    turned = jnp.concatenate(
        [
            piece
            for w in (w_own, w_other)
            for at in (0, 2 * rows)
            for piece in (w[at + rows : at + 2 * rows, :], -w[at : at + rows, :])
        ],
        axis=0,
    )
    for turn in range(planes):
        a = a_ref[turn * block : (turn + 1) * block, :]
        real = dot(a, straight)
        imag = dot(a, turned)
        out = outs[turn]
        if turn:
            top = jnp.maximum(jnp.max(jnp.abs(real)), jnp.max(jnp.abs(imag)))
            power = 14.0 - jnp.ceil(jnp.log2(jnp.full((PAD_ROWS, half), jnp.maximum(top, 1e-30), F32)))
            power = jnp.clip(power, -110.0, 110.0)
            scale = jnp.exp2(power)[:1]
            out[: block, :] = real * scale
            out[block : 2 * block, :] = imag * scale
            out[2 * block :, :] = power
        else:
            out[: block, :] = real
            out[block :, :] = imag


def shards(green, direction, partners, counts):
    tile_dev, kmax = partners.shape
    rows, half = green.shape[1:]
    count = lax.axis_size("tile")
    planes = count // 2
    place = lax.axis_index("tile")
    side, plane = place % 2, place // 2
    core = lax.axis_index("src")
    left_side, right_side = side == 0, side == 1
    odd = plane % 2 == 1
    last_plane = planes - 1
    vmem = pl.BlockSpec(memory_space=pltpu.VMEM)
    smem = pl.BlockSpec(memory_space=pltpu.SMEM)
    params = pltpu.CompilerParams(vmem_limit_bytes=VMEM_LIMIT)

    def other_side(index):
        return index ^ 1

    def even_pair(index):
        return index ^ 2

    def odd_pair(index):
        target = (index // 2 - 1 ^ 1) + 1
        return 2 * target + index % 2 if 0 <= target < planes else -1

    def group(p, s):
        return 2 * p + s

    table = jnp.concatenate([partners, counts[:, None]], axis=1)
    table_mate = move(table, other_side)
    direction_other = cores(direction)
    mate = move(green, other_side)
    pair = move(green, even_pair)
    next_pair = move(green, odd_pair)
    late_green, table_mate = lax.optimization_barrier((green, table_mate))
    green_other = cores(late_green)

    near_left = plane >= 2
    near_right = plane <= planes - 3
    from_above = jnp.where(
        left_side,
        jnp.where(plane + 1 == last_plane, group(plane + 1, 1), group(plane + 2, 0)),
        group(plane + 1, 0),
    )
    from_below = jnp.where(
        left_side,
        group(plane - 1, 1),
        jnp.where(plane == 1, group(0, 0), group(plane - 2, 1)),
    )
    groups = [
        group(plane, side),
        group(plane, 1 - side),
        group(jnp.where(odd, plane - 1, plane + 1), side),
        group(jnp.where(odd, plane + 1, plane - 1), side),
        jnp.where(odd, from_below, from_above),
        jnp.where(odd, from_above, from_below),
        jnp.where(
            left_side,
            jnp.where(near_right, group(plane + 1, 1), NOWHERE),
            jnp.where(near_left, group(plane - 1, 0), NOWHERE),
        ),
        jnp.where(
            left_side,
            jnp.where(near_left, group(plane - 2, 1), NOWHERE),
            jnp.where(near_right, group(plane + 2, 0), NOWHERE),
        ),
    ]
    row_tiles = tile_dev // 2
    table_here = jnp.concatenate(
        [lax.dynamic_slice_in_dim(t, core * row_tiles, row_tiles, 0) for t in (table, table_mate)], axis=0
    )
    slots = jnp.arange(kmax, dtype=jnp.int32)[None, :]
    sampled = jnp.where(slots < table_here[:, kmax:], table_here[:, :kmax], NOWHERE * 4)
    ids = jnp.stack(groups).astype(jnp.int32)
    ids = ids[:, None] * tile_dev + jnp.arange(tile_dev, dtype=jnp.int32)[None, :]
    mask = jnp.any(sampled[None, :, None, :] == ids[:, None, :, None], axis=3).astype(F32)
    masks = (mask[:4], mask[4:7], mask[7:])

    def images(own, other):
        return pl.pallas_call(
            images_kernel,
            out_shape=jax.ShapeDtypeStruct((rows, 4 * half), BF16),
            in_specs=[smem, vmem, vmem, vmem, vmem],
            out_specs=vmem,
            compiler_params=params,
            cost_estimate=pl.CostEstimate(
                flops=4 * rows * 4 * half * half, bytes_accessed=8 * 1024 * 1024, transcendentals=0
            ),
        )(core.reshape(1).astype(jnp.int32), own, other, direction, direction_other)

    left_own = images(green, green_other)
    mate, left_own, masks = lax.optimization_barrier((mate, left_own, masks))

    even_choice = (jnp.where(odd, left_side & (plane < last_plane), right_side & (plane > 0)), next_pair, mate)
    odd_choice = (jnp.where(odd, right_side, left_side & (plane < last_plane)), pair, mate)
    near_choice = (side == plane % 2, next_pair, pair)
    even_real, odd_real, near_sent, even_imag, odd_imag = pick(
        (*even_choice, 0), (*odd_choice, 0), (*near_choice, None), (*even_choice, 1), (*odd_choice, 1)
    )
    pair_real = move(even_real, even_pair)
    next_real = move(odd_real, odd_pair)
    near = move(near_sent, other_side)
    mate_other = cores(mate)
    pair_other = cores(pair)
    next_other = cores(next_pair)
    even_imag, odd_imag, mate_other, pair_other, next_other = lax.optimization_barrier(
        (even_imag, odd_imag, mate_other, pair_other, next_other)
    )
    pair_imag = move(even_imag, even_pair)
    next_imag = move(odd_imag, odd_pair)
    left = (left_own, images(mate, mate_other))

    block = 2 * half // count
    inner = planes == 4
    if inner:
        outer_plane = (plane == 0) | (plane == last_plane)
        mirror, across, beside = last_plane - plane, plane ^ 2, plane ^ 1
        order = [
            plane,
            jnp.where(outer_plane, mirror, beside),
            jnp.where(outer_plane, across, mirror),
            jnp.where(outer_plane, beside, across),
        ]
    else:
        order = [(plane + turn) % planes for turn in range(planes)]
    order = jnp.stack(order).astype(jnp.int32)
    if block % 128 == 0:
        columns = pl.pallas_call(
            functools.partial(columns_kernel, planes, block),
            out_shape=jax.ShapeDtypeStruct((planes * block, 4 * rows), BF16),
            in_specs=[smem, vmem, vmem, vmem, vmem],
            out_specs=vmem,
            compiler_params=params,
        )(
            jnp.concatenate([jnp.stack([side, core]).astype(jnp.int32), order]),
            green, green_other, mate, mate_other,
        )
    else:

        def whole(own, other):
            both = jnp.concatenate(
                [jnp.where(core == 0, own, other), jnp.where(core == 0, other, own)], axis=2
            )
            here, there = both[:, : rows // 2], both[:, rows // 2 :]
            return jnp.stack([jnp.where(core == 0, here, there), jnp.where(core == 0, there, here)])

        columns = jnp.stack([whole(green, green_other), whole(mate, mate_other)], axis=1)
        columns = columns.reshape(2, 2, 2, rows // 2, planes, 2, block)
        columns = lax.dynamic_index_in_dim(columns, side, 5, keepdims=False)
        columns = jnp.take(columns, order, axis=4)
        columns = columns.transpose(4, 5, 0, 1, 2, 3).reshape(planes * block, 4 * rows)

    left, columns, pair_real, next_real = lax.optimization_barrier((left, columns, pair_real, next_real))
    far_choice = side == plane % 2
    (far_real,) = pick((far_choice, pair_real, next_real, None))
    far_real = move(far_real, other_side)
    sums = window_call(
        masks[0],
        left,
        [
            ([green], [green_other]),
            ([mate], [mate_other]),
            ([pair], [pair_other]),
            ([next_pair], [next_other]),
        ],
        None,
        False,
    )
    pair_imag, next_imag, near, sums = lax.optimization_barrier((pair_imag, next_imag, near, sums))
    (far_imag,) = pick((far_choice, pair_imag, next_imag, None))
    far_imag = move(far_imag, other_side)
    sums = window_call(
        masks[1],
        left,
        [
            ([pair_real, pair_imag], [cores(pair_real), cores(pair_imag)]),
            ([next_real, next_imag], [cores(next_real), cores(next_imag)]),
            ([near], [cores(near)]),
        ],
        sums,
        False,
    )
    far_imag, sums = lax.optimization_barrier((far_imag, sums))
    weighted = window_call(
        masks[2], left, [([far_real, far_imag], [cores(far_real), cores(far_imag)])], sums, True
    )
    weighted_mate = cores(weighted[1])

    out_shapes = [jax.ShapeDtypeStruct((2 * block, half), F32)]
    out_shapes += [jax.ShapeDtypeStruct((2 * block + PAD_ROWS, half), F32)] * (planes - 1)
    terms = pl.pallas_call(
        functools.partial(outer_kernel, planes),
        out_shape=tuple(out_shapes),
        in_specs=[vmem, vmem, vmem],
        out_specs=(vmem,) * planes,
        compiler_params=params,
        cost_estimate=pl.CostEstimate(
            flops=2 * planes * block * 4 * rows * 2 * half,
            bytes_accessed=8 * 1024 * 1024,
            transcendentals=0,
        ),
    )(columns, weighted[0], weighted_mate)

    def power_of(term):
        return term[2 * block : 2 * block + 1]

    def value_of(term):
        return term[: 2 * block] * jnp.exp2(-power_of(term))

    total = terms[0]
    if inner:
        sent = [term.astype(jnp.float16) for term in terms[1:3]]
        beside_got = move(sent[0], even_pair)
        across_got = move(sent[1], lambda i: i ^ 4 if i // 2 in (0, last_plane) else -1)
        middle_got = move(sent[1], lambda i: -1 if i // 2 in (0, last_plane) else odd_pair(i))
        first = beside_got.astype(F32)
        power = jnp.where(outer_plane, power_of(terms[3]), jnp.minimum(power_of(terms[3]), power_of(first)) - 1.0)
        share = jnp.where(outer_plane, 0.0, jnp.exp2(power - power_of(first)))
        carried = terms[3][: 2 * block] * jnp.exp2(power - power_of(terms[3])) + first[: 2 * block] * share
        carried = jnp.concatenate([carried, jnp.broadcast_to(power, (PAD_ROWS, half))], axis=0)
        carried = carried.astype(jnp.float16)
        last_got = move(carried, lambda i: i ^ 2 if i // 2 in (0, last_plane) else i ^ 4)
        total = total + jnp.where(outer_plane, 1.0, 0.0) * value_of(first)
        total = total + value_of(across_got.astype(F32)) + value_of(middle_got.astype(F32))
        total = total + value_of(last_got.astype(F32))
    else:
        for turn in range(1, planes):
            sent = terms[turn].astype(jnp.float16)
            got = move(sent, lambda index: (index + 2 * turn) % count).astype(F32)
            total = total + value_of(got)
    return jnp.stack([total[:block], total[block:]], axis=1)


def solution(mesh):
    in_specs = (
        P(None, ("freq", "tile"), "src"),
        P(None, ("freq", "src"), None),
        P(("freq", "tile"), None),
        P(("freq", "tile")),
    )
    out_specs = P(("freq", "tile"), None, "src")
    return jax.shard_map(shards, mesh=mesh, in_specs=in_specs, out_specs=out_specs, check_vma=False)
```

```python
import functools

import jax
import jax.numpy as jnp
from jax import lax
from jax.experimental import pallas as pl
from jax.experimental.pallas import tpu as pltpu
from jax.sharding import PartitionSpec as P

F32 = jnp.float32
BF16 = jnp.bfloat16
NOWHERE = -1000
PAD_ROWS = 16
SMEM = pl.BlockSpec(memory_space=pltpu.SMEM)
VMEM = pl.BlockSpec(memory_space=pltpu.VMEM)
PARAMS = pltpu.CompilerParams(vmem_limit_bytes=16 * 1024 * 1024)


def move(value, target):
    count = lax.axis_size("tile")
    pairs = [(source, target(source)) for source in range(count) if 0 <= target(source) < count]
    return lax.ppermute(value, "tile", pairs)


def here():
    place = lax.axis_index("tile")
    return place // 2, place % 2, lax.axis_index("src")


def cores(value):
    return lax.ppermute(value, "src", [(0, 1), (1, 0)])


def dot(a, b):
    return jnp.dot(a, b, preferred_element_type=F32)


def dot_t(a, b):
    return lax.dot_general(a, b, (((1,), (1,)), ((), ())), preferred_element_type=F32)


def images_kernel(a_own, a_other, v_own, v_other, left):
    rows, half = a_own.shape[1:]
    core = lax.axis_index("src")
    real = [a_own[0], -a_own[1], a_other[0], -a_other[1]]
    imag = [a_own[1], a_own[0], a_other[1], a_other[0]]
    sensors = jnp.concatenate(
        [jnp.concatenate(real, axis=1), jnp.concatenate(imag, axis=1)], axis=0
    )
    for index, column in enumerate((core, 1 - core)):
        cols = pl.ds(pl.multiple_of(column * half, half), half)
        values = jnp.concatenate(
            [v_own[0, :, cols], v_own[1, :, cols], v_other[0, :, cols], v_other[1, :, cols]], axis=0
        )
        images = dot(sensors, values).astype(BF16)
        at = 2 * index * half
        left[:, at : at + half] = images
        left[:rows, at + half : at + 2 * half] = images[rows:]
        left[rows:, at + half : at + 2 * half] = -images[:rows]


def table_kernel(partners_ref, counts_ref, table_ref):
    row = lax.broadcasted_iota(jnp.int32, table_ref.shape, 0)
    col = lax.broadcasted_iota(jnp.int32, table_ref.shape, 1)
    tile_rows, kmax = partners_ref.shape
    table = jnp.zeros(table_ref.shape, jnp.int32)
    for r in range(tile_rows):
        for k in range(kmax + 1):
            value = partners_ref[r, k] if k < kmax else counts_ref[r]
            table = jnp.where((row == r) & (col == k), value, table)
    table_ref[...] = table


def parts_of(refs):
    if len(refs) == 1:
        return refs[0][0], refs[0][1]
    return refs[0][...], refs[1][...]


def window_kernel(groups_of, kmax, tiles, widths, start, last, table_ref, mate_ref, left, *refs):
    blocks = []
    for width in widths:
        blocks.append((parts_of(refs[:width]), parts_of(refs[width : 2 * width])))
        refs = refs[2 * width :]
    rows, half = left.shape[0] // 2, left.shape[1] // 4
    tile = rows // tiles
    couples = refs[-1]
    refs = refs[:-1]
    plane, side, core = here()
    mine = side == core
    groups = groups_of(plane, side)
    sampled = []
    for r in range(tiles):
        count = jnp.where(mine, table_ref[r, kmax], mate_ref[r, kmax])
        sampled.append(
            [jnp.where(k < count, jnp.where(mine, table_ref[r, k], mate_ref[r, k]), NOWHERE * 4) for k in range(kmax)]
        )
    for block, (own, other) in enumerate(blocks):
        couple = dot_t(left[...], jnp.concatenate([*own, *other], axis=1))
        at = 2 * block * rows
        for r in range(tiles):
            for c in range(tiles):
                hits = sum((partner == groups[block] * tiles + c).astype(jnp.int32) for partner in sampled[r])
                keep = jnp.minimum(hits, 1).astype(F32)
                upper = slice(r * tile, (r + 1) * tile)
                lower = slice(rows + r * tile, rows + (r + 1) * tile)
                real = (couple[upper, c * tile : (c + 1) * tile] * keep).astype(BF16)
                imag = (couple[lower, c * tile : (c + 1) * tile] * keep).astype(BF16)
                first = slice(at + c * tile, at + (c + 1) * tile)
                second = slice(at + rows + c * tile, at + rows + (c + 1) * tile)
                couples[upper, first] = real
                couples[lower, first] = imag
                couples[upper, second] = -imag
                couples[lower, second] = real
    for index in range(2):
        values = jnp.concatenate([part for block in blocks for part in block[index]], axis=0)
        total = dot(couples[...], values)
        if not start:
            total += refs[index][...]
        out = refs[index if start else index + 2]
        out[...] = total.astype(BF16) if last else total


def window_call(tables, shape, groups_of, left, blocks, sums, last):
    args = [*tables, left]
    for own, other in blocks:
        args.extend(own)
        args.extend(other)
    if sums is not None:
        args.extend(sums)
    rows2, half = left.shape[0], left.shape[1] // 4
    tiles, kmax = shape
    out = jax.ShapeDtypeStruct((rows2, half), BF16 if last else F32)
    return pl.pallas_call(
        functools.partial(
            window_kernel, groups_of, kmax, tiles, [len(own) for own, _ in blocks], sums is None, last
        ),
        out_shape=(out, out),
        in_specs=[SMEM] * 2 + [VMEM] * (len(args) - 2),
        out_specs=(VMEM, VMEM),
        scratch_shapes=[pltpu.VMEM((rows2, len(blocks) * rows2), BF16)],
        compiler_params=PARAMS,
        cost_estimate=pl.CostEstimate(
            flops=len(blocks) * 2 * 2 * rows2 * half * rows2 * 2,
            bytes_accessed=sum(a.size * a.dtype.itemsize for a in args[2:]) + 2 * rows2 * half * 4,
            transcendentals=0,
        ),
    )(*args)


def pick_kernel(choices, *refs):
    place = here()
    outs = refs[len(refs) - len(choices) :]

    def put(out, value, part):
        out[...] = value[...] if part is None else value[part]

    for index, (flag_of, part) in enumerate(choices):
        flag = flag_of(*place)
        first, second, out = refs[2 * index], refs[2 * index + 1], outs[index]
        pl.when(flag)(functools.partial(put, out, first, part))
        pl.when(jnp.logical_not(flag))(functools.partial(put, out, second, part))


def pick(*choices):
    args = [value for choice in choices for value in choice[1:3]]
    shapes = [a.shape if choice[3] is None else a.shape[1:] for a, choice in zip(args[::2], choices)]
    return pl.pallas_call(
        functools.partial(pick_kernel, [(choice[0], choice[3]) for choice in choices]),
        out_shape=tuple(jax.ShapeDtypeStruct(shape, args[0].dtype) for shape in shapes),
        in_specs=[VMEM] * len(args),
        out_specs=(VMEM,) * len(choices),
        compiler_params=PARAMS,
    )(*args)


def columns_kernel(planes, block, turn_of, *refs):
    out = refs[-1]
    plane, side, core = here()
    rows, half = refs[0].shape[1:]
    for distance in range(planes):
        at = (2 * turn_of(plane, distance) + side) * block
        own = at // half == core
        cols = pl.ds(pl.multiple_of(lax.rem(at, half), block), block)
        for group in range(2):
            for part in range(2):
                value = jnp.where(own, refs[2 * group][part, :, cols], refs[2 * group + 1][part, :, cols])
                start = (2 * group + part) * rows
                out[distance * block : (distance + 1) * block, start : start + rows] = value.T


def outer_kernel(planes, a_ref, w_own, w_other, *outs):
    rows = w_own.shape[0] // 2
    half = w_own.shape[1]
    rows2 = 2 * rows
    block = a_ref.shape[0] // planes
    for plane in range(planes):
        a = a_ref[plane * block : (plane + 1) * block, :]
        real = dot(a[:, :rows2], w_own[...]) + dot(a[:, rows2:], w_other[...])
        imag = (
            dot(a[:, :rows], w_own[rows:, :])
            - dot(a[:, rows:rows2], w_own[:rows, :])
            + dot(a[:, rows2 : rows2 + rows], w_other[rows:, :])
            - dot(a[:, rows2 + rows :], w_other[:rows, :])
        )
        out = outs[plane]
        if plane:
            top = jnp.maximum(jnp.max(jnp.abs(real)), jnp.max(jnp.abs(imag)))
            power = 14.0 - jnp.ceil(jnp.log2(jnp.full((PAD_ROWS, half), jnp.maximum(top, 1e-30), F32)))
            power = jnp.clip(power, -110.0, 110.0)
            scale = jnp.exp2(power)[:1]
            out[: block, :] = real * scale
            out[block : 2 * block, :] = imag * scale
            out[2 * block :, :] = power
        else:
            out[: block, :] = real
            out[block :, :] = imag


def shards(green, direction, partners, counts):
    shape = partners.shape
    rows, half = green.shape[1:]
    count = lax.axis_size("tile")
    planes = count // 2
    last_plane = planes - 1

    def other_side(index):
        return index ^ 1

    def even_pair(index):
        return index ^ 2

    def odd_pair(index):
        target = (index // 2 - 1 ^ 1) + 1
        return 2 * target + index % 2 if 0 <= target < planes else -1

    def turned(p, turn):
        return p ^ turn if planes == 4 else lax.rem(p + turn, planes) if isinstance(p, jax.Array) else (p + turn) % planes

    def group(p, s):
        return 2 * p + s

    def mine(plane, side, core):
        return side == core

    def rest(plane, side, core):
        return side != core

    direction_other = cores(direction)
    green_other = cores(green)
    mate = move(green, other_side)
    pair = move(green, even_pair)
    next_pair = move(green, odd_pair)
    late_partners, green_other = lax.optimization_barrier((partners, green_other))
    table = pl.pallas_call(
        table_kernel,
        out_shape=jax.ShapeDtypeStruct((8, 128), jnp.int32),
        in_specs=[SMEM, SMEM],
        out_specs=VMEM,
    )(late_partners, counts)
    table_mate = move(table, other_side)
    mate, direction_other, green_other, table_mate = lax.optimization_barrier(
        (mate, direction_other, green_other, table_mate)
    )

    def by_side(plane, side, core):
        return side == plane % 2

    def by_pair(plane, side, core):
        return jnp.where(plane % 2 == 1, (side == 0) & (plane < last_plane), (side == 1) & (plane > 0))

    def by_next(plane, side, core):
        return jnp.where(plane % 2 == 1, side == 1, (side == 0) & (plane < last_plane))

    near_sent, pair_sent, next_sent = pick(
        (by_side, next_pair, pair, None),
        (by_pair, next_pair, mate, None),
        (by_next, pair, mate, None),
    )
    pair_two = move(pair_sent, even_pair)
    next_two = move(next_sent, odd_pair)
    near = move(near_sent, other_side)
    mate_other = cores(mate)
    pair_other = cores(pair)
    next_other = cores(next_pair)

    def first_groups(plane, side):
        odd = plane % 2 == 1
        return [
            group(plane, side),
            group(plane, 1 - side),
            group(jnp.where(odd, plane - 1, plane + 1), side),
            group(jnp.where(odd, plane + 1, plane - 1), side),
        ]

    def second_groups(plane, side):
        odd = plane % 2 == 1
        from_above = jnp.where(
            side == 0,
            jnp.where(plane + 1 == last_plane, group(plane + 1, 1), group(plane + 2, 0)),
            group(plane + 1, 0),
        )
        from_below = jnp.where(
            side == 0, group(plane - 1, 1), jnp.where(plane == 1, group(0, 0), group(plane - 2, 1))
        )
        return [
            jnp.where(
                side == 0,
                jnp.where(plane <= planes - 3, group(plane + 1, 1), NOWHERE),
                jnp.where(plane >= 2, group(plane - 1, 0), NOWHERE),
            ),
            jnp.where(odd, from_below, from_above),
            jnp.where(odd, from_above, from_below),
        ]

    def third_groups(plane, side):
        return [
            jnp.where(
                side == 0,
                jnp.where(plane >= 2, group(plane - 2, 1), NOWHERE),
                jnp.where(plane <= planes - 3, group(plane + 2, 0), NOWHERE),
            )
        ]

    rows_own, rows_other, rest_own, rest_other = pick(
        (mine, green, mate, None),
        (mine, green_other, mate_other, None),
        (rest, green, mate, None),
        (rest, green_other, mate_other, None),
    )
    left = pl.pallas_call(
        images_kernel,
        out_shape=jax.ShapeDtypeStruct((2 * rows, 4 * half), BF16),
        in_specs=[VMEM, VMEM, VMEM, VMEM],
        out_specs=VMEM,
        compiler_params=PARAMS,
        cost_estimate=pl.CostEstimate(
            flops=2 * 4 * rows * 4 * half * half, bytes_accessed=8 * 1024 * 1024, transcendentals=0
        ),
    )(rows_own, rows_other, direction, direction_other)

    block = 2 * half // count
    if block % 128 == 0:
        columns = pl.pallas_call(
            functools.partial(columns_kernel, planes, block, turned),
            out_shape=jax.ShapeDtypeStruct((planes * block, 4 * rows), BF16),
            in_specs=[VMEM, VMEM, VMEM, VMEM],
            out_specs=VMEM,
            compiler_params=PARAMS,
        )(rows_own, rows_other, rest_own, rest_other)
    else:
        plane, side, core = here()

        def whole(own, other):
            return jnp.concatenate(
                [jnp.where(core == 0, own, other), jnp.where(core == 0, other, own)], axis=2
            )

        columns = jnp.stack([whole(rows_own, rows_other), whole(rest_own, rest_other)])
        columns = columns.reshape(2, 2, rows, planes, 2, block)
        columns = lax.dynamic_index_in_dim(columns, side, 4, keepdims=False)
        columns = jnp.concatenate([columns, columns], axis=3)
        columns = lax.dynamic_slice_in_dim(columns, plane, planes, axis=3)
        columns = columns.transpose(3, 4, 0, 1, 2).reshape(planes * block, 4 * rows)

    add = functools.partial(window_call, (table, table_mate), shape)
    sums = add(
        first_groups,
        left,
        [
            ([green], [green_other]),
            ([mate], [mate_other]),
            ([pair], [pair_other]),
            ([next_pair], [next_other]),
        ],
        None,
        False,
    )
    near, pair_two, next_two, sums, columns = lax.optimization_barrier(
        (near, pair_two, next_two, sums, columns)
    )
    far_real, far_imag = pick(
        (by_side, pair_two, next_two, 0), (by_side, next_two, pair_two, 1)
    )
    far = [move(far_real, other_side), move(far_imag, lambda i: i - 2 if i % 2 else i + 2)]
    sums = add(
        second_groups, left, [([block], [cores(block)]) for block in (near, pair_two, next_two)], sums, False
    )
    far, sums = lax.optimization_barrier((far, sums))
    weighted = add(third_groups, left, [(far, [cores(part) for part in far])], sums, True)
    weighted_mate = cores(weighted[1])

    out_shapes = [jax.ShapeDtypeStruct((2 * block, half), F32)]
    out_shapes += [jax.ShapeDtypeStruct((2 * block + PAD_ROWS, half), F32)] * (planes - 1)
    terms = pl.pallas_call(
        functools.partial(outer_kernel, planes),
        out_shape=tuple(out_shapes),
        in_specs=[VMEM, VMEM, VMEM],
        out_specs=(VMEM,) * planes,
        compiler_params=PARAMS,
        cost_estimate=pl.CostEstimate(
            flops=2 * planes * block * 4 * rows * 2 * half,
            bytes_accessed=8 * 1024 * 1024,
            transcendentals=0,
        ),
    )(columns, weighted[0], weighted_mate)
    total = terms[0]
    for turn in (2, 3, 1) if planes == 4 else range(1, planes):
        sent = terms[turn].astype(jnp.float16)
        got = move(sent, lambda index: turned(index // 2, turn) * 2 + index % 2).astype(F32)
        total = total + got[: 2 * block] * jnp.exp2(-got[2 * block : 2 * block + 1])
    return jnp.stack([total[:block], total[block:]], axis=1)


def solution(mesh):
    in_specs = (
        P(None, ("freq", "tile"), "src"),
        P(None, ("freq", "src"), None),
        P(("freq", "tile"), None),
        P(("freq", "tile")),
    )
    out_specs = P(("freq", "tile"), None, "src")
    return jax.shard_map(shards, mesh=mesh, in_specs=in_specs, out_specs=out_specs, check_vma=False)
```

```python
import functools

import jax
import jax.numpy as jnp
from jax import lax
from jax.experimental import pallas as pl
from jax.experimental.pallas import tpu as pltpu
from jax.sharding import PartitionSpec as P

F32 = jnp.float32
BF16 = jnp.bfloat16
NOWHERE = -1000
PAD_ROWS = 16
SMEM = pl.BlockSpec(memory_space=pltpu.SMEM)
VMEM = pl.BlockSpec(memory_space=pltpu.VMEM)
PARAMS = pltpu.CompilerParams(vmem_limit_bytes=16 * 1024 * 1024)


def move(value, target):
    count = lax.axis_size("tile")
    pairs = [(source, target(source)) for source in range(count) if 0 <= target(source) < count]
    return lax.ppermute(value, "tile", pairs)


def here():
    place = lax.axis_index("tile")
    return place // 2, place % 2, lax.axis_index("src")


def cores(value):
    return lax.ppermute(value, "src", [(0, 1), (1, 0)])


def dot(a, b):
    return jnp.dot(a, b, preferred_element_type=F32)


def dot_t(a, b):
    return lax.dot_general(a, b, (((1,), (1,)), ((), ())), preferred_element_type=F32)


def images_kernel(a_own, a_other, v_own, v_other, left):
    rows, half = a_own.shape[1:]
    core = lax.axis_index("src")
    real = [a_own[0], -a_own[1], a_other[0], -a_other[1]]
    imag = [a_own[1], a_own[0], a_other[1], a_other[0]]
    sensors = jnp.concatenate(
        [jnp.concatenate(real, axis=1), jnp.concatenate(imag, axis=1)], axis=0
    )
    for index, column in enumerate((core, 1 - core)):
        cols = pl.ds(pl.multiple_of(column * half, half), half)
        values = jnp.concatenate(
            [v_own[0, :, cols], v_own[1, :, cols], v_other[0, :, cols], v_other[1, :, cols]], axis=0
        )
        images = dot(sensors, values).astype(BF16)
        at = 2 * index * half
        left[:, at : at + half] = images
        left[:rows, at + half : at + 2 * half] = images[rows:]
        left[rows:, at + half : at + 2 * half] = -images[:rows]


def table_kernel(partners_ref, counts_ref, table_ref):
    row = lax.broadcasted_iota(jnp.int32, table_ref.shape, 0)
    col = lax.broadcasted_iota(jnp.int32, table_ref.shape, 1)
    tile_rows, kmax = partners_ref.shape
    table = jnp.zeros(table_ref.shape, jnp.int32)
    for r in range(tile_rows):
        for k in range(kmax + 1):
            value = partners_ref[r, k] if k < kmax else counts_ref[r]
            table = jnp.where((row == r) & (col == k), value, table)
    table_ref[...] = table


def parts_of(refs):
    if len(refs) == 1:
        return refs[0][0], refs[0][1]
    return refs[0][...], refs[1][...]


def window_kernel(groups_of, kmax, tiles, widths, start, last, table_ref, mate_ref, left, *refs):
    blocks = []
    for width in widths:
        blocks.append((parts_of(refs[:width]), parts_of(refs[width : 2 * width])))
        refs = refs[2 * width :]
    rows, half = left.shape[0] // 2, left.shape[1] // 4
    tile = rows // tiles
    couples = refs[-1]
    refs = refs[:-1]
    plane, side, core = here()
    mine = side == core
    groups = groups_of(plane, side)
    sampled = []
    for r in range(tiles):
        count = jnp.where(mine, table_ref[r, kmax], mate_ref[r, kmax])
        sampled.append(
            [jnp.where(k < count, jnp.where(mine, table_ref[r, k], mate_ref[r, k]), NOWHERE * 4) for k in range(kmax)]
        )
    for block, (own, other) in enumerate(blocks):
        couple = dot_t(left[...], jnp.concatenate([*own, *other], axis=1))
        at = 2 * block * rows
        for r in range(tiles):
            for c in range(tiles):
                hits = sum((partner == groups[block] * tiles + c).astype(jnp.int32) for partner in sampled[r])
                keep = jnp.minimum(hits, 1).astype(F32)
                upper = slice(r * tile, (r + 1) * tile)
                lower = slice(rows + r * tile, rows + (r + 1) * tile)
                real = (couple[upper, c * tile : (c + 1) * tile] * keep).astype(BF16)
                imag = (couple[lower, c * tile : (c + 1) * tile] * keep).astype(BF16)
                first = slice(at + c * tile, at + (c + 1) * tile)
                second = slice(at + rows + c * tile, at + rows + (c + 1) * tile)
                couples[upper, first] = real
                couples[lower, first] = imag
                couples[upper, second] = -imag
                couples[lower, second] = real
    for index in range(2):
        values = jnp.concatenate([part for block in blocks for part in block[index]], axis=0)
        total = dot(couples[...], values)
        if not start:
            total += refs[index][...]
        out = refs[index if start else index + 2]
        out[...] = total.astype(BF16) if last else total


def window_call(tables, shape, groups_of, left, blocks, sums, last):
    args = [*tables, left]
    for own, other in blocks:
        args.extend(own)
        args.extend(other)
    if sums is not None:
        args.extend(sums)
    rows2, half = left.shape[0], left.shape[1] // 4
    tiles, kmax = shape
    out = jax.ShapeDtypeStruct((rows2, half), BF16 if last else F32)
    return pl.pallas_call(
        functools.partial(
            window_kernel, groups_of, kmax, tiles, [len(own) for own, _ in blocks], sums is None, last
        ),
        out_shape=(out, out),
        in_specs=[SMEM] * 2 + [VMEM] * (len(args) - 2),
        out_specs=(VMEM, VMEM),
        scratch_shapes=[pltpu.VMEM((rows2, len(blocks) * rows2), BF16)],
        compiler_params=PARAMS,
        cost_estimate=pl.CostEstimate(
            flops=len(blocks) * 2 * 2 * rows2 * half * rows2 * 2,
            bytes_accessed=sum(a.size * a.dtype.itemsize for a in args[2:]) + 2 * rows2 * half * 4,
            transcendentals=0,
        ),
    )(*args)


def pick_kernel(choices, *refs):
    place = here()
    outs = refs[len(refs) - len(choices) :]

    def put(out, value, part):
        out[...] = value[...] if part is None else value[part]

    for index, (flag_of, part) in enumerate(choices):
        flag = flag_of(*place)
        first, second, out = refs[2 * index], refs[2 * index + 1], outs[index]
        pl.when(flag)(functools.partial(put, out, first, part))
        pl.when(jnp.logical_not(flag))(functools.partial(put, out, second, part))


def pick(*choices):
    args = [value for choice in choices for value in choice[1:3]]
    shapes = [a.shape if choice[3] is None else a.shape[1:] for a, choice in zip(args[::2], choices)]
    return pl.pallas_call(
        functools.partial(pick_kernel, [(choice[0], choice[3]) for choice in choices]),
        out_shape=tuple(jax.ShapeDtypeStruct(shape, args[0].dtype) for shape in shapes),
        in_specs=[VMEM] * len(args),
        out_specs=(VMEM,) * len(choices),
        compiler_params=PARAMS,
    )(*args)


def columns_kernel(turns, block, turn_of, *refs):
    out = refs[-1]
    plane, side, core = here()
    rows, half = refs[0].shape[1:]
    for index, turn in enumerate(turns):
        at = (2 * turn_of(plane, turn) + side) * block
        own = at // half == core
        cols = pl.ds(pl.multiple_of(lax.rem(at, half), block), block)
        for group in range(2):
            for part in range(2):
                value = jnp.where(own, refs[2 * group][part, :, cols], refs[2 * group + 1][part, :, cols])
                start = (2 * group + part) * rows
                out[index * block : (index + 1) * block, start : start + rows] = value.T


def outer_kernel(first, block, a_ref, w_own, w_other, *outs):
    rows = w_own.shape[0] // 2
    half = w_own.shape[1]
    straight = jnp.concatenate([w_own[...], w_other[...]], axis=0)
    turned = jnp.concatenate([w_own[rows:, :], -w_own[:rows, :], w_other[rows:, :], -w_other[:rows, :]], axis=0)
    for index, out in enumerate(outs):
        a = a_ref[(first + index) * block : (first + index + 1) * block, :]
        real = dot(a, straight)
        imag = dot(a, turned)
        if out.shape[0] > 2 * block:
            top = jnp.maximum(jnp.max(jnp.abs(real)), jnp.max(jnp.abs(imag)))
            power = 14.0 - jnp.ceil(jnp.log2(jnp.full((PAD_ROWS, half), jnp.maximum(top, 1e-30), F32)))
            power = jnp.clip(power, -110.0, 110.0)
            scale = jnp.exp2(power)[:1]
            out[:block, :] = real * scale
            out[block : 2 * block, :] = imag * scale
            out[2 * block :, :] = power
        else:
            out[:block, :] = real
            out[block:, :] = imag


def lay_kernel(total, out):
    block = out.shape[0]
    out[:, 0, :] = total[:block, :]
    out[:, 1, :] = total[block:, :]


def shards(green, direction, partners, counts):
    shape = partners.shape
    rows, half = green.shape[1:]
    count = lax.axis_size("tile")
    planes = count // 2
    last_plane = planes - 1

    def other_side(index):
        return index ^ 1

    def even_pair(index):
        return index ^ 2

    def odd_pair(index):
        target = (index // 2 - 1 ^ 1) + 1
        return 2 * target + index % 2 if 0 <= target < planes else -1

    def turned(p, turn):
        return p ^ turn if planes == 4 else lax.rem(p + turn, planes) if isinstance(p, jax.Array) else (p + turn) % planes

    def group(p, s):
        return 2 * p + s

    def mine(plane, side, core):
        return side == core

    def rest(plane, side, core):
        return side != core

    direction_other = cores(direction)
    green_other = cores(green)
    mate = move(green, other_side)
    pair = move(green, even_pair)
    next_pair = move(green, odd_pair)
    late_partners, green_other = lax.optimization_barrier((partners, green_other))
    table = pl.pallas_call(
        table_kernel,
        out_shape=jax.ShapeDtypeStruct((8, 128), jnp.int32),
        in_specs=[SMEM, SMEM],
        out_specs=VMEM,
    )(late_partners, counts)
    table_mate = move(table, other_side)
    mate, direction_other, green_other, table_mate = lax.optimization_barrier(
        (mate, direction_other, green_other, table_mate)
    )

    def by_side(plane, side, core):
        return side == plane % 2

    def by_pair(plane, side, core):
        return jnp.where(plane % 2 == 1, (side == 0) & (plane < last_plane), (side == 1) & (plane > 0))

    def by_next(plane, side, core):
        return jnp.where(plane % 2 == 1, side == 1, (side == 0) & (plane < last_plane))

    near_sent, pair_sent, next_sent = pick(
        (by_side, next_pair, pair, None),
        (by_pair, next_pair, mate, None),
        (by_next, pair, mate, None),
    )
    pair_two = move(pair_sent, even_pair)
    next_two = move(next_sent, odd_pair)
    near = move(near_sent, other_side)
    mate_other = cores(mate)
    pair_other = cores(pair)
    next_other = cores(next_pair)

    def first_groups(plane, side):
        odd = plane % 2 == 1
        return [
            group(plane, side),
            group(plane, 1 - side),
            group(jnp.where(odd, plane - 1, plane + 1), side),
            group(jnp.where(odd, plane + 1, plane - 1), side),
        ]

    def second_groups(plane, side):
        odd = plane % 2 == 1
        from_above = jnp.where(
            side == 0,
            jnp.where(plane + 1 == last_plane, group(plane + 1, 1), group(plane + 2, 0)),
            group(plane + 1, 0),
        )
        from_below = jnp.where(
            side == 0, group(plane - 1, 1), jnp.where(plane == 1, group(0, 0), group(plane - 2, 1))
        )
        return [
            jnp.where(
                side == 0,
                jnp.where(plane <= planes - 3, group(plane + 1, 1), NOWHERE),
                jnp.where(plane >= 2, group(plane - 1, 0), NOWHERE),
            ),
            jnp.where(odd, from_below, from_above),
            jnp.where(odd, from_above, from_below),
        ]

    def third_groups(plane, side):
        return [
            jnp.where(
                side == 0,
                jnp.where(plane >= 2, group(plane - 2, 1), NOWHERE),
                jnp.where(plane <= planes - 3, group(plane + 2, 0), NOWHERE),
            )
        ]

    rows_own, rows_other, rest_own, rest_other = pick(
        (mine, green, mate, None),
        (mine, green_other, mate_other, None),
        (rest, green, mate, None),
        (rest, green_other, mate_other, None),
    )
    left = pl.pallas_call(
        images_kernel,
        out_shape=jax.ShapeDtypeStruct((2 * rows, 4 * half), BF16),
        in_specs=[VMEM, VMEM, VMEM, VMEM],
        out_specs=VMEM,
        compiler_params=PARAMS,
        cost_estimate=pl.CostEstimate(
            flops=2 * 4 * rows * 4 * half * half, bytes_accessed=8 * 1024 * 1024, transcendentals=0
        ),
    )(rows_own, rows_other, direction, direction_other)

    block = 2 * half // count
    turns = [2, 3, 1, 0] if planes == 4 else [*range(1, planes), 0]
    if block % 128 == 0:
        columns = pl.pallas_call(
            functools.partial(columns_kernel, turns, block, turned),
            out_shape=jax.ShapeDtypeStruct((planes * block, 4 * rows), BF16),
            in_specs=[VMEM, VMEM, VMEM, VMEM],
            out_specs=VMEM,
            compiler_params=PARAMS,
        )(rows_own, rows_other, rest_own, rest_other)
    else:
        plane, side, core = here()

        def whole(own, other):
            return jnp.concatenate(
                [jnp.where(core == 0, own, other), jnp.where(core == 0, other, own)], axis=2
            )

        columns = jnp.stack([whole(rows_own, rows_other), whole(rest_own, rest_other)])
        columns = columns.reshape(2, 2, rows, planes, 2, block)
        columns = lax.dynamic_index_in_dim(columns, side, 4, keepdims=False)
        columns = jnp.take(columns, jnp.stack([turned(plane, turn) for turn in turns]), axis=3)
        columns = columns.transpose(3, 4, 0, 1, 2).reshape(planes * block, 4 * rows)

    add = functools.partial(window_call, (table, table_mate), shape)
    sums = add(
        first_groups,
        left,
        [
            ([green], [green_other]),
            ([mate], [mate_other]),
            ([pair], [pair_other]),
            ([next_pair], [next_other]),
        ],
        None,
        False,
    )
    pair_two, next_two, sums, columns = lax.optimization_barrier((pair_two, next_two, sums, columns))
    far_real, far_imag = pick(
        (by_side, pair_two, next_two, 0), (by_side, next_two, pair_two, 1)
    )
    far = [move(far_real, other_side), move(far_imag, lambda i: i - 2 if i % 2 else i + 2)]
    sums = add(
        second_groups, left, [([block], [cores(block)]) for block in (near, pair_two, next_two)], sums, False
    )
    far, sums = lax.optimization_barrier((far, sums))
    weighted = add(third_groups, left, [(far, [cores(part) for part in far])], sums, True)
    weighted_mate = cores(weighted[1])

    def terms(first, turns):
        pads = [PAD_ROWS if turn else 0 for turn in turns]
        return pl.pallas_call(
            functools.partial(outer_kernel, first, block),
            out_shape=tuple(jax.ShapeDtypeStruct((2 * block + pad, half), F32) for pad in pads),
            in_specs=[VMEM, VMEM, VMEM],
            out_specs=(VMEM,) * len(turns),
            compiler_params=PARAMS,
            cost_estimate=pl.CostEstimate(
                flops=2 * len(turns) * block * 4 * rows * 2 * half,
                bytes_accessed=4 * 1024 * 1024,
                transcendentals=0,
            ),
        )(columns, weighted[0], weighted_mate)

    ahead = len(turns) // 4
    sent = terms(0, turns[:ahead]) + terms(ahead, turns[ahead:-1])
    (total,) = terms(planes - 1, turns[-1:])
    for turn, term in zip(turns, sent):
        got = move(term.astype(jnp.float16), lambda index: turned(index // 2, turn) * 2 + index % 2).astype(F32)
        total = total + got[: 2 * block] * jnp.exp2(-got[2 * block : 2 * block + 1])
    return pl.pallas_call(
        lay_kernel,
        out_shape=jax.ShapeDtypeStruct((block, 2, half), F32),
        in_specs=[VMEM],
        out_specs=VMEM,
        compiler_params=PARAMS,
    )(total)


def solution(mesh):
    in_specs = (
        P(None, ("freq", "tile"), "src"),
        P(None, ("freq", "src"), None),
        P(("freq", "tile"), None),
        P(("freq", "tile")),
    )
    out_specs = P(("freq", "tile"), None, "src")
    return jax.shard_map(shards, mesh=mesh, in_specs=in_specs, out_specs=out_specs, check_vma=False)
```

```python
import functools

import jax
import jax.numpy as jnp
from jax import lax
from jax.experimental import pallas as pl
from jax.experimental.pallas import tpu as pltpu
from jax.sharding import PartitionSpec as P

F32 = jnp.float32
BF16 = jnp.bfloat16
NOWHERE = -1000
PAD_ROWS = 8
SMEM = pl.BlockSpec(memory_space=pltpu.SMEM)
VMEM = pl.BlockSpec(memory_space=pltpu.VMEM)
PARAMS = pltpu.CompilerParams(vmem_limit_bytes=16 * 1024 * 1024)


def move(value, target):
    count = lax.axis_size("tile")
    pairs = [(source, target(source)) for source in range(count) if 0 <= target(source) < count]
    return lax.ppermute(value, "tile", pairs)


def here():
    place = lax.axis_index("tile")
    return place // 2, place % 2, lax.axis_index("src")


def cores(value):
    return lax.ppermute(value, "src", [(0, 1), (1, 0)])


def dot(a, b):
    return jnp.dot(a, b, preferred_element_type=F32)


def dot_t(a, b):
    return lax.dot_general(a, b, (((1,), (1,)), ((), ())), preferred_element_type=F32)


def images_kernel(core_rows, a_own, a_other, b_own, b_other, v_own, v_other, left):
    half = a_own.shape[2]
    core = lax.axis_index("src")
    at = pl.ds(pl.multiple_of(core * core_rows, core_rows), core_rows)
    sensors = []
    for own, other in ((a_own, a_other), (b_own, b_other)):
        own_real, own_imag, other_real, other_imag = own[0, at, :], own[1, at, :], other[0, at, :], other[1, at, :]
        sensors.append(jnp.concatenate([own_real, -own_imag, other_real, -other_imag], axis=1))
        sensors.append(jnp.concatenate([own_imag, own_real, other_imag, other_real], axis=1))
    sensors = jnp.concatenate(sensors, axis=0)
    for index, column in enumerate((core, 1 - core)):
        cols = pl.ds(pl.multiple_of(column * half, half), half)
        values = jnp.concatenate(
            [v_own[0, :, cols], v_own[1, :, cols], v_other[0, :, cols], v_other[1, :, cols]], axis=0
        )
        images = dot(sensors, values).astype(BF16)
        first = slice(2 * index * half, (2 * index + 1) * half)
        second = slice((2 * index + 1) * half, (2 * index + 2) * half)
        left[:, first] = images
        for slot in range(2):
            real = slice(2 * slot * core_rows, (2 * slot + 1) * core_rows)
            imag = slice((2 * slot + 1) * core_rows, (2 * slot + 2) * core_rows)
            left[real, second] = images[imag]
            left[imag, second] = -images[real]


def table_kernel(partners_ref, counts_ref, table_ref):
    row = lax.broadcasted_iota(jnp.int32, table_ref.shape, 0)
    col = lax.broadcasted_iota(jnp.int32, table_ref.shape, 1)
    tile_rows, kmax = partners_ref.shape
    table = jnp.zeros(table_ref.shape, jnp.int32)
    for r in range(tile_rows):
        for k in range(kmax + 1):
            value = partners_ref[r, k] if k < kmax else counts_ref[r]
            table = jnp.where((row == r) & (col == k), value, table)
    table_ref[...] = table


def parts_of(refs):
    if len(refs) == 1:
        return refs[0][0], refs[0][1]
    return refs[0][...], refs[1][...]


def window_kernel(groups_of, slot_group, shape, slots, done, widths, start, table_ref, mate_ref, left, *refs):
    blocks = []
    for width in widths:
        blocks.append((parts_of(refs[:width]), parts_of(refs[width : 2 * width])))
        refs = refs[2 * width :]
    sums, outs, couples = refs[: 0 if start else 2 * len(slots)], refs[-2 * len(slots) - 1 : -1], refs[-1]
    core_rows = left.shape[0] // 4
    tiles, kmax = shape
    row_tiles = tiles // 2
    tile = core_rows // row_tiles
    plane, side, core = here()
    groups = groups_of(plane, side)
    sampled = []
    for slot in slots:
        mine = side == slot_group(plane, slot)
        for row_tile in range(row_tiles):
            r = core * row_tiles + row_tile
            count = jnp.where(mine, table_ref[r, kmax], mate_ref[r, kmax])
            partners = [jnp.where(mine, table_ref[r, k], mate_ref[r, k]) for k in range(kmax)]
            sampled.append([jnp.where(k < count, partner, NOWHERE * 4) for k, partner in enumerate(partners)])
    left_rows = left[slots[0] * 2 * core_rows :, :]
    wide = tiles * tile
    for block, (own, other) in enumerate(blocks):
        couple = dot_t(left_rows, jnp.concatenate([*own, *other], axis=1))
        for index, row_partners in enumerate(sampled):
            begin = index // row_tiles * 2 * core_rows + index % row_tiles * tile
            upper = slice(begin, begin + tile)
            lower = slice(begin + core_rows, begin + core_rows + tile)
            for c in range(tiles):
                hits = sum((partner == groups[block] * tiles + c).astype(jnp.int32) for partner in row_partners)
                keep = jnp.minimum(hits, 1).astype(F32)
                real = (couple[upper, c * tile : (c + 1) * tile] * keep).astype(BF16)
                imag = (couple[lower, c * tile : (c + 1) * tile] * keep).astype(BF16)
                at = 2 * block * wide + c * tile
                couples[upper, at : at + tile] = real
                couples[lower, at : at + tile] = imag
                couples[upper, at + wide : at + wide + tile] = -imag
                couples[lower, at + wide : at + wide + tile] = real
    for index in range(2):
        values = jnp.concatenate([part for block in blocks for part in block[index]], axis=0)
        total = dot(couples[...], values)
        for position, slot in enumerate(slots):
            part = total[position * 2 * core_rows : (position + 1) * 2 * core_rows]
            if not start:
                part = part + sums[2 * position + index][...]
            outs[2 * position + index][...] = part.astype(BF16) if slot in done else part


def window_call(tables, shape, slot_group, groups_of, left, blocks, sums, slots, done):
    args = [*tables, left]
    for own, other in blocks:
        args.extend(own)
        args.extend(other)
    if sums is not None:
        args.extend(sums)
    rows2, half = left.shape[0] // 2, left.shape[1] // 4
    outs = [jax.ShapeDtypeStruct((rows2, half), BF16 if slot in done else F32) for slot in slots for _ in range(2)]
    wide = 4 * left.shape[0] // 4
    return pl.pallas_call(
        functools.partial(
            window_kernel, groups_of, slot_group, shape, slots, done, [len(own) for own, _ in blocks], sums is None
        ),
        out_shape=tuple(outs),
        in_specs=[SMEM] * 2 + [VMEM] * (len(args) - 2),
        out_specs=(VMEM,) * len(outs),
        scratch_shapes=[pltpu.VMEM((len(slots) * rows2, len(blocks) * wide), BF16)],
        compiler_params=PARAMS,
        cost_estimate=pl.CostEstimate(
            flops=len(blocks) * 2 * 2 * len(slots) * rows2 * half * rows2 * 4,
            bytes_accessed=sum(a.size * a.dtype.itemsize for a in args[2:]) + 2 * rows2 * half * 8,
            transcendentals=0,
        ),
    )(*args)


def pick_kernel(choices, *refs):
    place = here()
    outs = refs[len(refs) - len(choices) :]

    def put(out, value, part):
        out[...] = value[...] if part is None else value[part]

    for index, (flag_of, part) in enumerate(choices):
        flag = flag_of(*place)
        first, second, out = refs[2 * index], refs[2 * index + 1], outs[index]
        pl.when(flag)(functools.partial(put, out, first, part))
        pl.when(jnp.logical_not(flag))(functools.partial(put, out, second, part))


def pick(*choices):
    args = [value for choice in choices for value in choice[1:3]]
    shapes = [a.shape if choice[3] is None else a.shape[1:] for a, choice in zip(args[::2], choices)]
    return pl.pallas_call(
        functools.partial(pick_kernel, [(choice[0], choice[3]) for choice in choices]),
        out_shape=tuple(jax.ShapeDtypeStruct(shape, args[0].dtype) for shape in shapes),
        in_specs=[VMEM] * len(args),
        out_specs=(VMEM,) * len(choices),
        compiler_params=PARAMS,
    )(*args)


def columns_kernel(turns, block, core_rows, turn_of, *refs):
    plane, side, core = here()
    half = refs[0].shape[2]
    for index, turn in enumerate(turns):
        first = (2 * turn_of(plane, turn) + side) * block
        own = first // half == core
        cols = pl.ds(pl.multiple_of(lax.rem(first, half), block), block)
        for slot in range(2):
            out = refs[4 + slot]
            for position, reader in enumerate((core, 1 - core)):
                at = pl.ds(pl.multiple_of(reader * core_rows, core_rows), core_rows)
                for part in range(2):
                    value = jnp.where(own, refs[2 * slot][part, at, cols], refs[2 * slot + 1][part, at, cols])
                    start = (2 * position + part) * core_rows
                    out[index * block : (index + 1) * block, start : start + core_rows] = value.T


def outer_kernel(first, block, pairs, base, *refs):
    half = refs[1].shape[1]
    straight, turned = [], []
    for index in range(pairs):
        for w in refs[3 * index + 1 : 3 * index + 3]:
            rows = w.shape[0] // 2
            straight.append(w[...])
            turned.extend([w[rows:, :], -w[:rows, :]])
    straight = jnp.concatenate(straight, axis=0)
    turned = jnp.concatenate(turned, axis=0)
    for index, out in enumerate(refs[3 * pairs + base :]):
        at = slice((first + index) * block, (first + index + 1) * block)
        a = jnp.concatenate([refs[3 * pair][at, :] for pair in range(pairs)], axis=1)
        real = dot(a, straight)
        imag = dot(a, turned)
        if base:
            begin = 2 * (first + index) * block
            real += refs[3 * pairs][begin : begin + block, :]
            imag += refs[3 * pairs][begin + block : begin + 2 * block, :]
        if out.shape[0] > 2 * block:
            top = jnp.maximum(jnp.max(jnp.abs(real)), jnp.max(jnp.abs(imag)))
            power = 14.0 - jnp.ceil(jnp.log2(jnp.full((PAD_ROWS, half), jnp.maximum(top, 1e-30), F32)))
            power = jnp.clip(power, -110.0, 110.0)
            scale = jnp.exp2(power)[:1]
            out[:block, :] = real * scale
            out[block : 2 * block, :] = imag * scale
            out[2 * block :, :] = power
        else:
            out[:block, :] = real
            out[block:, :] = imag


def base_kernel(block, a_ref, w_own, w_other, out):
    rows = w_own.shape[0] // 2
    straight = jnp.concatenate([w_own[...], w_other[...]], axis=0)
    turned = jnp.concatenate([w_own[rows:, :], -w_own[:rows, :], w_other[rows:, :], -w_other[:rows, :]], axis=0)
    for index in range(a_ref.shape[0] // block):
        a = a_ref[index * block : (index + 1) * block, :]
        out[2 * index * block : (2 * index + 1) * block, :] = dot(a, straight)
        out[(2 * index + 1) * block : (2 * index + 2) * block, :] = dot(a, turned)


def lay_kernel(total, out):
    block = out.shape[0]
    out[:, 0, :] = total[:block, :]
    out[:, 1, :] = total[block:, :]


def shards(green, direction, partners, counts):
    shape = partners.shape
    rows, half = green.shape[1:]
    count = lax.axis_size("tile")
    planes = count // 2
    last_plane = planes - 1

    def other_side(index):
        return index ^ 1

    def even_pair(index):
        return index ^ 2

    def odd_pair(index):
        target = (index // 2 - 1 ^ 1) + 1
        return 2 * target + index % 2 if 0 <= target < planes else -1

    def turned(p, turn):
        return p ^ turn if planes == 4 else lax.rem(p + turn, planes) if isinstance(p, jax.Array) else (p + turn) % planes

    def group(p, s):
        return 2 * p + s

    def slot_group(plane, slot):
        second = jnp.where(plane < 2, 1, 0) if planes == 4 else 1
        return second if slot else 1 - second

    def first_mine(plane, side, core):
        return side == slot_group(plane, 0)

    def second_mine(plane, side, core):
        return side == slot_group(plane, 1)

    direction_other = cores(direction)
    green_other = cores(green)
    mate = move(green, other_side)
    pair = move(green, even_pair)
    next_pair = move(green, odd_pair)
    late_partners, green_other = lax.optimization_barrier((partners, green_other))
    table = pl.pallas_call(
        table_kernel,
        out_shape=jax.ShapeDtypeStruct((8, 128), jnp.int32),
        in_specs=[SMEM, SMEM],
        out_specs=VMEM,
        compiler_params=PARAMS,
    )(late_partners, counts)
    table_mate = move(table, other_side)
    mate, direction_other, green_other, table_mate = lax.optimization_barrier(
        (mate, direction_other, green_other, table_mate)
    )

    def by_side(plane, side, core):
        return side == plane % 2

    def by_pair(plane, side, core):
        return jnp.where(plane % 2 == 1, (side == 0) & (plane < last_plane), (side == 1) & (plane > 0))

    def by_next(plane, side, core):
        return jnp.where(plane % 2 == 1, side == 1, (side == 0) & (plane < last_plane))

    near_sent, pair_sent, next_sent = pick(
        (by_side, next_pair, pair, None),
        (by_pair, next_pair, mate, None),
        (by_next, pair, mate, None),
    )
    pair_two = move(pair_sent, even_pair)
    next_two = move(next_sent, odd_pair)
    near = move(near_sent, other_side)
    mate_other = cores(mate)
    pair_other = cores(pair)
    next_other = cores(next_pair)

    def first_groups(plane, side):
        odd = plane % 2 == 1
        return [
            group(plane, side),
            group(plane, 1 - side),
            group(jnp.where(odd, plane - 1, plane + 1), side),
            group(jnp.where(odd, plane + 1, plane - 1), side),
        ]

    def second_groups(plane, side):
        odd = plane % 2 == 1
        from_above = jnp.where(
            side == 0,
            jnp.where(plane + 1 == last_plane, group(plane + 1, 1), group(plane + 2, 0)),
            group(plane + 1, 0),
        )
        from_below = jnp.where(
            side == 0, group(plane - 1, 1), jnp.where(plane == 1, group(0, 0), group(plane - 2, 1))
        )
        return [
            jnp.where(
                side == 0,
                jnp.where(plane <= planes - 3, group(plane + 1, 1), NOWHERE),
                jnp.where(plane >= 2, group(plane - 1, 0), NOWHERE),
            ),
            jnp.where(odd, from_below, from_above),
            jnp.where(odd, from_above, from_below),
        ]

    def third_groups(plane, side):
        return [
            jnp.where(
                side == 0,
                jnp.where(plane >= 2, group(plane - 2, 1), NOWHERE),
                jnp.where(plane <= planes - 3, group(plane + 2, 0), NOWHERE),
            )
        ]

    rows_of = pick(
        (first_mine, green, mate, None),
        (first_mine, green_other, mate_other, None),
        (second_mine, green, mate, None),
        (second_mine, green_other, mate_other, None),
    )
    core_rows = rows // 2
    left = pl.pallas_call(
        functools.partial(images_kernel, core_rows),
        out_shape=jax.ShapeDtypeStruct((2 * rows, 4 * half), BF16),
        in_specs=[VMEM] * 6,
        out_specs=VMEM,
        compiler_params=PARAMS,
        cost_estimate=pl.CostEstimate(
            flops=2 * 4 * rows * 4 * half * half, bytes_accessed=8 * 1024 * 1024, transcendentals=0
        ),
    )(*rows_of, direction, direction_other)

    block = 2 * half // count
    turns = [2, 3, 1, 0] if planes == 4 else [*range(1, planes), 0]
    if block % 128 == 0:
        columns = pl.pallas_call(
            functools.partial(columns_kernel, turns, block, core_rows, turned),
            out_shape=(jax.ShapeDtypeStruct((planes * block, 2 * rows), BF16),) * 2,
            in_specs=[VMEM] * 4,
            out_specs=(VMEM,) * 2,
            compiler_params=PARAMS,
        )(*rows_of)
    else:
        plane, side, core = here()

        def transposed(own, other):
            both = jnp.concatenate([jnp.where(core == 0, own, other), jnp.where(core == 0, other, own)], axis=2)
            both = both.reshape(2, 2, core_rows, planes, 2, block)
            both = lax.dynamic_index_in_dim(both, side, 4, keepdims=False)
            both = jnp.take(both, jnp.stack([turned(plane, turn) for turn in turns]), axis=3)
            both = jnp.where(core == 0, both, both[:, ::-1])
            return both.transpose(3, 4, 1, 0, 2).reshape(planes * block, 2 * rows)

        columns = [transposed(*rows_of[:2]), transposed(*rows_of[2:])]

    add = functools.partial(window_call, (table, table_mate), shape, slot_group)
    sums = add(
        first_groups,
        left,
        [
            ([green], [green_other]),
            ([mate], [mate_other]),
            ([pair], [pair_other]),
            ([next_pair], [next_other]),
        ],
        None,
        (0, 1),
        (),
    )
    pair_two, next_two, sums, columns = lax.optimization_barrier((pair_two, next_two, sums, columns))
    far_real, far_imag = pick(
        (by_side, pair_two, next_two, 0), (by_side, next_two, pair_two, 1)
    )
    far = [move(far_real, other_side), move(far_imag, lambda i: i - 2 if i % 2 else i + 2)]
    far_slots = (1,) if planes == 4 else (0, 1)
    sums = add(
        second_groups,
        left,
        [([block_of], [cores(block_of)]) for block_of in (near, pair_two, next_two)],
        sums,
        (0, 1),
        () if planes != 4 else (0,),
    )
    operands = []
    if planes == 4:
        base = pl.pallas_call(
            functools.partial(base_kernel, block),
            out_shape=jax.ShapeDtypeStruct((2 * planes * block, half), F32),
            in_specs=[VMEM] * 3,
            out_specs=VMEM,
            compiler_params=PARAMS,
        )(columns[0], sums[0], cores(sums[1]))
        sums = sums[2:]
        far, sums = lax.optimization_barrier((far, sums))
        operands = [base]
    else:
        far, sums = lax.optimization_barrier((far, sums))
    weighted = add(third_groups, left, [(far, [cores(part) for part in far])], sums, far_slots, far_slots)
    pairs = [
        operand
        for position, slot in enumerate(far_slots)
        for operand in (columns[slot], weighted[2 * position], cores(weighted[2 * position + 1]))
    ]
    operands = pairs + operands

    def terms(first, turns):
        pads = [PAD_ROWS if turn else 0 for turn in turns]
        return pl.pallas_call(
            functools.partial(outer_kernel, first, block, len(pairs) // 3, len(operands) - len(pairs)),
            out_shape=tuple(jax.ShapeDtypeStruct((2 * block + pad, half), F32) for pad in pads),
            in_specs=[VMEM] * len(operands),
            out_specs=(VMEM,) * len(turns),
            compiler_params=PARAMS,
            cost_estimate=pl.CostEstimate(
                flops=2 * len(turns) * block * 4 * rows * 2 * half,
                bytes_accessed=4 * 1024 * 1024,
                transcendentals=0,
            ),
        )(*operands)

    ahead = len(turns) // 4
    sent = terms(0, turns[:ahead]) + terms(ahead, turns[ahead:-1])
    (total,) = terms(planes - 1, turns[-1:])
    for turn, term in zip(turns, sent):
        got = move(term.astype(jnp.float16), lambda index: turned(index // 2, turn) * 2 + index % 2).astype(F32)
        total = total + got[: 2 * block] * jnp.exp2(-got[2 * block : 2 * block + 1])
    return pl.pallas_call(
        lay_kernel,
        out_shape=jax.ShapeDtypeStruct((block, 2, half), F32),
        in_specs=[VMEM],
        out_specs=VMEM,
        compiler_params=PARAMS,
    )(total)


def solution(mesh):
    in_specs = (
        P(None, ("freq", "tile"), "src"),
        P(None, ("freq", "src"), None),
        P(("freq", "tile"), None),
        P(("freq", "tile")),
    )
    out_specs = P(("freq", "tile"), None, "src")
    return jax.shard_map(shards, mesh=mesh, in_specs=in_specs, out_specs=out_specs, check_vma=False)
```

```python
import functools

import jax
import jax.numpy as jnp
from jax import lax
from jax.experimental import pallas as pl
from jax.experimental.pallas import tpu as pltpu
from jax.sharding import PartitionSpec as P

F32 = jnp.float32
BF16 = jnp.bfloat16
NOWHERE = -4000
BAND_DEV = 3
PAD_ROWS = 8
TABLE_ROWS = 8
SMEM = pl.BlockSpec(memory_space=pltpu.SMEM)
VMEM = pl.BlockSpec(memory_space=pltpu.VMEM)
PARAMS = pltpu.CompilerParams(vmem_limit_bytes=24 * 1024 * 1024)


def move(value, target):
    count = lax.axis_size("tile")
    pairs = [(source, target(source)) for source in range(count) if 0 <= target(source) < count]
    return lax.ppermute(value, "tile", pairs)


def here():
    place = lax.axis_index("tile")
    return place // 2, place % 2, lax.axis_index("src")


def cores(value):
    return lax.ppermute(value, "src", [(0, 1), (1, 0)])


def dot(a, b):
    return jnp.dot(a, b, preferred_element_type=F32)


def dot_t(a, b):
    return lax.dot_general(a, b, (((1,), (1,)), ((), ())), preferred_element_type=F32)


def images_kernel(core_rows, slots, *refs):
    v_own, v_other, left = refs[2 * slots :]
    half = v_own.shape[1]
    core = lax.axis_index("src")
    at = pl.ds(pl.multiple_of(core * core_rows, core_rows), core_rows)
    sensors = []
    for own, other in zip(refs[: 2 * slots : 2], refs[1 : 2 * slots : 2]):
        own_real, own_imag, other_real, other_imag = own[0, at, :], own[1, at, :], other[0, at, :], other[1, at, :]
        sensors.append(jnp.concatenate([own_real, -own_imag, other_real, -other_imag], axis=1))
        sensors.append(jnp.concatenate([own_imag, own_real, other_imag, other_real], axis=1))
    sensors = jnp.concatenate(sensors, axis=0)
    for index, column in enumerate((core, 1 - core)):
        cols = pl.ds(pl.multiple_of(column * half, half), half)
        values = jnp.concatenate(
            [v_own[0, :, cols], v_own[1, :, cols], v_other[0, :, cols], v_other[1, :, cols]], axis=0
        )
        images = dot(sensors, values).astype(BF16)
        first = slice(2 * index * half, (2 * index + 1) * half)
        second = slice((2 * index + 1) * half, (2 * index + 2) * half)
        left[:, first] = images
        for slot in range(slots):
            real = slice(2 * slot * core_rows, (2 * slot + 1) * core_rows)
            imag = slice((2 * slot + 1) * core_rows, (2 * slot + 2) * core_rows)
            left[real, second] = images[imag]
            left[imag, second] = -images[real]


def images_call(core_rows, groups, direction, direction_other):
    half = direction.shape[1]
    args = [array for pair in groups for array in pair] + [direction, direction_other]
    return pl.pallas_call(
        functools.partial(images_kernel, core_rows, len(groups)),
        out_shape=jax.ShapeDtypeStruct((2 * len(groups) * core_rows, 4 * half), BF16),
        in_specs=[VMEM] * len(args),
        out_specs=VMEM,
        compiler_params=PARAMS,
        cost_estimate=pl.CostEstimate(
            flops=2 * len(groups) * 2 * core_rows * 8 * half * half, bytes_accessed=6 * 1024 * 1024, transcendentals=0
        ),
    )(*args)


def table_kernel(partners_ref, counts_ref, table_ref):
    row = lax.broadcasted_iota(jnp.int32, table_ref.shape, 0)
    col = lax.broadcasted_iota(jnp.int32, table_ref.shape, 1)
    tile_rows, kmax = partners_ref.shape
    table = jnp.zeros(table_ref.shape, F32)
    for r in range(tile_rows):
        for k in range(kmax + 1):
            value = partners_ref[r, k] if k < kmax else counts_ref[r]
            table = jnp.where((row == r) & (col == k), value.astype(F32), table)
    table_ref[...] = table


def extend_kernel(block_ref, table_ref, out):
    rows = block_ref.shape[1]
    lanes = table_ref.shape[1]
    for part in range(2):
        out[part, :rows, :] = block_ref[part]
        out[part, rows:, :lanes] = table_ref[...].astype(BF16)
        out[part, rows:, lanes:] = jnp.zeros((TABLE_ROWS, out.shape[2] - lanes), BF16)


def sampled_kernel(kmax, row_tiles, slots, *refs):
    out = refs[-1]
    plane, side, core = here()
    lanes = out.shape[1]

    def table_of(ref):
        return ref[...] if len(ref.shape) == 2 else ref[0, ref.shape[1] - TABLE_ROWS :, :lanes].astype(F32)

    sublane = lax.broadcasted_iota(jnp.int32, (TABLE_ROWS, lanes), 0)
    lane = lax.broadcasted_iota(jnp.int32, (1, lanes), 1)
    out[...] = jnp.full(out.shape, NOWHERE, F32)
    for slot, mine_of in enumerate(slots):
        table = jnp.where(mine_of(plane, side), table_of(refs[2 * slot]), table_of(refs[2 * slot + 1]))
        for row_tile in range(row_tiles):
            wanted = core * row_tiles + row_tile
            row = jnp.sum(jnp.where(sublane == wanted, table, 0.0), axis=0, keepdims=True)
            count = jnp.sum(jnp.where(lane == kmax, row, 0.0), axis=1, keepdims=True)
            count = jnp.where((plane == 0) | (plane == 3), 0.0, count)
            at = slot * row_tiles + row_tile
            out[at : at + 1, :] = jnp.where(lane.astype(F32) < jnp.minimum(count, kmax), row, NOWHERE)


def sampled_call(shape, slots):
    tiles, kmax = shape
    args = [array for slot in slots for array in slot[1:]]
    return pl.pallas_call(
        functools.partial(sampled_kernel, kmax, tiles // 2, [slot[0] for slot in slots]),
        out_shape=jax.ShapeDtypeStruct((8, 128), F32),
        in_specs=[VMEM] * len(args),
        out_specs=VMEM,
        compiler_params=PARAMS,
    )(*args)


def window_kernel(blocks, slots, skip, shape, done, start, sampled, left, *refs):
    plane, side, core = here()
    tiles = shape[0]
    row_tiles = tiles // 2
    core_rows = left.shape[0] // (2 * (skip + slots)) if not skip else refs[1].shape[0] // 2
    rows = 2 * core_rows
    held = []
    for group_of, width in blocks:
        halves = []
        for _ in range(2):
            if width == 1:
                halves.append((refs[0][0, :rows, :], refs[0][1, :rows, :]))
            else:
                late = side == plane % 2
                whole, real, imag = refs[:3]
                halves.append(
                    (jnp.where(late, real[...], whole[0, :rows, :]), jnp.where(late, imag[...], whole[1, :rows, :]))
                )
            refs = refs[width:]
        held.append((group_of(plane, side), *halves))
    tile = core_rows // row_tiles
    sums, outs, couples = refs[: 0 if start else 2 * slots], refs[-2 * slots - 1 : -1], refs[-1]
    left_rows = left[skip * rows : (skip + slots) * rows, :]
    wide = tiles * tile
    for block, (group, own, other) in enumerate(held):
        couple = dot_t(left_rows, jnp.concatenate([*own, *other], axis=1))
        for index in range(slots * row_tiles):
            partners = sampled[skip * row_tiles + index : skip * row_tiles + index + 1, :]
            begin = index // row_tiles * rows + index % row_tiles * tile
            upper = slice(begin, begin + tile)
            lower = slice(begin + core_rows, begin + core_rows + tile)
            for c in range(tiles):
                wanted = (group * tiles + c).astype(F32)
                keep = jnp.max(jnp.where(partners == wanted, 1.0, 0.0), axis=1, keepdims=True)
                real = (couple[upper, c * tile : (c + 1) * tile] * keep).astype(BF16)
                imag = (couple[lower, c * tile : (c + 1) * tile] * keep).astype(BF16)
                at = 2 * block * wide + c * tile
                couples[upper, at : at + tile] = real
                couples[lower, at : at + tile] = imag
                couples[upper, at + wide : at + wide + tile] = -imag
                couples[lower, at + wide : at + wide + tile] = real
    for index in range(2):
        values = jnp.concatenate([part for block in held for part in block[1 + index]], axis=0)
        total = dot(couples[...], values)
        for slot in range(slots):
            part = total[slot * rows : (slot + 1) * rows]
            if not start:
                part = part + sums[2 * slot + index][...]
            outs[2 * slot + index][...] = part.astype(BF16) if slot in done else part


def window_call(sampled, shape, rows, left, skip, slots, blocks, sums, done):
    args = [sampled, left]
    for _, own, other in blocks:
        args.extend(own)
        args.extend(other)
    if sums is not None:
        args.extend(sums)
    half = left.shape[1] // 4
    outs = [jax.ShapeDtypeStruct((rows, half), BF16 if slot in done else F32) for slot in range(slots) for _ in range(2)]
    return pl.pallas_call(
        functools.partial(
            window_kernel, [(group_of, len(own)) for group_of, own, _ in blocks], slots, skip, shape, done, sums is None
        ),
        out_shape=tuple(outs),
        in_specs=[VMEM] * len(args),
        out_specs=(VMEM,) * len(outs),
        scratch_shapes=[pltpu.VMEM((slots * rows, 2 * len(blocks) * rows), BF16)],
        compiler_params=PARAMS,
        cost_estimate=pl.CostEstimate(
            flops=len(blocks) * slots * 2 * 2 * rows * 4 * half * rows,
            bytes_accessed=sum(a.size * a.dtype.itemsize for a in args),
            transcendentals=0,
        ),
    )(*args)


def pick_kernel(choices, *refs):
    place = here()
    outs = refs[len(refs) - len(choices) :]

    def put(out, value, part):
        out[...] = value[...] if part is None else value[part, : out.shape[0], :]

    for index, (flag_of, part) in enumerate(choices):
        flag = flag_of(*place)
        first, second, out = refs[2 * index], refs[2 * index + 1], outs[index]
        pl.when(flag)(functools.partial(put, out, first, part))
        pl.when(jnp.logical_not(flag))(functools.partial(put, out, second, part))


def pick(*choices, rows=None):
    args = [value for choice in choices for value in choice[1:3]]
    shapes = [
        a.shape if choice[3] is None else (rows, a.shape[2]) for a, choice in zip(args[::2], choices)
    ]
    return pl.pallas_call(
        functools.partial(pick_kernel, [(choice[0], choice[3]) for choice in choices]),
        out_shape=tuple(jax.ShapeDtypeStruct(shape, args[0].dtype) for shape in shapes),
        in_specs=[VMEM] * len(args),
        out_specs=(VMEM,) * len(choices),
        compiler_params=PARAMS,
    )(*args)


def columns_kernel(turns, block, core_rows, *refs):
    plane, side, core = here()
    slots = len(refs) // 3
    half = refs[0].shape[2]
    for index, turn in enumerate(turns):
        first = (2 * (plane ^ turn) + side) * block
        own = first // half == core
        cols = pl.ds(pl.multiple_of(lax.rem(first, half), block), block)
        for slot in range(slots):
            out = refs[2 * slots + slot]
            for position, reader in enumerate((core, 1 - core)):
                at = pl.ds(pl.multiple_of(reader * core_rows, core_rows), core_rows)
                for part in range(2):
                    value = jnp.where(own, refs[2 * slot][part, at, cols], refs[2 * slot + 1][part, at, cols])
                    start = (2 * position + part) * core_rows
                    out[index * block : (index + 1) * block, start : start + core_rows] = value.T


def columns_call(turns, block, core_rows, groups):
    args = [array for pair in groups for array in pair]
    out = jax.ShapeDtypeStruct((len(turns) * block, 4 * core_rows), BF16)
    return pl.pallas_call(
        functools.partial(columns_kernel, turns, block, core_rows),
        out_shape=(out,) * len(groups),
        in_specs=[VMEM] * len(args),
        out_specs=(VMEM,) * len(groups),
        compiler_params=PARAMS,
    )(*args)


def outer_kernel(first, block, pairs, base, *refs):
    half = refs[1].shape[1]
    straight, turned = [], []
    for index in range(pairs):
        for w in refs[3 * index + 1 : 3 * index + 3]:
            rows = w.shape[0] // 2
            straight.append(w[...])
            turned.extend([w[rows:, :], -w[:rows, :]])
    straight = jnp.concatenate(straight, axis=0)
    turned = jnp.concatenate(turned, axis=0)
    for index, out in enumerate(refs[3 * pairs + base :]):
        at = slice((first + index) * block, (first + index + 1) * block)
        a = jnp.concatenate([refs[3 * pair][at, :] for pair in range(pairs)], axis=1)
        real = dot(a, straight)
        imag = dot(a, turned)
        if base:
            begin = 2 * (first + index) * block
            real += refs[3 * pairs][begin : begin + block, :]
            imag += refs[3 * pairs][begin + block : begin + 2 * block, :]
        if out.shape[0] > 2 * block:
            top = jnp.maximum(jnp.max(jnp.abs(real)), jnp.max(jnp.abs(imag)))
            power = 14.0 - jnp.ceil(jnp.log2(jnp.full((PAD_ROWS, half), jnp.maximum(top, 1e-30), F32)))
            power = jnp.clip(power, -110.0, 110.0)
            scale = jnp.exp2(power)[:1]
            out[:block, :] = real * scale
            out[block : 2 * block, :] = imag * scale
            out[2 * block :, :] = power
        else:
            out[:block, :] = real
            out[block:, :] = imag


def base_kernel(block, *refs):
    out = refs[-1]
    straight, turned = [], []
    for index in range(len(refs) // 3):
        for w in refs[3 * index + 1 : 3 * index + 3]:
            rows = w.shape[0] // 2
            straight.append(w[...])
            turned.extend([w[rows:, :], -w[:rows, :]])
    straight = jnp.concatenate(straight, axis=0)
    turned = jnp.concatenate(turned, axis=0)
    for index in range(out.shape[0] // (2 * block)):
        a = jnp.concatenate([ref[index * block : (index + 1) * block, :] for ref in refs[:-1:3]], axis=1)
        out[2 * index * block : (2 * index + 1) * block, :] = dot(a, straight)
        out[(2 * index + 1) * block : (2 * index + 2) * block, :] = dot(a, turned)


def lay_kernel(total, out):
    block = out.shape[0]
    out[:, 0, :] = total[:block, :]
    out[:, 1, :] = total[block:, :]


def from_behind(value, axis, steps):
    count = lax.axis_size(axis)
    first, last = (max(0, -steps), min(count, count - steps))
    return lax.ppermute(value, axis, [(source, source + steps) for source in range(first, last)])


def any_shards(green, direction, partners, counts):
    tile_dev, kmax = partners.shape
    rows = green.shape[1]
    half = green.shape[2]
    tile = rows // tile_dev
    real_part = jnp.dot(green[0], direction[0], preferred_element_type=jnp.float32) - jnp.dot(
        green[1], direction[1], preferred_element_type=jnp.float32
    )
    imag_part = jnp.dot(green[0], direction[1], preferred_element_type=jnp.float32) + jnp.dot(
        green[1], direction[0], preferred_element_type=jnp.float32
    )
    images = lax.psum_scatter(
        jnp.stack([real_part, imag_part]), "src", scatter_dimension=2, tiled=True
    ).astype(jnp.bfloat16)
    tiles = green.reshape(2, tile_dev, tile, half)
    count_tile = lax.axis_size("tile")
    reach = min(BAND_DEV, count_tile - 1)
    empty = jnp.zeros_like(tiles)
    offsets = [offset for offset in range(-reach, reach + 1) if offset != 0]
    moved = [from_behind(tiles, "tile", -offset) for offset in offsets]
    nearby = dict(zip(offsets, moved))
    nearby[0] = tiles
    window = jnp.concatenate(
        [nearby.get(offset, empty) for offset in range(-BAND_DEV, BAND_DEV + 1)], axis=1
    )
    first_tile = (lax.axis_index("tile") - BAND_DEV) * tile_dev
    local_index = partners - first_tile
    live = (jnp.arange(kmax, dtype=jnp.int32)[None, :] < counts[:, None]).astype(jnp.float32)
    across = (((1,), (1,)), ((), ()))
    stacks = []
    pieces = []
    for row in range(tile_dev):
        stack = jnp.take(window, local_index[row], axis=1).reshape(2, kmax * tile, half)
        stacks.append(stack)
        image_row = images[:, row * tile : (row + 1) * tile]
        couple_real = lax.dot_general(
            image_row[0], stack[0], across, preferred_element_type=jnp.float32
        ) + lax.dot_general(image_row[1], stack[1], across, preferred_element_type=jnp.float32)
        couple_imag = lax.dot_general(
            image_row[1], stack[0], across, preferred_element_type=jnp.float32
        ) - lax.dot_general(image_row[0], stack[1], across, preferred_element_type=jnp.float32)
        blocks = jnp.stack([couple_real, couple_imag]).reshape(2, tile, kmax, tile)
        pieces.append(blocks * live[row][None, None, :, None])
    partial_blocks = jnp.stack(pieces, axis=1)
    coupling = lax.psum(partial_blocks, "src").astype(jnp.bfloat16)
    weight_rows = []
    for row in range(tile_dev):
        stack = stacks[row]
        flat = coupling[:, row].reshape(2, tile, kmax * tile)
        weight_real = jnp.dot(flat[0], stack[0], preferred_element_type=jnp.float32) - jnp.dot(
            flat[1], stack[1], preferred_element_type=jnp.float32
        )
        weight_imag = jnp.dot(flat[0], stack[1], preferred_element_type=jnp.float32) + jnp.dot(
            flat[1], stack[0], preferred_element_type=jnp.float32
        )
        weight_rows.append(jnp.stack([weight_real, weight_imag]))
    weighted = jnp.concatenate(weight_rows, axis=1).astype(jnp.bfloat16)
    full_rows = lax.all_gather(green, "src", axis=2, tiled=True)
    down = (((0,), (0,)), ((), ()))
    out_real = lax.dot_general(
        full_rows[0], weighted[0], down, preferred_element_type=jnp.float32
    ) + lax.dot_general(full_rows[1], weighted[1], down, preferred_element_type=jnp.float32)
    out_imag = lax.dot_general(
        full_rows[0], weighted[1], down, preferred_element_type=jnp.float32
    ) - lax.dot_general(full_rows[1], weighted[0], down, preferred_element_type=jnp.float32)
    return lax.psum_scatter(
        jnp.stack([out_real, out_imag], axis=1), "tile", scatter_dimension=0, tiled=True
    )


def four_shards(green, direction, partners, counts):
    shape = partners.shape
    rows, half = green.shape[1:]
    core_rows = rows // 2
    block = 2 * half // lax.axis_size("tile")
    turns = [2, 3, 1, 0]

    def other_side(index):
        return index ^ 1

    def even_pair(index):
        return index ^ 2

    def odd_pair(index):
        return index ^ 6 if inner(index) else -1

    def inner(index):
        return index // 2 in (1, 2)

    def early(index):
        return inner(index) and index // 2 % 2 != index % 2

    def second_mine(plane, side, core=None):
        return jnp.where(plane < 2, side, 1 - side) == 1

    def first_mine(plane, side, core=None):
        return jnp.where(plane < 2, side, 1 - side) == 0

    def always(plane, side, core=None):
        return plane >= 0

    def of_own(plane, side):
        return 2 * plane + side

    def of_mate(plane, side):
        return 2 * plane + 1 - side

    def of_pair(plane, side):
        return 2 * (plane ^ 1) + side

    def of_next(plane, side):
        return 2 * (3 - plane) + side

    def of_across(plane, side):
        return 2 * (plane ^ 1) + 1 - side

    def of_near(plane, side):
        return 2 * (3 - plane) + 1 - side

    def of_far(plane, side):
        return jnp.where(plane < 2, 6, 1)

    direction_other = cores(direction)
    green_other = cores(green)
    mate = move(green, other_side)
    pair = move(green, even_pair)
    beyond = move(green, odd_pair)
    late_partners, green_other = lax.optimization_barrier((partners, green_other))
    table = pl.pallas_call(
        table_kernel,
        out_shape=jax.ShapeDtypeStruct((TABLE_ROWS, 128), F32),
        in_specs=[SMEM, SMEM],
        out_specs=VMEM,
        compiler_params=PARAMS,
    )(late_partners, counts)
    table_mate = move(table, other_side)
    late_table, direction_other = lax.optimization_barrier((table, direction_other))
    table_pair = move(late_table, even_pair)
    mate, direction_other, green_other, table_mate = lax.optimization_barrier(
        (mate, direction_other, green_other, table_mate)
    )
    pair, beyond, table_pair = lax.optimization_barrier((pair, beyond, table_pair))

    mate_sent = pl.pallas_call(
        extend_kernel,
        out_shape=jax.ShapeDtypeStruct((2, rows + TABLE_ROWS, half), BF16),
        in_specs=[VMEM, VMEM],
        out_specs=VMEM,
        compiler_params=PARAMS,
    )(mate, table_mate)
    across = move(mate_sent, lambda i: -1 if inner(i) else even_pair(i))
    ahead = move(pair, lambda i: odd_pair(i) if inner(i) and not early(i) else -1)
    near = move(beyond, lambda i: other_side(i) if inner(i) else -1)
    mate_other = cores(mate)
    pair_other = cores(pair)
    beyond_other = cores(beyond)

    first_rows = pick(
        (first_mine, green, mate, None),
        (first_mine, green_other, mate_other, None),
        (second_mine, green, mate, None),
        (second_mine, green_other, mate_other, None),
    )
    row_groups = [first_rows[:2], first_rows[2:], (pair, pair_other)]
    left = images_call(core_rows, row_groups, direction, direction_other)
    columns = columns_call(turns, block, core_rows, row_groups)

    sampled = sampled_call(
        shape,
        [(first_mine, table, table_mate), (second_mine, table, table_mate), (always, table_pair, table_pair)],
    )
    first_blocks = [
        (of_own, [green], [green_other]),
        (of_mate, [mate], [mate_other]),
        (of_pair, [pair], [pair_other]),
        (of_next, [beyond], [beyond_other]),
    ]
    sums = window_call(sampled, shape, rows, left, 0, 3, first_blocks, None, ())
    across, ahead, sums, columns = lax.optimization_barrier((across, ahead, sums, columns))

    far_real, far_imag = pick((always, ahead, ahead, 0), (always, across, across, 1), rows=rows)
    far_real = move(far_real, lambda i: other_side(i) if early(i) else -1)
    far_imag = move(far_imag, lambda i: odd_pair(i) if early(i) else -1)
    across_other = cores(across)
    last_row = (across, across_other)
    across_block = (of_across, [across], [across_other])
    sums = window_call(
        sampled, shape, rows, left, 0, 3, [across_block, (of_near, [near], [cores(near)])], sums, (0, 2)
    )
    last_left = images_call(core_rows, [last_row], direction, direction_other)
    last_sampled = sampled_call(shape, [(always, across, across)])
    last_sums = window_call(
        last_sampled, shape, rows, last_left, 0, 1, [*first_blocks, across_block], None, (0,)
    )
    (last_columns,) = columns_call(turns, block, core_rows, [last_row])
    done = [
        columns[0], sums[0], cores(sums[1]),
        columns[2], sums[4], cores(sums[5]),
        last_columns, last_sums[0], cores(last_sums[1]),
    ]
    base = pl.pallas_call(
        functools.partial(base_kernel, block),
        out_shape=jax.ShapeDtypeStruct((2 * len(turns) * block, half), F32),
        in_specs=[VMEM] * len(done),
        out_specs=VMEM,
        compiler_params=PARAMS,
    )(*done)
    ahead_other = cores(ahead)
    far_real, far_imag, sums, last_sums = lax.optimization_barrier((far_real, far_imag, sums, last_sums))
    weighted = window_call(
        sampled,
        shape,
        rows,
        left,
        1,
        1,
        [(of_far, [ahead, far_real, far_imag], [ahead_other, cores(far_real), cores(far_imag)])],
        sums[2:4],
        (0,),
    )
    operands = [columns[1], weighted[0], cores(weighted[1]), base]

    def terms(first, turns):
        pads = [PAD_ROWS if turn else 0 for turn in turns]
        return pl.pallas_call(
            functools.partial(outer_kernel, first, block, 1, 1),
            out_shape=tuple(jax.ShapeDtypeStruct((2 * block + pad, half), F32) for pad in pads),
            in_specs=[VMEM] * len(operands),
            out_specs=(VMEM,) * len(turns),
            compiler_params=PARAMS,
        )(*operands)

    sent = terms(0, turns[:1]) + terms(1, turns[1:-1])
    (total,) = terms(len(turns) - 1, turns[-1:])
    for turn, term in zip(turns, sent):
        got = move(term.astype(jnp.float16), lambda i: i ^ 2 * turn if inner(i) else -1).astype(F32)
        total = total + got[: 2 * block] * jnp.exp2(-got[2 * block : 2 * block + 1])
    return pl.pallas_call(
        lay_kernel,
        out_shape=jax.ShapeDtypeStruct((block, 2, half), F32),
        in_specs=[VMEM],
        out_specs=VMEM,
        compiler_params=PARAMS,
    )(total)


def solution(mesh):
    in_specs = (
        P(None, ("freq", "tile"), "src"),
        P(None, ("freq", "src"), None),
        P(("freq", "tile"), None),
        P(("freq", "tile")),
    )
    out_specs = P(("freq", "tile"), None, "src")
    shards = four_shards if mesh.shape["tile"] == 8 else any_shards
    return jax.shard_map(shards, mesh=mesh, in_specs=in_specs, out_specs=out_specs, check_vma=False)
```

```python
import functools

import jax
import jax.numpy as jnp
from jax import lax
from jax.experimental import pallas as pl
from jax.experimental.pallas import tpu as pltpu
from jax.sharding import PartitionSpec as P

F32 = jnp.float32
BF16 = jnp.bfloat16
NOWHERE = -4000
BAND_DEV = 3
PAD_ROWS = 8
TABLE_ROWS = 8
SMEM = pl.BlockSpec(memory_space=pltpu.SMEM)
VMEM = pl.BlockSpec(memory_space=pltpu.VMEM)
PARAMS = pltpu.CompilerParams(vmem_limit_bytes=24 * 1024 * 1024)


def move(value, target):
    count = lax.axis_size("tile")
    pairs = [(source, target(source)) for source in range(count) if 0 <= target(source) < count]
    return lax.ppermute(value, "tile", pairs)


def here():
    place = lax.axis_index("tile")
    return place // 2, place % 2, lax.axis_index("src")


def cores(value):
    return lax.ppermute(value, "src", [(0, 1), (1, 0)])


def dot(a, b):
    return jnp.dot(a, b, preferred_element_type=F32)


def dot_t(a, b):
    return lax.dot_general(a, b, (((1,), (1,)), ((), ())), preferred_element_type=F32)


def images_kernel(core_rows, slots, *refs):
    v_own, v_other, left = refs[2 * slots :]
    half = v_own.shape[1]
    core = lax.axis_index("src")
    at = pl.ds(pl.multiple_of(core * core_rows, core_rows), core_rows)
    sensors = []
    for own, other in zip(refs[: 2 * slots : 2], refs[1 : 2 * slots : 2]):
        own_real, own_imag, other_real, other_imag = own[0, at, :], own[1, at, :], other[0, at, :], other[1, at, :]
        sensors.append(jnp.concatenate([own_real, -own_imag, other_real, -other_imag], axis=1))
        sensors.append(jnp.concatenate([own_imag, own_real, other_imag, other_real], axis=1))
    sensors = jnp.concatenate(sensors, axis=0)
    for index, column in enumerate((core, 1 - core)):
        cols = pl.ds(pl.multiple_of(column * half, half), half)
        values = jnp.concatenate(
            [v_own[0, :, cols], v_own[1, :, cols], v_other[0, :, cols], v_other[1, :, cols]], axis=0
        )
        images = dot(sensors, values).astype(BF16)
        first = slice(2 * index * half, (2 * index + 1) * half)
        second = slice((2 * index + 1) * half, (2 * index + 2) * half)
        left[:, first] = images
        for slot in range(slots):
            real = slice(2 * slot * core_rows, (2 * slot + 1) * core_rows)
            imag = slice((2 * slot + 1) * core_rows, (2 * slot + 2) * core_rows)
            left[real, second] = images[imag]
            left[imag, second] = -images[real]


def images_call(core_rows, groups, direction, direction_other):
    half = direction.shape[1]
    args = [array for pair in groups for array in pair] + [direction, direction_other]
    return pl.pallas_call(
        functools.partial(images_kernel, core_rows, len(groups)),
        out_shape=jax.ShapeDtypeStruct((2 * len(groups) * core_rows, 4 * half), BF16),
        in_specs=[VMEM] * len(args),
        out_specs=VMEM,
        compiler_params=PARAMS,
        cost_estimate=pl.CostEstimate(
            flops=2 * len(groups) * 2 * core_rows * 8 * half * half, bytes_accessed=6 * 1024 * 1024, transcendentals=0
        ),
    )(*args)


def table_kernel(partners_ref, counts_ref, table_ref):
    row = lax.broadcasted_iota(jnp.int32, table_ref.shape, 0)
    col = lax.broadcasted_iota(jnp.int32, table_ref.shape, 1)
    tile_rows, kmax = partners_ref.shape
    table = jnp.zeros(table_ref.shape, F32)
    for r in range(tile_rows):
        for k in range(kmax + 1):
            value = partners_ref[r, k] if k < kmax else counts_ref[r]
            table = jnp.where((row == r) & (col == k), value.astype(F32), table)
    table_ref[...] = table


def stage_kernel(count, *refs):
    sources, targets, arrived = refs[:count], refs[count:-1], refs[-1]
    copies = [pltpu.make_async_copy(a, b, arrived.at[i]) for i, (a, b) in enumerate(zip(sources, targets))]
    for copy in copies:
        copy.start()
    for copy in copies:
        copy.wait()


def stage(*arrays):
    return pl.pallas_call(
        functools.partial(stage_kernel, len(arrays)),
        out_shape=tuple(jax.ShapeDtypeStruct(a.shape, a.dtype) for a in arrays),
        in_specs=[pl.BlockSpec(memory_space=pl.ANY)] * len(arrays),
        out_specs=(VMEM,) * len(arrays),
        scratch_shapes=[pltpu.SemaphoreType.DMA((len(arrays),))],
        compiler_params=PARAMS,
    )(*arrays)


def extend_kernel(block_ref, table_ref, out):
    rows = block_ref.shape[1]
    lanes = table_ref.shape[1]
    for part in range(2):
        out[part, :rows, :] = block_ref[part]
        out[part, rows:, :lanes] = table_ref[...].astype(BF16)
        out[part, rows:, lanes:] = jnp.zeros((TABLE_ROWS, out.shape[2] - lanes), BF16)


def sampled_kernel(kmax, row_tiles, slots, *refs):
    out = refs[-1]
    plane, side, core = here()
    lanes = out.shape[1]

    def table_of(ref):
        return ref[...] if len(ref.shape) == 2 else ref[0, ref.shape[1] - TABLE_ROWS :, :lanes].astype(F32)

    sublane = lax.broadcasted_iota(jnp.int32, (TABLE_ROWS, lanes), 0)
    lane = lax.broadcasted_iota(jnp.int32, (1, lanes), 1)
    out[...] = jnp.full(out.shape, NOWHERE, F32)
    for slot, mine_of in enumerate(slots):
        table = jnp.where(mine_of(plane, side), table_of(refs[2 * slot]), table_of(refs[2 * slot + 1]))
        for row_tile in range(row_tiles):
            wanted = core * row_tiles + row_tile
            row = jnp.sum(jnp.where(sublane == wanted, table, 0.0), axis=0, keepdims=True)
            count = jnp.sum(jnp.where(lane == kmax, row, 0.0), axis=1, keepdims=True)
            count = jnp.where((plane == 0) | (plane == 3), 0.0, count)
            at = slot * row_tiles + row_tile
            out[at : at + 1, :] = jnp.where(lane.astype(F32) < jnp.minimum(count, kmax), row, NOWHERE)


def sampled_call(shape, slots):
    tiles, kmax = shape
    args = [array for slot in slots for array in slot[1:]]
    return pl.pallas_call(
        functools.partial(sampled_kernel, kmax, tiles // 2, [slot[0] for slot in slots]),
        out_shape=jax.ShapeDtypeStruct((8, 128), F32),
        in_specs=[VMEM] * len(args),
        out_specs=VMEM,
        compiler_params=PARAMS,
    )(*args)


def window_kernel(blocks, slots, skip, shape, done, start, sampled, left, *refs):
    plane, side, core = here()
    tiles = shape[0]
    row_tiles = tiles // 2
    core_rows = left.shape[0] // (2 * (skip + slots)) if not skip else refs[1].shape[0] // 2
    rows = 2 * core_rows
    held = []
    for group_of, width in blocks:
        halves = []
        for _ in range(2):
            if width == 1:
                halves.append((refs[0][0, :rows, :], refs[0][1, :rows, :]))
            else:
                late = side == plane % 2
                whole, real, imag = refs[:3]
                halves.append(
                    (jnp.where(late, real[...], whole[0, :rows, :]), jnp.where(late, imag[...], whole[1, :rows, :]))
                )
            refs = refs[width:]
        held.append((group_of(plane, side), *halves))
    tile = core_rows // row_tiles
    sums, outs, couples = refs[: 0 if start else 2 * slots], refs[-2 * slots - 1 : -1], refs[-1]
    left_rows = left[skip * rows : (skip + slots) * rows, :]
    wide = tiles * tile
    for block, (group, own, other) in enumerate(held):
        couple = dot_t(left_rows, jnp.concatenate([*own, *other], axis=1))
        for index in range(slots * row_tiles):
            partners = sampled[skip * row_tiles + index : skip * row_tiles + index + 1, :]
            begin = index // row_tiles * rows + index % row_tiles * tile
            upper = slice(begin, begin + tile)
            lower = slice(begin + core_rows, begin + core_rows + tile)
            for c in range(tiles):
                wanted = (group * tiles + c).astype(F32)
                keep = jnp.max(jnp.where(partners == wanted, 1.0, 0.0), axis=1, keepdims=True)
                real = (couple[upper, c * tile : (c + 1) * tile] * keep).astype(BF16)
                imag = (couple[lower, c * tile : (c + 1) * tile] * keep).astype(BF16)
                at = 2 * block * wide + c * tile
                couples[upper, at : at + tile] = real
                couples[lower, at : at + tile] = imag
                couples[upper, at + wide : at + wide + tile] = -imag
                couples[lower, at + wide : at + wide + tile] = real
    for index in range(2):
        values = jnp.concatenate([part for block in held for part in block[1 + index]], axis=0)
        total = dot(couples[...], values)
        for slot in range(slots):
            part = total[slot * rows : (slot + 1) * rows]
            if not start:
                part = part + sums[2 * slot + index][...]
            outs[2 * slot + index][...] = part.astype(BF16) if slot in done else part


def window_call(sampled, shape, rows, left, skip, slots, blocks, sums, done):
    args = [sampled, left]
    for _, own, other in blocks:
        args.extend(own)
        args.extend(other)
    if sums is not None:
        args.extend(sums)
    half = left.shape[1] // 4
    outs = [jax.ShapeDtypeStruct((rows, half), BF16 if slot in done else F32) for slot in range(slots) for _ in range(2)]
    return pl.pallas_call(
        functools.partial(
            window_kernel, [(group_of, len(own)) for group_of, own, _ in blocks], slots, skip, shape, done, sums is None
        ),
        out_shape=tuple(outs),
        in_specs=[VMEM] * len(args),
        out_specs=(VMEM,) * len(outs),
        scratch_shapes=[pltpu.VMEM((slots * rows, 2 * len(blocks) * rows), BF16)],
        compiler_params=PARAMS,
        cost_estimate=pl.CostEstimate(
            flops=len(blocks) * slots * 2 * 2 * rows * 4 * half * rows,
            bytes_accessed=sum(a.size * a.dtype.itemsize for a in args),
            transcendentals=0,
        ),
    )(*args)


def pick_kernel(choices, *refs):
    place = here()
    outs = refs[len(refs) - len(choices) :]

    def put(out, value, part):
        out[...] = value[...] if part is None else value[part, : out.shape[0], :]

    for index, (flag_of, part) in enumerate(choices):
        flag = flag_of(*place)
        first, second, out = refs[2 * index], refs[2 * index + 1], outs[index]
        pl.when(flag)(functools.partial(put, out, first, part))
        pl.when(jnp.logical_not(flag))(functools.partial(put, out, second, part))


def pick(*choices, rows=None):
    args = [value for choice in choices for value in choice[1:3]]
    shapes = [
        a.shape if choice[3] is None else (rows, a.shape[2]) for a, choice in zip(args[::2], choices)
    ]
    return pl.pallas_call(
        functools.partial(pick_kernel, [(choice[0], choice[3]) for choice in choices]),
        out_shape=tuple(jax.ShapeDtypeStruct(shape, args[0].dtype) for shape in shapes),
        in_specs=[VMEM] * len(args),
        out_specs=(VMEM,) * len(choices),
        compiler_params=PARAMS,
    )(*args)


def columns_kernel(turns, block, core_rows, *refs):
    plane, side, core = here()
    slots = len(refs) // 3
    half = refs[0].shape[2]
    for index, turn in enumerate(turns):
        first = (2 * (plane ^ turn) + side) * block
        own = first // half == core
        cols = pl.ds(pl.multiple_of(lax.rem(first, half), block), block)
        for slot in range(slots):
            out = refs[2 * slots + slot]
            for position, reader in enumerate((core, 1 - core)):
                at = pl.ds(pl.multiple_of(reader * core_rows, core_rows), core_rows)
                for part in range(2):
                    value = jnp.where(own, refs[2 * slot][part, at, cols], refs[2 * slot + 1][part, at, cols])
                    start = (2 * position + part) * core_rows
                    out[index * block : (index + 1) * block, start : start + core_rows] = value.T


def columns_call(turns, block, core_rows, groups):
    args = [array for pair in groups for array in pair]
    out = jax.ShapeDtypeStruct((len(turns) * block, 4 * core_rows), BF16)
    return pl.pallas_call(
        functools.partial(columns_kernel, turns, block, core_rows),
        out_shape=(out,) * len(groups),
        in_specs=[VMEM] * len(args),
        out_specs=(VMEM,) * len(groups),
        compiler_params=PARAMS,
    )(*args)


def outer_kernel(first, block, pairs, base, *refs):
    half = refs[1].shape[1]
    straight, turned = [], []
    for index in range(pairs):
        for w in refs[3 * index + 1 : 3 * index + 3]:
            rows = w.shape[0] // 2
            straight.append(w[...])
            turned.extend([w[rows:, :], -w[:rows, :]])
    straight = jnp.concatenate(straight, axis=0)
    turned = jnp.concatenate(turned, axis=0)
    for index, out in enumerate(refs[3 * pairs + base :]):
        at = slice((first + index) * block, (first + index + 1) * block)
        a = jnp.concatenate([refs[3 * pair][at, :] for pair in range(pairs)], axis=1)
        real = dot(a, straight)
        imag = dot(a, turned)
        if base:
            begin = 2 * (first + index) * block
            real += refs[3 * pairs][begin : begin + block, :]
            imag += refs[3 * pairs][begin + block : begin + 2 * block, :]
        if out.shape[0] > 2 * block:
            top = jnp.maximum(jnp.max(jnp.abs(real)), jnp.max(jnp.abs(imag)))
            power = 14.0 - jnp.ceil(jnp.log2(jnp.full((PAD_ROWS, half), jnp.maximum(top, 1e-30), F32)))
            power = jnp.clip(power, -110.0, 110.0)
            scale = jnp.exp2(power)[:1]
            out[:block, :] = real * scale
            out[block : 2 * block, :] = imag * scale
            out[2 * block :, :] = power
        else:
            out[:block, :] = real
            out[block:, :] = imag


def base_kernel(block, pairs, *refs):
    out = refs[-1]
    straight, turned = [], []
    for index in range(pairs):
        for w in refs[3 * index + 1 : 3 * index + 3]:
            rows = w.shape[0] // 2
            straight.append(w[...])
            turned.extend([w[rows:, :], -w[:rows, :]])
    straight = jnp.concatenate(straight, axis=0)
    turned = jnp.concatenate(turned, axis=0)
    for index in range(out.shape[0] // (2 * block)):
        a = jnp.concatenate([ref[index * block : (index + 1) * block, :] for ref in refs[: 3 * pairs : 3]], axis=1)
        for part, w in enumerate((straight, turned)):
            at = slice((2 * index + part) * block, (2 * index + part + 1) * block)
            term = dot(a, w)
            out[at, :] = term if len(refs) == 3 * pairs + 1 else term + refs[-2][at, :]


def lay_kernel(total, out):
    block = out.shape[0]
    out[:, 0, :] = total[:block, :]
    out[:, 1, :] = total[block:, :]


def from_behind(value, axis, steps):
    count = lax.axis_size(axis)
    first, last = (max(0, -steps), min(count, count - steps))
    return lax.ppermute(value, axis, [(source, source + steps) for source in range(first, last)])


def any_shards(green, direction, partners, counts):
    tile_dev, kmax = partners.shape
    rows = green.shape[1]
    half = green.shape[2]
    tile = rows // tile_dev
    real_part = jnp.dot(green[0], direction[0], preferred_element_type=jnp.float32) - jnp.dot(
        green[1], direction[1], preferred_element_type=jnp.float32
    )
    imag_part = jnp.dot(green[0], direction[1], preferred_element_type=jnp.float32) + jnp.dot(
        green[1], direction[0], preferred_element_type=jnp.float32
    )
    images = lax.psum_scatter(
        jnp.stack([real_part, imag_part]), "src", scatter_dimension=2, tiled=True
    ).astype(jnp.bfloat16)
    tiles = green.reshape(2, tile_dev, tile, half)
    count_tile = lax.axis_size("tile")
    reach = min(BAND_DEV, count_tile - 1)
    empty = jnp.zeros_like(tiles)
    offsets = [offset for offset in range(-reach, reach + 1) if offset != 0]
    moved = [from_behind(tiles, "tile", -offset) for offset in offsets]
    nearby = dict(zip(offsets, moved))
    nearby[0] = tiles
    window = jnp.concatenate(
        [nearby.get(offset, empty) for offset in range(-BAND_DEV, BAND_DEV + 1)], axis=1
    )
    first_tile = (lax.axis_index("tile") - BAND_DEV) * tile_dev
    local_index = partners - first_tile
    live = (jnp.arange(kmax, dtype=jnp.int32)[None, :] < counts[:, None]).astype(jnp.float32)
    across = (((1,), (1,)), ((), ()))
    stacks = []
    pieces = []
    for row in range(tile_dev):
        stack = jnp.take(window, local_index[row], axis=1).reshape(2, kmax * tile, half)
        stacks.append(stack)
        image_row = images[:, row * tile : (row + 1) * tile]
        couple_real = lax.dot_general(
            image_row[0], stack[0], across, preferred_element_type=jnp.float32
        ) + lax.dot_general(image_row[1], stack[1], across, preferred_element_type=jnp.float32)
        couple_imag = lax.dot_general(
            image_row[1], stack[0], across, preferred_element_type=jnp.float32
        ) - lax.dot_general(image_row[0], stack[1], across, preferred_element_type=jnp.float32)
        blocks = jnp.stack([couple_real, couple_imag]).reshape(2, tile, kmax, tile)
        pieces.append(blocks * live[row][None, None, :, None])
    partial_blocks = jnp.stack(pieces, axis=1)
    coupling = lax.psum(partial_blocks, "src").astype(jnp.bfloat16)
    weight_rows = []
    for row in range(tile_dev):
        stack = stacks[row]
        flat = coupling[:, row].reshape(2, tile, kmax * tile)
        weight_real = jnp.dot(flat[0], stack[0], preferred_element_type=jnp.float32) - jnp.dot(
            flat[1], stack[1], preferred_element_type=jnp.float32
        )
        weight_imag = jnp.dot(flat[0], stack[1], preferred_element_type=jnp.float32) + jnp.dot(
            flat[1], stack[0], preferred_element_type=jnp.float32
        )
        weight_rows.append(jnp.stack([weight_real, weight_imag]))
    weighted = jnp.concatenate(weight_rows, axis=1).astype(jnp.bfloat16)
    full_rows = lax.all_gather(green, "src", axis=2, tiled=True)
    down = (((0,), (0,)), ((), ()))
    out_real = lax.dot_general(
        full_rows[0], weighted[0], down, preferred_element_type=jnp.float32
    ) + lax.dot_general(full_rows[1], weighted[1], down, preferred_element_type=jnp.float32)
    out_imag = lax.dot_general(
        full_rows[0], weighted[1], down, preferred_element_type=jnp.float32
    ) - lax.dot_general(full_rows[1], weighted[0], down, preferred_element_type=jnp.float32)
    return lax.psum_scatter(
        jnp.stack([out_real, out_imag], axis=1), "tile", scatter_dimension=0, tiled=True
    )


def four_shards(green, direction, partners, counts):
    shape = partners.shape
    rows, half = green.shape[1:]
    core_rows = rows // 2
    block = 2 * half // lax.axis_size("tile")
    turns = [2, 3, 1, 0]

    def other_side(index):
        return index ^ 1

    def even_pair(index):
        return index ^ 2

    def odd_pair(index):
        return index ^ 6 if inner(index) else -1

    def inner(index):
        return index // 2 in (1, 2)

    def early(index):
        return inner(index) and index // 2 % 2 != index % 2

    def second_mine(plane, side, core=None):
        return jnp.where(plane < 2, side, 1 - side) == 1

    def first_mine(plane, side, core=None):
        return jnp.where(plane < 2, side, 1 - side) == 0

    def always(plane, side, core=None):
        return plane >= 0

    def of_own(plane, side):
        return 2 * plane + side

    def of_mate(plane, side):
        return 2 * plane + 1 - side

    def of_pair(plane, side):
        return 2 * (plane ^ 1) + side

    def of_next(plane, side):
        return 2 * (3 - plane) + side

    def of_across(plane, side):
        return 2 * (plane ^ 1) + 1 - side

    def of_near(plane, side):
        return 2 * (3 - plane) + 1 - side

    def of_far(plane, side):
        return jnp.where(plane < 2, 6, 1)

    direction_other = cores(direction)
    green_other = cores(green)
    mate = move(green, other_side)
    pair = move(green, even_pair)
    beyond = move(green, odd_pair)
    late_partners, green_other = lax.optimization_barrier((partners, green_other))
    table = pl.pallas_call(
        table_kernel,
        out_shape=jax.ShapeDtypeStruct((TABLE_ROWS, 128), F32),
        in_specs=[SMEM, SMEM],
        out_specs=VMEM,
        compiler_params=PARAMS,
    )(late_partners, counts)
    table_mate = move(table, other_side)
    late_green, late_direction, table = lax.optimization_barrier((green, direction, table))
    green_here, direction_here = stage(late_green, late_direction)
    late_table, direction_other = lax.optimization_barrier((table, direction_other))
    table_pair = move(late_table, even_pair)
    mate, direction_other, green_other, table_mate, green, direction = lax.optimization_barrier(
        (mate, direction_other, green_other, table_mate, green_here, direction_here)
    )
    pair, beyond, table_pair = lax.optimization_barrier((pair, beyond, table_pair))

    mate_sent = pl.pallas_call(
        extend_kernel,
        out_shape=jax.ShapeDtypeStruct((2, rows + TABLE_ROWS, half), BF16),
        in_specs=[VMEM, VMEM],
        out_specs=VMEM,
        compiler_params=PARAMS,
    )(mate, table_mate)
    across = move(mate_sent, lambda i: -1 if inner(i) else even_pair(i))
    ahead = move(pair, lambda i: odd_pair(i) if inner(i) and not early(i) else -1)
    near = move(beyond, lambda i: other_side(i) if inner(i) else -1)
    mate_other = cores(mate)
    pair_other = cores(pair)
    beyond_other = cores(beyond)

    first_rows = pick(
        (first_mine, green, mate, None),
        (first_mine, green_other, mate_other, None),
        (second_mine, green, mate, None),
        (second_mine, green_other, mate_other, None),
    )
    row_groups = [first_rows[:2], first_rows[2:], (pair, pair_other)]
    left = images_call(core_rows, row_groups, direction, direction_other)
    columns = columns_call(turns, block, core_rows, row_groups)

    sampled = sampled_call(
        shape,
        [(first_mine, table, table_mate), (second_mine, table, table_mate), (always, table_pair, table_pair)],
    )
    first_blocks = [
        (of_own, [green], [green_other]),
        (of_mate, [mate], [mate_other]),
        (of_pair, [pair], [pair_other]),
        (of_next, [beyond], [beyond_other]),
    ]
    sums = window_call(sampled, shape, rows, left, 0, 3, first_blocks, None, ())
    across, ahead, sums, columns = lax.optimization_barrier((across, ahead, sums, columns))

    far_real, far_imag = pick((always, ahead, ahead, 0), (always, across, across, 1), rows=rows)
    far_real = move(far_real, lambda i: other_side(i) if early(i) else -1)
    far_imag = move(far_imag, lambda i: odd_pair(i) if early(i) else -1)
    across_other = cores(across)
    last_row = (across, across_other)
    across_block = (of_across, [across], [across_other])
    sums = window_call(
        sampled, shape, rows, left, 0, 3, [across_block, (of_near, [near], [cores(near)])], sums, (0, 2)
    )
    last_left = images_call(core_rows, [last_row], direction, direction_other)
    last_sampled = sampled_call(shape, [(always, across, across)])
    last_sums = window_call(
        last_sampled, shape, rows, last_left, 0, 1, [*first_blocks, across_block], None, (0,)
    )
    (last_columns,) = columns_call(turns, block, core_rows, [last_row])
    def share(*operands):
        pairs = len(operands) // 3
        return pl.pallas_call(
            functools.partial(base_kernel, block, pairs),
            out_shape=jax.ShapeDtypeStruct((2 * len(turns) * block, half), F32),
            in_specs=[VMEM] * len(operands),
            out_specs=VMEM,
            compiler_params=PARAMS,
        )(*operands)

    base = share(columns[0], sums[0], cores(sums[1]), columns[2], sums[4], cores(sums[5]))
    ahead_other = cores(ahead)
    far_real, far_imag, sums, last_sums = lax.optimization_barrier((far_real, far_imag, sums, last_sums))
    sums, base = lax.optimization_barrier((sums, base))
    weighted = window_call(
        sampled,
        shape,
        rows,
        left,
        1,
        1,
        [(of_far, [ahead, far_real, far_imag], [ahead_other, cores(far_real), cores(far_imag)])],
        sums[2:4],
        (0,),
    )
    last_base = share(last_columns, last_sums[0], cores(last_sums[1]), base)
    operands = [columns[1], weighted[0], cores(weighted[1]), last_base]

    def terms(first, turns):
        pads = [PAD_ROWS if turn else 0 for turn in turns]
        return pl.pallas_call(
            functools.partial(outer_kernel, first, block, 1, 1),
            out_shape=tuple(jax.ShapeDtypeStruct((2 * block + pad, half), F32) for pad in pads),
            in_specs=[VMEM] * len(operands),
            out_specs=(VMEM,) * len(turns),
            compiler_params=PARAMS,
        )(*operands)

    def send(term, turn):
        return move(term.astype(jnp.float16), lambda i: i ^ 2 * turn if inner(i) else -1)

    (first,) = terms(0, turns[:1])
    operands[0], first = lax.optimization_barrier((operands[0], first))
    sent = [send(first, turns[0])]
    sent += [send(term, turn) for term, turn in zip(terms(1, turns[1:-1]), turns[1:-1])]
    (total,) = terms(len(turns) - 1, turns[-1:])
    for got in sent:
        got = got.astype(F32)
        total = total + got[: 2 * block] * jnp.exp2(-got[2 * block : 2 * block + 1])
    return pl.pallas_call(
        lay_kernel,
        out_shape=jax.ShapeDtypeStruct((block, 2, half), F32),
        in_specs=[VMEM],
        out_specs=VMEM,
        compiler_params=PARAMS,
    )(total)


def solution(mesh):
    in_specs = (
        P(None, ("freq", "tile"), "src"),
        P(None, ("freq", "src"), None),
        P(("freq", "tile"), None),
        P(("freq", "tile")),
    )
    out_specs = P(("freq", "tile"), None, "src")
    shards = four_shards if mesh.shape["tile"] == 8 else any_shards
    return jax.shard_map(shards, mesh=mesh, in_specs=in_specs, out_specs=out_specs, check_vma=False)
```

```python
import functools

import jax
import jax.numpy as jnp
from jax import lax
from jax.experimental import pallas as pl
from jax.experimental.pallas import tpu as pltpu
from jax.sharding import PartitionSpec as P

F32 = jnp.float32
BF16 = jnp.bfloat16
NOWHERE = -4000
BAND_DEV = 3
PAD_ROWS = 8
TABLE_ROWS = 8
SMEM = pl.BlockSpec(memory_space=pltpu.SMEM)
VMEM = pl.BlockSpec(memory_space=pltpu.VMEM)
PARAMS = pltpu.CompilerParams(vmem_limit_bytes=24 * 1024 * 1024)


def move(value, target):
    count = lax.axis_size("tile")
    pairs = [(source, target(source)) for source in range(count) if 0 <= target(source) < count]
    return lax.ppermute(value, "tile", pairs)


def here():
    place = lax.axis_index("tile")
    return place // 2, place % 2, lax.axis_index("src")


def cores(value):
    return lax.ppermute(value, "src", [(0, 1), (1, 0)])


def dot(a, b):
    return jnp.dot(a, b, preferred_element_type=F32)


def dot_t(a, b):
    return lax.dot_general(a, b, (((1,), (1,)), ((), ())), preferred_element_type=F32)


def images_kernel(core_rows, slots, *refs):
    v_own, v_other, left = refs[2 * slots :]
    half = v_own.shape[1]
    core = lax.axis_index("src")
    at = pl.ds(pl.multiple_of(core * core_rows, core_rows), core_rows)
    sensors = []
    for own, other in zip(refs[: 2 * slots : 2], refs[1 : 2 * slots : 2]):
        own_real, own_imag, other_real, other_imag = own[0, at, :], own[1, at, :], other[0, at, :], other[1, at, :]
        sensors.append(jnp.concatenate([own_real, -own_imag, other_real, -other_imag], axis=1))
        sensors.append(jnp.concatenate([own_imag, own_real, other_imag, other_real], axis=1))
    sensors = jnp.concatenate(sensors, axis=0)
    for index, column in enumerate((core, 1 - core)):
        cols = pl.ds(pl.multiple_of(column * half, half), half)
        values = jnp.concatenate(
            [v_own[0, :, cols], v_own[1, :, cols], v_other[0, :, cols], v_other[1, :, cols]], axis=0
        )
        images = dot(sensors, values).astype(BF16)
        first = slice(2 * index * half, (2 * index + 1) * half)
        second = slice((2 * index + 1) * half, (2 * index + 2) * half)
        left[:, first] = images
        for slot in range(slots):
            real = slice(2 * slot * core_rows, (2 * slot + 1) * core_rows)
            imag = slice((2 * slot + 1) * core_rows, (2 * slot + 2) * core_rows)
            left[real, second] = images[imag]
            left[imag, second] = -images[real]


def images_call(core_rows, groups, direction, direction_other):
    half = direction.shape[1]
    args = [array for pair in groups for array in pair] + [direction, direction_other]
    return pl.pallas_call(
        functools.partial(images_kernel, core_rows, len(groups)),
        out_shape=jax.ShapeDtypeStruct((2 * len(groups) * core_rows, 4 * half), BF16),
        in_specs=[VMEM] * len(args),
        out_specs=VMEM,
        compiler_params=PARAMS,
        cost_estimate=pl.CostEstimate(
            flops=2 * len(groups) * 2 * core_rows * 8 * half * half, bytes_accessed=6 * 1024 * 1024, transcendentals=0
        ),
    )(*args)


def table_kernel(partners_ref, counts_ref, table_ref):
    row = lax.broadcasted_iota(jnp.int32, table_ref.shape, 0)
    col = lax.broadcasted_iota(jnp.int32, table_ref.shape, 1)
    tile_rows, kmax = partners_ref.shape
    table = jnp.zeros(table_ref.shape, F32)
    for r in range(tile_rows):
        for k in range(kmax + 1):
            value = partners_ref[r, k] if k < kmax else counts_ref[r]
            table = jnp.where((row == r) & (col == k), value.astype(F32), table)
    table_ref[...] = table


def stage_kernel(count, *refs):
    sources, targets, arrived = refs[:count], refs[count:-1], refs[-1]
    copies = [pltpu.make_async_copy(a, b, arrived.at[i]) for i, (a, b) in enumerate(zip(sources, targets))]
    for copy in copies:
        copy.start()
    for copy in copies:
        copy.wait()


def stage(*arrays):
    return pl.pallas_call(
        functools.partial(stage_kernel, len(arrays)),
        out_shape=tuple(jax.ShapeDtypeStruct(a.shape, a.dtype) for a in arrays),
        in_specs=[pl.BlockSpec(memory_space=pl.ANY)] * len(arrays),
        out_specs=(VMEM,) * len(arrays),
        scratch_shapes=[pltpu.SemaphoreType.DMA((len(arrays),))],
        compiler_params=PARAMS,
    )(*arrays)


def extend_kernel(block_ref, table_ref, out):
    rows = block_ref.shape[1]
    lanes = table_ref.shape[1]
    for part in range(2):
        out[part, :rows, :] = block_ref[part]
        out[part, rows:, :lanes] = table_ref[...].astype(BF16)
        out[part, rows:, lanes:] = jnp.zeros((TABLE_ROWS, out.shape[2] - lanes), BF16)


def sampled_kernel(kmax, row_tiles, slots, *refs):
    out = refs[-1]
    plane, side, core = here()
    lanes = out.shape[1]

    def table_of(ref):
        return ref[...] if len(ref.shape) == 2 else ref[0, ref.shape[1] - TABLE_ROWS :, :lanes].astype(F32)

    sublane = lax.broadcasted_iota(jnp.int32, (TABLE_ROWS, lanes), 0)
    lane = lax.broadcasted_iota(jnp.int32, (1, lanes), 1)
    out[...] = jnp.full(out.shape, NOWHERE, F32)
    for slot, mine_of in enumerate(slots):
        table = jnp.where(mine_of(plane, side), table_of(refs[2 * slot]), table_of(refs[2 * slot + 1]))
        for row_tile in range(row_tiles):
            wanted = core * row_tiles + row_tile
            row = jnp.sum(jnp.where(sublane == wanted, table, 0.0), axis=0, keepdims=True)
            count = jnp.sum(jnp.where(lane == kmax, row, 0.0), axis=1, keepdims=True)
            count = jnp.where((plane == 0) | (plane == 3), 0.0, count)
            at = slot * row_tiles + row_tile
            out[at : at + 1, :] = jnp.where(lane.astype(F32) < jnp.minimum(count, kmax), row, NOWHERE)


def sampled_call(shape, slots):
    tiles, kmax = shape
    args = [array for slot in slots for array in slot[1:]]
    return pl.pallas_call(
        functools.partial(sampled_kernel, kmax, tiles // 2, [slot[0] for slot in slots]),
        out_shape=jax.ShapeDtypeStruct((8, 128), F32),
        in_specs=[VMEM] * len(args),
        out_specs=VMEM,
        compiler_params=PARAMS,
    )(*args)


def window_kernel(blocks, slots, skip, shape, done, start, sampled, left, *refs):
    plane, side, core = here()
    tiles = shape[0]
    row_tiles = tiles // 2
    core_rows = left.shape[0] // (2 * (skip + slots)) if not skip else refs[1].shape[0] // 2
    rows = 2 * core_rows
    held = []
    for group_of, width in blocks:
        halves = []
        for _ in range(2):
            if width == 1:
                halves.append((refs[0][0, :rows, :], refs[0][1, :rows, :]))
            else:
                late = side == plane % 2
                whole, real, imag = refs[:3]
                halves.append(
                    (jnp.where(late, real[...], whole[0, :rows, :]), jnp.where(late, imag[...], whole[1, :rows, :]))
                )
            refs = refs[width:]
        held.append((group_of(plane, side), *halves))
    tile = core_rows // row_tiles
    sums, outs, couples = refs[: 0 if start else 2 * slots], refs[-2 * slots - 1 : -1], refs[-1]
    left_rows = left[skip * rows : (skip + slots) * rows, :]
    wide = tiles * tile
    for block, (group, own, other) in enumerate(held):
        couple = dot_t(left_rows, jnp.concatenate([*own, *other], axis=1))
        for index in range(slots * row_tiles):
            partners = sampled[skip * row_tiles + index : skip * row_tiles + index + 1, :]
            begin = index // row_tiles * rows + index % row_tiles * tile
            upper = slice(begin, begin + tile)
            lower = slice(begin + core_rows, begin + core_rows + tile)
            for c in range(tiles):
                wanted = (group * tiles + c).astype(F32)
                keep = jnp.max(jnp.where(partners == wanted, 1.0, 0.0), axis=1, keepdims=True)
                real = (couple[upper, c * tile : (c + 1) * tile] * keep).astype(BF16)
                imag = (couple[lower, c * tile : (c + 1) * tile] * keep).astype(BF16)
                at = 2 * block * wide + c * tile
                couples[upper, at : at + tile] = real
                couples[lower, at : at + tile] = imag
                couples[upper, at + wide : at + wide + tile] = -imag
                couples[lower, at + wide : at + wide + tile] = real
    for index in range(2):
        values = jnp.concatenate([part for block in held for part in block[1 + index]], axis=0)
        total = dot(couples[...], values)
        for slot in range(slots):
            part = total[slot * rows : (slot + 1) * rows]
            if not start:
                part = part + sums[2 * slot + index][...]
            outs[2 * slot + index][...] = part.astype(BF16) if slot in done else part


def window_call(sampled, shape, rows, left, skip, slots, blocks, sums, done):
    args = [sampled, left]
    for _, own, other in blocks:
        args.extend(own)
        args.extend(other)
    if sums is not None:
        args.extend(sums)
    half = left.shape[1] // 4
    outs = [jax.ShapeDtypeStruct((rows, half), BF16 if slot in done else F32) for slot in range(slots) for _ in range(2)]
    return pl.pallas_call(
        functools.partial(
            window_kernel, [(group_of, len(own)) for group_of, own, _ in blocks], slots, skip, shape, done, sums is None
        ),
        out_shape=tuple(outs),
        in_specs=[VMEM] * len(args),
        out_specs=(VMEM,) * len(outs),
        scratch_shapes=[pltpu.VMEM((slots * rows, 2 * len(blocks) * rows), BF16)],
        compiler_params=PARAMS,
        cost_estimate=pl.CostEstimate(
            flops=len(blocks) * slots * 2 * 2 * rows * 4 * half * rows,
            bytes_accessed=sum(a.size * a.dtype.itemsize for a in args),
            transcendentals=0,
        ),
    )(*args)


def pick_kernel(choices, *refs):
    place = here()
    outs = refs[len(refs) - len(choices) :]

    def put(out, value, part):
        out[...] = value[...] if part is None else value[part, : out.shape[0], :]

    for index, (flag_of, part) in enumerate(choices):
        flag = flag_of(*place)
        first, second, out = refs[2 * index], refs[2 * index + 1], outs[index]
        pl.when(flag)(functools.partial(put, out, first, part))
        pl.when(jnp.logical_not(flag))(functools.partial(put, out, second, part))


def pick(*choices, rows=None):
    args = [value for choice in choices for value in choice[1:3]]
    shapes = [
        a.shape if choice[3] is None else (rows, a.shape[2]) for a, choice in zip(args[::2], choices)
    ]
    return pl.pallas_call(
        functools.partial(pick_kernel, [(choice[0], choice[3]) for choice in choices]),
        out_shape=tuple(jax.ShapeDtypeStruct(shape, args[0].dtype) for shape in shapes),
        in_specs=[VMEM] * len(args),
        out_specs=(VMEM,) * len(choices),
        compiler_params=PARAMS,
    )(*args)


def columns_kernel(turns, block, core_rows, *refs):
    plane, side, core = here()
    slots = len(refs) // 3
    half = refs[0].shape[2]
    for index, turn in enumerate(turns):
        first = (2 * (plane ^ turn) + side) * block
        own = first // half == core
        cols = pl.ds(pl.multiple_of(lax.rem(first, half), block), block)
        for slot in range(slots):
            out = refs[2 * slots + slot]
            for position, reader in enumerate((core, 1 - core)):
                at = pl.ds(pl.multiple_of(reader * core_rows, core_rows), core_rows)
                for part in range(2):
                    value = jnp.where(own, refs[2 * slot][part, at, cols], refs[2 * slot + 1][part, at, cols])
                    start = (2 * position + part) * core_rows
                    out[index * block : (index + 1) * block, start : start + core_rows] = value.T


def columns_call(turns, block, core_rows, groups):
    args = [array for pair in groups for array in pair]
    out = jax.ShapeDtypeStruct((len(turns) * block, 4 * core_rows), BF16)
    return pl.pallas_call(
        functools.partial(columns_kernel, turns, block, core_rows),
        out_shape=(out,) * len(groups),
        in_specs=[VMEM] * len(args),
        out_specs=(VMEM,) * len(groups),
        compiler_params=PARAMS,
    )(*args)


def outer_kernel(first, block, pairs, base, *refs):
    half = refs[1].shape[1]
    straight, turned = [], []
    for index in range(pairs):
        for w in refs[3 * index + 1 : 3 * index + 3]:
            rows = w.shape[0] // 2
            straight.append(w[...])
            turned.extend([w[rows:, :], -w[:rows, :]])
    straight = jnp.concatenate(straight, axis=0)
    turned = jnp.concatenate(turned, axis=0)
    for index, out in enumerate(refs[3 * pairs + base :]):
        at = slice((first + index) * block, (first + index + 1) * block)
        a = jnp.concatenate([refs[3 * pair][at, :] for pair in range(pairs)], axis=1)
        real = dot(a, straight)
        imag = dot(a, turned)
        if base:
            begin = 2 * (first + index) * block
            real += refs[3 * pairs][begin : begin + block, :]
            imag += refs[3 * pairs][begin + block : begin + 2 * block, :]
        if out.shape[0] > 2 * block:
            top = jnp.maximum(jnp.max(jnp.abs(real)), jnp.max(jnp.abs(imag)))
            power = 14.0 - jnp.ceil(jnp.log2(jnp.full((PAD_ROWS, half), jnp.maximum(top, 1e-30), F32)))
            power = jnp.clip(power, -110.0, 110.0)
            scale = jnp.exp2(power)[:1]
            out[:block, :] = real * scale
            out[block : 2 * block, :] = imag * scale
            out[2 * block :, :] = power
        else:
            out[:block, :] = real
            out[block:, :] = imag


def base_kernel(block, pairs, *refs):
    out = refs[-1]
    straight, turned = [], []
    for index in range(pairs):
        for w in refs[3 * index + 1 : 3 * index + 3]:
            rows = w.shape[0] // 2
            straight.append(w[...])
            turned.extend([w[rows:, :], -w[:rows, :]])
    straight = jnp.concatenate(straight, axis=0)
    turned = jnp.concatenate(turned, axis=0)
    for index in range(out.shape[0] // (2 * block)):
        a = jnp.concatenate([ref[index * block : (index + 1) * block, :] for ref in refs[: 3 * pairs : 3]], axis=1)
        for part, w in enumerate((straight, turned)):
            at = slice((2 * index + part) * block, (2 * index + part + 1) * block)
            term = dot(a, w)
            out[at, :] = term if len(refs) == 3 * pairs + 1 else term + refs[-2][at, :]


def lay_kernel(total, out):
    block = out.shape[0]
    out[:, 0, :] = total[:block, :]
    out[:, 1, :] = total[block:, :]


def from_behind(value, axis, steps):
    count = lax.axis_size(axis)
    first, last = (max(0, -steps), min(count, count - steps))
    return lax.ppermute(value, axis, [(source, source + steps) for source in range(first, last)])


def any_shards(green, direction, partners, counts):
    tile_dev, kmax = partners.shape
    rows = green.shape[1]
    half = green.shape[2]
    tile = rows // tile_dev
    real_part = jnp.dot(green[0], direction[0], preferred_element_type=jnp.float32) - jnp.dot(
        green[1], direction[1], preferred_element_type=jnp.float32
    )
    imag_part = jnp.dot(green[0], direction[1], preferred_element_type=jnp.float32) + jnp.dot(
        green[1], direction[0], preferred_element_type=jnp.float32
    )
    images = lax.psum_scatter(
        jnp.stack([real_part, imag_part]), "src", scatter_dimension=2, tiled=True
    ).astype(jnp.bfloat16)
    tiles = green.reshape(2, tile_dev, tile, half)
    count_tile = lax.axis_size("tile")
    reach = min(BAND_DEV, count_tile - 1)
    empty = jnp.zeros_like(tiles)
    offsets = [offset for offset in range(-reach, reach + 1) if offset != 0]
    moved = [from_behind(tiles, "tile", -offset) for offset in offsets]
    nearby = dict(zip(offsets, moved))
    nearby[0] = tiles
    window = jnp.concatenate(
        [nearby.get(offset, empty) for offset in range(-BAND_DEV, BAND_DEV + 1)], axis=1
    )
    first_tile = (lax.axis_index("tile") - BAND_DEV) * tile_dev
    local_index = partners - first_tile
    live = (jnp.arange(kmax, dtype=jnp.int32)[None, :] < counts[:, None]).astype(jnp.float32)
    across = (((1,), (1,)), ((), ()))
    stacks = []
    pieces = []
    for row in range(tile_dev):
        stack = jnp.take(window, local_index[row], axis=1).reshape(2, kmax * tile, half)
        stacks.append(stack)
        image_row = images[:, row * tile : (row + 1) * tile]
        couple_real = lax.dot_general(
            image_row[0], stack[0], across, preferred_element_type=jnp.float32
        ) + lax.dot_general(image_row[1], stack[1], across, preferred_element_type=jnp.float32)
        couple_imag = lax.dot_general(
            image_row[1], stack[0], across, preferred_element_type=jnp.float32
        ) - lax.dot_general(image_row[0], stack[1], across, preferred_element_type=jnp.float32)
        blocks = jnp.stack([couple_real, couple_imag]).reshape(2, tile, kmax, tile)
        pieces.append(blocks * live[row][None, None, :, None])
    partial_blocks = jnp.stack(pieces, axis=1)
    coupling = lax.psum(partial_blocks, "src").astype(jnp.bfloat16)
    weight_rows = []
    for row in range(tile_dev):
        stack = stacks[row]
        flat = coupling[:, row].reshape(2, tile, kmax * tile)
        weight_real = jnp.dot(flat[0], stack[0], preferred_element_type=jnp.float32) - jnp.dot(
            flat[1], stack[1], preferred_element_type=jnp.float32
        )
        weight_imag = jnp.dot(flat[0], stack[1], preferred_element_type=jnp.float32) + jnp.dot(
            flat[1], stack[0], preferred_element_type=jnp.float32
        )
        weight_rows.append(jnp.stack([weight_real, weight_imag]))
    weighted = jnp.concatenate(weight_rows, axis=1).astype(jnp.bfloat16)
    full_rows = lax.all_gather(green, "src", axis=2, tiled=True)
    down = (((0,), (0,)), ((), ()))
    out_real = lax.dot_general(
        full_rows[0], weighted[0], down, preferred_element_type=jnp.float32
    ) + lax.dot_general(full_rows[1], weighted[1], down, preferred_element_type=jnp.float32)
    out_imag = lax.dot_general(
        full_rows[0], weighted[1], down, preferred_element_type=jnp.float32
    ) - lax.dot_general(full_rows[1], weighted[0], down, preferred_element_type=jnp.float32)
    return lax.psum_scatter(
        jnp.stack([out_real, out_imag], axis=1), "tile", scatter_dimension=0, tiled=True
    )


def four_shards(green, direction, partners, counts):
    shape = partners.shape
    rows, half = green.shape[1:]
    core_rows = rows // 2
    block = 2 * half // lax.axis_size("tile")
    turns = [2, 3, 1, 0]

    def other_side(index):
        return index ^ 1

    def even_pair(index):
        return index ^ 2

    def odd_pair(index):
        return index ^ 6 if inner(index) else -1

    def inner(index):
        return index // 2 in (1, 2)

    def early(index):
        return inner(index) and index // 2 % 2 != index % 2

    def second_mine(plane, side, core=None):
        return jnp.where(plane < 2, side, 1 - side) == 1

    def first_mine(plane, side, core=None):
        return jnp.where(plane < 2, side, 1 - side) == 0

    def always(plane, side, core=None):
        return plane >= 0

    def of_own(plane, side):
        return 2 * plane + side

    def of_mate(plane, side):
        return 2 * plane + 1 - side

    def of_pair(plane, side):
        return 2 * (plane ^ 1) + side

    def of_next(plane, side):
        return 2 * (3 - plane) + side

    def of_across(plane, side):
        return 2 * (plane ^ 1) + 1 - side

    def of_near(plane, side):
        return 2 * (3 - plane) + 1 - side

    def of_far(plane, side):
        return jnp.where(plane < 2, 6, 1)

    direction_other = cores(direction)
    green_other = cores(green)
    mate = move(green, other_side)
    pair = move(green, even_pair)
    beyond = move(green, odd_pair)
    late_partners, green_other = lax.optimization_barrier((partners, green_other))
    table = pl.pallas_call(
        table_kernel,
        out_shape=jax.ShapeDtypeStruct((TABLE_ROWS, 128), F32),
        in_specs=[SMEM, SMEM],
        out_specs=VMEM,
        compiler_params=PARAMS,
    )(late_partners, counts)
    table_mate = move(table, other_side)
    late_green, late_direction, table = lax.optimization_barrier((green, direction, table))
    green_here, direction_here = stage(late_green, late_direction)
    late_table, direction_other = lax.optimization_barrier((table, direction_other))
    table_pair = move(late_table, even_pair)
    mate, direction_other, green_other, table_mate, green, direction = lax.optimization_barrier(
        (mate, direction_other, green_other, table_mate, green_here, direction_here)
    )
    pair, beyond, table_pair = lax.optimization_barrier((pair, beyond, table_pair))

    mate_sent = pl.pallas_call(
        extend_kernel,
        out_shape=jax.ShapeDtypeStruct((2, rows + TABLE_ROWS, half), BF16),
        in_specs=[VMEM, VMEM],
        out_specs=VMEM,
        compiler_params=PARAMS,
    )(mate, table_mate)
    across = move(mate_sent, even_pair)
    ahead = move(pair, lambda i: odd_pair(i) if inner(i) and not early(i) else -1)
    near = move(beyond, other_side)
    mate_other = cores(mate)
    pair_other = cores(pair)
    beyond_other = cores(beyond)

    first_rows = pick(
        (first_mine, green, mate, None),
        (first_mine, green_other, mate_other, None),
        (second_mine, green, mate, None),
        (second_mine, green_other, mate_other, None),
    )
    row_groups = [first_rows[:2], first_rows[2:], (pair, pair_other)]
    left = images_call(core_rows, row_groups, direction, direction_other)
    columns = columns_call(turns, block, core_rows, row_groups)

    sampled = sampled_call(
        shape,
        [(first_mine, table, table_mate), (second_mine, table, table_mate), (always, table_pair, table_pair)],
    )
    first_blocks = [
        (of_own, [green], [green_other]),
        (of_mate, [mate], [mate_other]),
        (of_pair, [pair], [pair_other]),
        (of_next, [beyond], [beyond_other]),
    ]
    sums = window_call(sampled, shape, rows, left, 0, 3, first_blocks, None, ())
    across, ahead, sums, columns = lax.optimization_barrier((across, ahead, sums, columns))

    far_real, far_imag = pick((always, ahead, ahead, 0), (always, across, across, 1), rows=rows)
    far_real = move(far_real, lambda i: other_side(i) if early(i) else -1)
    far_imag = move(far_imag, lambda i: odd_pair(i) if early(i) else -1)
    across_other = cores(across)
    last_row = (across, across_other)
    across_block = (of_across, [across], [across_other])
    sums = window_call(
        sampled, shape, rows, left, 0, 3, [across_block, (of_near, [near], [cores(near)])], sums, (0, 2)
    )
    last_left = images_call(core_rows, [last_row], direction, direction_other)
    last_sampled = sampled_call(shape, [(always, across, across)])
    last_sums = window_call(
        last_sampled, shape, rows, last_left, 0, 1, [*first_blocks, across_block], None, (0,)
    )
    (last_columns,) = columns_call(turns, block, core_rows, [last_row])
    def share(*operands):
        pairs = len(operands) // 3
        return pl.pallas_call(
            functools.partial(base_kernel, block, pairs),
            out_shape=jax.ShapeDtypeStruct((2 * len(turns) * block, half), F32),
            in_specs=[VMEM] * len(operands),
            out_specs=VMEM,
            compiler_params=PARAMS,
        )(*operands)

    base = share(columns[0], sums[0], cores(sums[1]), columns[2], sums[4], cores(sums[5]))
    ahead_other = cores(ahead)
    far_real, far_imag, sums, last_sums = lax.optimization_barrier((far_real, far_imag, sums, last_sums))
    sums, base = lax.optimization_barrier((sums, base))
    weighted = window_call(
        sampled,
        shape,
        rows,
        left,
        1,
        1,
        [(of_far, [ahead, far_real, far_imag], [ahead_other, cores(far_real), cores(far_imag)])],
        sums[2:4],
        (0,),
    )
    last_base = share(last_columns, last_sums[0], cores(last_sums[1]), base)
    operands = [columns[1], weighted[0], cores(weighted[1]), last_base]

    def terms(first, turns):
        pads = [PAD_ROWS if turn else 0 for turn in turns]
        return pl.pallas_call(
            functools.partial(outer_kernel, first, block, 1, 1),
            out_shape=tuple(jax.ShapeDtypeStruct((2 * block + pad, half), F32) for pad in pads),
            in_specs=[VMEM] * len(operands),
            out_specs=(VMEM,) * len(turns),
            compiler_params=PARAMS,
        )(*operands)

    def send(term, turn):
        return move(term.astype(jnp.float16), lambda i: i ^ 2 * turn if inner(i) else -1)

    (first,) = terms(0, turns[:1])
    operands[0], first = lax.optimization_barrier((operands[0], first))
    sent = [send(first, turns[0])]
    sent += [send(term, turn) for term, turn in zip(terms(1, turns[1:-1]), turns[1:-1])]
    (total,) = terms(len(turns) - 1, turns[-1:])
    for got in sent:
        got = got.astype(F32)
        total = total + got[: 2 * block] * jnp.exp2(-got[2 * block : 2 * block + 1])
    return pl.pallas_call(
        lay_kernel,
        out_shape=jax.ShapeDtypeStruct((block, 2, half), F32),
        in_specs=[VMEM],
        out_specs=VMEM,
        compiler_params=PARAMS,
    )(total)


def solution(mesh):
    in_specs = (
        P(None, ("freq", "tile"), "src"),
        P(None, ("freq", "src"), None),
        P(("freq", "tile"), None),
        P(("freq", "tile")),
    )
    out_specs = P(("freq", "tile"), None, "src")
    shards = four_shards if mesh.shape["tile"] == 8 else any_shards
    return jax.shard_map(shards, mesh=mesh, in_specs=in_specs, out_specs=out_specs, check_vma=False)
```

```python
import functools

import jax
import jax.numpy as jnp
from jax import lax
from jax.experimental import pallas as pl
from jax.experimental.pallas import tpu as pltpu
from jax.sharding import PartitionSpec as P

F32 = jnp.float32
BF16 = jnp.bfloat16
NOWHERE = -4000
BAND_DEV = 3
PAD_ROWS = 8
TABLE_ROWS = 8
SMEM = pl.BlockSpec(memory_space=pltpu.SMEM)
VMEM = pl.BlockSpec(memory_space=pltpu.VMEM)
PARAMS = pltpu.CompilerParams(vmem_limit_bytes=24 * 1024 * 1024)


def move(value, target):
    count = lax.axis_size("tile")
    pairs = [(source, target(source)) for source in range(count) if 0 <= target(source) < count]
    return lax.ppermute(value, "tile", pairs)


def here():
    place = lax.axis_index("tile")
    return place // 2, place % 2, lax.axis_index("src")


def cores(value):
    return lax.ppermute(value, "src", [(0, 1), (1, 0)])


def dot(a, b):
    return jnp.dot(a, b, preferred_element_type=F32)


def dot_t(a, b):
    return lax.dot_general(a, b, (((1,), (1,)), ((), ())), preferred_element_type=F32)


def images_kernel(core_rows, slots, *refs):
    v_own, v_other, left = refs[2 * slots :]
    half = v_own.shape[1]
    core = lax.axis_index("src")
    at = pl.ds(pl.multiple_of(core * core_rows, core_rows), core_rows)
    sensors = []
    for own, other in zip(refs[: 2 * slots : 2], refs[1 : 2 * slots : 2]):
        own_real, own_imag, other_real, other_imag = own[0, at, :], own[1, at, :], other[0, at, :], other[1, at, :]
        sensors.append(jnp.concatenate([own_real, -own_imag, other_real, -other_imag], axis=1))
        sensors.append(jnp.concatenate([own_imag, own_real, other_imag, other_real], axis=1))
    sensors = jnp.concatenate(sensors, axis=0)
    for index, column in enumerate((core, 1 - core)):
        cols = pl.ds(pl.multiple_of(column * half, half), half)
        values = jnp.concatenate(
            [v_own[0, :, cols], v_own[1, :, cols], v_other[0, :, cols], v_other[1, :, cols]], axis=0
        )
        images = dot(sensors, values).astype(BF16)
        first = slice(2 * index * half, (2 * index + 1) * half)
        second = slice((2 * index + 1) * half, (2 * index + 2) * half)
        left[:, first] = images
        for slot in range(slots):
            real = slice(2 * slot * core_rows, (2 * slot + 1) * core_rows)
            imag = slice((2 * slot + 1) * core_rows, (2 * slot + 2) * core_rows)
            left[real, second] = images[imag]
            left[imag, second] = -images[real]


def images_call(core_rows, groups, direction, direction_other):
    half = direction.shape[1]
    args = [array for pair in groups for array in pair] + [direction, direction_other]
    return pl.pallas_call(
        functools.partial(images_kernel, core_rows, len(groups)),
        out_shape=jax.ShapeDtypeStruct((2 * len(groups) * core_rows, 4 * half), BF16),
        in_specs=[VMEM] * len(args),
        out_specs=VMEM,
        compiler_params=PARAMS,
        cost_estimate=pl.CostEstimate(
            flops=2 * len(groups) * 2 * core_rows * 8 * half * half, bytes_accessed=6 * 1024 * 1024, transcendentals=0
        ),
    )(*args)


def table_kernel(partners_ref, counts_ref, table_ref):
    row = lax.broadcasted_iota(jnp.int32, table_ref.shape, 0)
    col = lax.broadcasted_iota(jnp.int32, table_ref.shape, 1)
    tile_rows, kmax = partners_ref.shape
    table = jnp.zeros(table_ref.shape, F32)
    for r in range(tile_rows):
        for k in range(kmax + 1):
            value = partners_ref[r, k] if k < kmax else counts_ref[r]
            table = jnp.where((row == r) & (col == k), value.astype(F32), table)
    table_ref[...] = table


def stage_kernel(count, *refs):
    sources, targets, arrived = refs[:count], refs[count:-1], refs[-1]
    copies = [pltpu.make_async_copy(a, b, arrived.at[i]) for i, (a, b) in enumerate(zip(sources, targets))]
    for copy in copies:
        copy.start()
    for copy in copies:
        copy.wait()


def stage(*arrays):
    return pl.pallas_call(
        functools.partial(stage_kernel, len(arrays)),
        out_shape=tuple(jax.ShapeDtypeStruct(a.shape, a.dtype) for a in arrays),
        in_specs=[pl.BlockSpec(memory_space=pl.ANY)] * len(arrays),
        out_specs=(VMEM,) * len(arrays),
        scratch_shapes=[pltpu.SemaphoreType.DMA((len(arrays),))],
        compiler_params=PARAMS,
    )(*arrays)


def extend_kernel(block_ref, table_ref, out):
    rows = block_ref.shape[1]
    lanes = table_ref.shape[1]
    for part in range(2):
        out[part, :rows, :] = block_ref[part]
        out[part, rows:, :lanes] = table_ref[...].astype(BF16)
        out[part, rows:, lanes:] = jnp.zeros((TABLE_ROWS, out.shape[2] - lanes), BF16)


def sampled_kernel(kmax, row_tiles, slots, *refs):
    out = refs[-1]
    plane, side, core = here()
    lanes = out.shape[1]

    def table_of(ref):
        return ref[...] if len(ref.shape) == 2 else ref[0, ref.shape[1] - TABLE_ROWS :, :lanes].astype(F32)

    sublane = lax.broadcasted_iota(jnp.int32, (TABLE_ROWS, lanes), 0)
    lane = lax.broadcasted_iota(jnp.int32, (1, lanes), 1)
    out[...] = jnp.full(out.shape, NOWHERE, F32)
    for slot, mine_of in enumerate(slots):
        table = jnp.where(mine_of(plane, side), table_of(refs[2 * slot]), table_of(refs[2 * slot + 1]))
        for row_tile in range(row_tiles):
            wanted = core * row_tiles + row_tile
            row = jnp.sum(jnp.where(sublane == wanted, table, 0.0), axis=0, keepdims=True)
            count = jnp.sum(jnp.where(lane == kmax, row, 0.0), axis=1, keepdims=True)
            count = jnp.where((plane == 0) | (plane == 3), 0.0, count)
            at = slot * row_tiles + row_tile
            out[at : at + 1, :] = jnp.where(lane.astype(F32) < jnp.minimum(count, kmax), row, NOWHERE)


def sampled_call(shape, slots):
    tiles, kmax = shape
    args = [array for slot in slots for array in slot[1:]]
    return pl.pallas_call(
        functools.partial(sampled_kernel, kmax, tiles // 2, [slot[0] for slot in slots]),
        out_shape=jax.ShapeDtypeStruct((8, 128), F32),
        in_specs=[VMEM] * len(args),
        out_specs=VMEM,
        compiler_params=PARAMS,
    )(*args)


def window_kernel(blocks, slots, skip, shape, done, start, source_halves, apart, sampled, left, *refs):
    plane, side, core = here()
    tiles = shape[0]
    row_tiles = tiles // 2
    core_rows = left.shape[0] // (2 * (skip + slots)) if not skip else refs[1].shape[0] // 2
    rows = 2 * core_rows
    held = []
    for group_of, width in blocks:
        halves = []
        for _ in range(2):
            if width == 1:
                halves.append((refs[0][0, :rows, :], refs[0][1, :rows, :]))
            else:
                late = side == plane % 2
                whole, real, imag = refs[:3]
                halves.append(
                    (jnp.where(late, real[...], whole[0, :rows, :]), jnp.where(late, imag[...], whole[1, :rows, :]))
                )
            refs = refs[width:]
        held.append((group_of(plane, side), *halves))
    tile = core_rows // row_tiles
    count = len(source_halves) * slots
    sums, outs, couples = refs[: 0 if start else count], refs[-count - 1 : -1], refs[-1]
    left_rows = left[skip * rows : (skip + slots) * rows, :]
    wide = tiles * tile
    for block, (group, own, other) in enumerate(held):
        readers = slots - 1 if apart and block == len(held) - 1 else slots
        couple = dot_t(left_rows[: readers * rows], jnp.concatenate([*own, *other], axis=1))
        for index in range(readers * row_tiles):
            partners = sampled[skip * row_tiles + index : skip * row_tiles + index + 1, :]
            begin = index // row_tiles * rows + index % row_tiles * tile
            upper = slice(begin, begin + tile)
            lower = slice(begin + core_rows, begin + core_rows + tile)
            for c in range(tiles):
                wanted = (group * tiles + c).astype(F32)
                keep = jnp.max(jnp.where(partners == wanted, 1.0, 0.0), axis=1, keepdims=True)
                real = (couple[upper, c * tile : (c + 1) * tile] * keep).astype(BF16)
                imag = (couple[lower, c * tile : (c + 1) * tile] * keep).astype(BF16)
                at = 2 * block * wide + c * tile
                couples[upper, at : at + tile] = real
                couples[lower, at : at + tile] = imag
                couples[upper, at + wide : at + wide + tile] = -imag
                couples[lower, at + wide : at + wide + tile] = real
    for position, index in enumerate(source_halves):
        values = jnp.concatenate([part for block in held for part in block[1 + index]], axis=0)
        if apart:
            cut, depth = (slots - 1) * rows, couples.shape[1] - 2 * rows
            total = jnp.concatenate(
                [dot(couples[:cut, :], values), dot(couples[cut:, :depth], values[:depth])], axis=0
            )
        else:
            total = dot(couples[...], values)
        for slot in range(slots):
            part = total[slot * rows : (slot + 1) * rows]
            if not start:
                part = part + sums[len(source_halves) * slot + position][...]
            outs[len(source_halves) * slot + position][...] = part.astype(BF16) if slot in done else part


def window_call(sampled, shape, rows, left, skip, slots, blocks, sums, done, halves=(0, 1), apart=False):
    args = [sampled, left]
    for _, own, other in blocks:
        args.extend(own)
        args.extend(other)
    if sums is not None:
        args.extend(sums)
    half = left.shape[1] // 4
    outs = [jax.ShapeDtypeStruct((rows, half), BF16 if slot in done else F32) for slot in range(slots) for _ in halves]
    couples = (slots * rows, 2 * len(blocks) * rows)
    if len(halves) == 1:
        outs.append(jax.ShapeDtypeStruct(couples, BF16))
    return pl.pallas_call(
        functools.partial(
            window_kernel,
            [(group_of, len(own)) for group_of, own, _ in blocks],
            slots,
            skip,
            shape,
            done,
            sums is None,
            halves,
            apart,
        ),
        out_shape=tuple(outs),
        in_specs=[VMEM] * len(args),
        out_specs=(VMEM,) * len(outs),
        scratch_shapes=[pltpu.VMEM(couples, BF16)] if len(halves) == 2 else [],
        compiler_params=PARAMS,
        cost_estimate=pl.CostEstimate(
            flops=len(blocks) * slots * 2 * 2 * rows * 4 * half * rows,
            bytes_accessed=sum(a.size * a.dtype.itemsize for a in args),
            transcendentals=0,
        ),
    )(*args)


def finish_kernel(couples, whole, real, imag, held, out):
    plane, side, core = here()
    late = side == plane % 2
    rows = out.shape[0]
    values = [jnp.where(late, part[...], whole[index, :rows, :]) for index, part in enumerate((real, imag))]
    out[...] = (held[...] + dot(couples[...], jnp.concatenate(values, axis=0))).astype(BF16)


def pick_kernel(choices, *refs):
    place = here()
    outs = refs[len(refs) - len(choices) :]

    def put(out, value, part):
        out[...] = value[...] if part is None else value[part, : out.shape[0], :]

    for index, (flag_of, part) in enumerate(choices):
        flag = flag_of(*place)
        first, second, out = refs[2 * index], refs[2 * index + 1], outs[index]
        pl.when(flag)(functools.partial(put, out, first, part))
        pl.when(jnp.logical_not(flag))(functools.partial(put, out, second, part))


def pick(*choices, rows=None):
    args = [value for choice in choices for value in choice[1:3]]
    shapes = [
        a.shape if choice[3] is None else (rows, a.shape[2]) for a, choice in zip(args[::2], choices)
    ]
    return pl.pallas_call(
        functools.partial(pick_kernel, [(choice[0], choice[3]) for choice in choices]),
        out_shape=tuple(jax.ShapeDtypeStruct(shape, args[0].dtype) for shape in shapes),
        in_specs=[VMEM] * len(args),
        out_specs=(VMEM,) * len(choices),
        compiler_params=PARAMS,
    )(*args)


def columns_kernel(turns, block, core_rows, *refs):
    plane, side, core = here()
    slots = len(refs) // 3
    half = refs[0].shape[2]
    for index, turn in enumerate(turns):
        first = (2 * (plane ^ turn) + side) * block
        own = first // half == core
        cols = pl.ds(pl.multiple_of(lax.rem(first, half), block), block)
        for slot in range(slots):
            out = refs[2 * slots + slot]
            for position, reader in enumerate((core, 1 - core)):
                at = pl.ds(pl.multiple_of(reader * core_rows, core_rows), core_rows)
                for part in range(2):
                    value = jnp.where(own, refs[2 * slot][part, at, cols], refs[2 * slot + 1][part, at, cols])
                    start = (2 * position + part) * core_rows
                    out[index * block : (index + 1) * block, start : start + core_rows] = value.T


def columns_call(turns, block, core_rows, groups):
    args = [array for pair in groups for array in pair]
    out = jax.ShapeDtypeStruct((len(turns) * block, 4 * core_rows), BF16)
    return pl.pallas_call(
        functools.partial(columns_kernel, turns, block, core_rows),
        out_shape=(out,) * len(groups),
        in_specs=[VMEM] * len(args),
        out_specs=(VMEM,) * len(groups),
        compiler_params=PARAMS,
    )(*args)


def outer_kernel(first, block, pairs, base, *refs):
    half = refs[1].shape[1]
    straight, turned = [], []
    for index in range(pairs):
        for w in refs[3 * index + 1 : 3 * index + 3]:
            rows = w.shape[0] // 2
            straight.append(w[...])
            turned.extend([w[rows:, :], -w[:rows, :]])
    straight = jnp.concatenate(straight, axis=0)
    turned = jnp.concatenate(turned, axis=0)
    for index, out in enumerate(refs[3 * pairs + base :]):
        at = slice((first + index) * block, (first + index + 1) * block)
        a = jnp.concatenate([refs[3 * pair][at, :] for pair in range(pairs)], axis=1)
        real = dot(a, straight)
        imag = dot(a, turned)
        if base:
            begin = 2 * (first + index) * block
            real += refs[3 * pairs][begin : begin + block, :]
            imag += refs[3 * pairs][begin + block : begin + 2 * block, :]
        if out.shape[0] > 2 * block:
            top = jnp.maximum(jnp.max(jnp.abs(real)), jnp.max(jnp.abs(imag)))
            power = 14.0 - jnp.ceil(jnp.log2(jnp.full((PAD_ROWS, half), jnp.maximum(top, 1e-30), F32)))
            power = jnp.clip(power, -110.0, 110.0)
            scale = jnp.exp2(power)[:1]
            out[:block, :] = real * scale
            out[block : 2 * block, :] = imag * scale
            out[2 * block :, :] = power
        else:
            out[:block, :] = real
            out[block:, :] = imag


def base_kernel(block, pairs, *refs):
    out = refs[-1]
    straight, turned = [], []
    for index in range(pairs):
        for w in refs[3 * index + 1 : 3 * index + 3]:
            rows = w.shape[0] // 2
            straight.append(w[...])
            turned.extend([w[rows:, :], -w[:rows, :]])
    straight = jnp.concatenate(straight, axis=0)
    turned = jnp.concatenate(turned, axis=0)
    for index in range(out.shape[0] // (2 * block)):
        a = jnp.concatenate([ref[index * block : (index + 1) * block, :] for ref in refs[: 3 * pairs : 3]], axis=1)
        for part, w in enumerate((straight, turned)):
            at = slice((2 * index + part) * block, (2 * index + part + 1) * block)
            term = dot(a, w)
            out[at, :] = term if len(refs) == 3 * pairs + 1 else term + refs[-2][at, :]


def lay_kernel(total, out):
    block = out.shape[0]
    out[:, 0, :] = total[:block, :]
    out[:, 1, :] = total[block:, :]


def from_behind(value, axis, steps):
    count = lax.axis_size(axis)
    first, last = (max(0, -steps), min(count, count - steps))
    return lax.ppermute(value, axis, [(source, source + steps) for source in range(first, last)])


def any_shards(green, direction, partners, counts):
    tile_dev, kmax = partners.shape
    rows = green.shape[1]
    half = green.shape[2]
    tile = rows // tile_dev
    real_part = jnp.dot(green[0], direction[0], preferred_element_type=jnp.float32) - jnp.dot(
        green[1], direction[1], preferred_element_type=jnp.float32
    )
    imag_part = jnp.dot(green[0], direction[1], preferred_element_type=jnp.float32) + jnp.dot(
        green[1], direction[0], preferred_element_type=jnp.float32
    )
    images = lax.psum_scatter(
        jnp.stack([real_part, imag_part]), "src", scatter_dimension=2, tiled=True
    ).astype(jnp.bfloat16)
    tiles = green.reshape(2, tile_dev, tile, half)
    count_tile = lax.axis_size("tile")
    reach = min(BAND_DEV, count_tile - 1)
    empty = jnp.zeros_like(tiles)
    offsets = [offset for offset in range(-reach, reach + 1) if offset != 0]
    moved = [from_behind(tiles, "tile", -offset) for offset in offsets]
    nearby = dict(zip(offsets, moved))
    nearby[0] = tiles
    window = jnp.concatenate(
        [nearby.get(offset, empty) for offset in range(-BAND_DEV, BAND_DEV + 1)], axis=1
    )
    first_tile = (lax.axis_index("tile") - BAND_DEV) * tile_dev
    local_index = partners - first_tile
    live = (jnp.arange(kmax, dtype=jnp.int32)[None, :] < counts[:, None]).astype(jnp.float32)
    across = (((1,), (1,)), ((), ()))
    stacks = []
    pieces = []
    for row in range(tile_dev):
        stack = jnp.take(window, local_index[row], axis=1).reshape(2, kmax * tile, half)
        stacks.append(stack)
        image_row = images[:, row * tile : (row + 1) * tile]
        couple_real = lax.dot_general(
            image_row[0], stack[0], across, preferred_element_type=jnp.float32
        ) + lax.dot_general(image_row[1], stack[1], across, preferred_element_type=jnp.float32)
        couple_imag = lax.dot_general(
            image_row[1], stack[0], across, preferred_element_type=jnp.float32
        ) - lax.dot_general(image_row[0], stack[1], across, preferred_element_type=jnp.float32)
        blocks = jnp.stack([couple_real, couple_imag]).reshape(2, tile, kmax, tile)
        pieces.append(blocks * live[row][None, None, :, None])
    partial_blocks = jnp.stack(pieces, axis=1)
    coupling = lax.psum(partial_blocks, "src").astype(jnp.bfloat16)
    weight_rows = []
    for row in range(tile_dev):
        stack = stacks[row]
        flat = coupling[:, row].reshape(2, tile, kmax * tile)
        weight_real = jnp.dot(flat[0], stack[0], preferred_element_type=jnp.float32) - jnp.dot(
            flat[1], stack[1], preferred_element_type=jnp.float32
        )
        weight_imag = jnp.dot(flat[0], stack[1], preferred_element_type=jnp.float32) + jnp.dot(
            flat[1], stack[0], preferred_element_type=jnp.float32
        )
        weight_rows.append(jnp.stack([weight_real, weight_imag]))
    weighted = jnp.concatenate(weight_rows, axis=1).astype(jnp.bfloat16)
    full_rows = lax.all_gather(green, "src", axis=2, tiled=True)
    down = (((0,), (0,)), ((), ()))
    out_real = lax.dot_general(
        full_rows[0], weighted[0], down, preferred_element_type=jnp.float32
    ) + lax.dot_general(full_rows[1], weighted[1], down, preferred_element_type=jnp.float32)
    out_imag = lax.dot_general(
        full_rows[0], weighted[1], down, preferred_element_type=jnp.float32
    ) - lax.dot_general(full_rows[1], weighted[0], down, preferred_element_type=jnp.float32)
    return lax.psum_scatter(
        jnp.stack([out_real, out_imag], axis=1), "tile", scatter_dimension=0, tiled=True
    )


def four_shards(green, direction, partners, counts):
    shape = partners.shape
    rows, half = green.shape[1:]
    core_rows = rows // 2
    block = 2 * half // lax.axis_size("tile")
    turns = [2, 3, 1, 0]

    def other_side(index):
        return index ^ 1

    def even_pair(index):
        return index ^ 2

    def odd_pair(index):
        return index ^ 6 if inner(index) else -1

    def inner(index):
        return index // 2 in (1, 2)

    def early(index):
        return inner(index) and index // 2 % 2 != index % 2

    def second_mine(plane, side, core=None):
        return jnp.where(plane < 2, side, 1 - side) == 1

    def first_mine(plane, side, core=None):
        return jnp.where(plane < 2, side, 1 - side) == 0

    def always(plane, side, core=None):
        return plane >= 0

    def of_own(plane, side):
        return 2 * plane + side

    def of_mate(plane, side):
        return 2 * plane + 1 - side

    def of_pair(plane, side):
        return 2 * (plane ^ 1) + side

    def of_next(plane, side):
        return 2 * (3 - plane) + side

    def of_across(plane, side):
        return 2 * (plane ^ 1) + 1 - side

    def of_near(plane, side):
        return 2 * (3 - plane) + 1 - side

    def of_far(plane, side):
        return jnp.where(plane < 2, 6, 1)

    direction_other = cores(direction)
    green_other = cores(green)
    mate = move(green, other_side)
    pair = move(green, even_pair)
    beyond = move(green, odd_pair)
    late_partners, green_other = lax.optimization_barrier((partners, green_other))
    table = pl.pallas_call(
        table_kernel,
        out_shape=jax.ShapeDtypeStruct((TABLE_ROWS, 128), F32),
        in_specs=[SMEM, SMEM],
        out_specs=VMEM,
        compiler_params=PARAMS,
    )(late_partners, counts)
    table_mate = move(table, other_side)
    late_green, late_direction, table = lax.optimization_barrier((green, direction, table))
    green_here, direction_here = stage(late_green, late_direction)
    late_table, direction_other = lax.optimization_barrier((table, direction_other))
    table_pair = move(late_table, even_pair)
    mate, direction_other, green_other, table_mate, green, direction = lax.optimization_barrier(
        (mate, direction_other, green_other, table_mate, green_here, direction_here)
    )
    pair, beyond, table_pair = lax.optimization_barrier((pair, beyond, table_pair))

    mate_sent = pl.pallas_call(
        extend_kernel,
        out_shape=jax.ShapeDtypeStruct((2, rows + TABLE_ROWS, half), BF16),
        in_specs=[VMEM, VMEM],
        out_specs=VMEM,
        compiler_params=PARAMS,
    )(mate, table_mate)
    across = move(mate_sent, even_pair)
    ahead = move(pair, lambda i: odd_pair(i) if inner(i) and not early(i) else -1)
    near = move(beyond, other_side)
    mate_other = cores(mate)
    pair_other = cores(pair)
    beyond_other = cores(beyond)

    first_rows = pick(
        (first_mine, green, mate, None),
        (first_mine, green_other, mate_other, None),
        (second_mine, green, mate, None),
        (second_mine, green_other, mate_other, None),
    )
    row_groups = [first_rows[:2], first_rows[2:], (pair, pair_other)]
    left = images_call(core_rows, row_groups, direction, direction_other)
    columns = columns_call(turns, block, core_rows, row_groups)

    sampled = sampled_call(
        shape,
        [(first_mine, table, table_mate), (second_mine, table, table_mate), (always, table_pair, table_pair)],
    )
    first_blocks = [
        (of_own, [green], [green_other]),
        (of_mate, [mate], [mate_other]),
        (of_pair, [pair], [pair_other]),
        (of_next, [beyond], [beyond_other]),
    ]
    sums = window_call(sampled, shape, rows, left, 0, 3, first_blocks, None, (), apart=True)
    across, ahead, sums, columns = lax.optimization_barrier((across, ahead, sums, columns))

    far_real, far_imag = pick((always, ahead, ahead, 0), (always, across, across, 1), rows=rows)
    far_real = move(far_real, lambda i: other_side(i) if early(i) else -1)
    far_imag = move(far_imag, lambda i: odd_pair(i) if early(i) else -1)
    across_other = cores(across)
    last_row = (across, across_other)
    across_block = (of_across, [across], [across_other])
    sums = window_call(
        sampled, shape, rows, left, 0, 3, [across_block, (of_near, [near], [cores(near)])], sums, (0, 2)
    )
    last_left = images_call(core_rows, [last_row], direction, direction_other)
    last_sampled = sampled_call(shape, [(always, across, across)])
    last_sums = window_call(
        last_sampled, shape, rows, last_left, 0, 1, [*first_blocks, across_block], None, (0,)
    )
    (last_columns,) = columns_call(turns, block, core_rows, [last_row])
    def share(*operands):
        pairs = len(operands) // 3
        return pl.pallas_call(
            functools.partial(base_kernel, block, pairs),
            out_shape=jax.ShapeDtypeStruct((2 * len(turns) * block, half), F32),
            in_specs=[VMEM] * len(operands),
            out_specs=VMEM,
            compiler_params=PARAMS,
        )(*operands)

    base = share(columns[0], sums[0], cores(sums[1]), columns[2], sums[4], cores(sums[5]))
    ahead_other = cores(ahead)
    far_real, far_imag, sums, last_sums = lax.optimization_barrier((far_real, far_imag, sums, last_sums))
    sums, base = lax.optimization_barrier((sums, base))
    weighted_other, couples = window_call(
        sampled,
        shape,
        rows,
        left,
        1,
        1,
        [(of_far, [ahead, far_real, far_imag], [ahead_other, cores(far_real), cores(far_imag)])],
        sums[3:4],
        (0,),
        (1,),
    )
    weighted_other = cores(weighted_other)
    weighted = pl.pallas_call(
        finish_kernel,
        out_shape=jax.ShapeDtypeStruct((rows, half), BF16),
        in_specs=[VMEM] * 5,
        out_specs=VMEM,
        compiler_params=PARAMS,
    )(couples, ahead, far_real, far_imag, sums[2])
    last_base = share(last_columns, last_sums[0], cores(last_sums[1]), base)
    operands = [columns[1], weighted, weighted_other, last_base]

    def terms(first, turns):
        pads = [PAD_ROWS if turn else 0 for turn in turns]
        return pl.pallas_call(
            functools.partial(outer_kernel, first, block, 1, 1),
            out_shape=tuple(jax.ShapeDtypeStruct((2 * block + pad, half), F32) for pad in pads),
            in_specs=[VMEM] * len(operands),
            out_specs=(VMEM,) * len(turns),
            compiler_params=PARAMS,
        )(*operands)

    def send(term, turn):
        return move(term.astype(jnp.float16), lambda i: i ^ 2 * turn if inner(i) or turn == 1 else -1)

    (first,) = terms(0, turns[:1])
    operands[0], first = lax.optimization_barrier((operands[0], first))
    sent = [send(first, turns[0])]
    sent += [send(term, turn) for term, turn in zip(terms(1, turns[1:-1]), turns[1:-1])]
    (total,) = terms(len(turns) - 1, turns[-1:])
    for got in sent:
        got = got.astype(F32)
        total = total + got[: 2 * block] * jnp.exp2(-got[2 * block : 2 * block + 1])
    return pl.pallas_call(
        lay_kernel,
        out_shape=jax.ShapeDtypeStruct((block, 2, half), F32),
        in_specs=[VMEM],
        out_specs=VMEM,
        compiler_params=PARAMS,
    )(total)


def solution(mesh):
    in_specs = (
        P(None, ("freq", "tile"), "src"),
        P(None, ("freq", "src"), None),
        P(("freq", "tile"), None),
        P(("freq", "tile")),
    )
    out_specs = P(("freq", "tile"), None, "src")
    shards = four_shards if mesh.shape["tile"] == 8 else any_shards
    return jax.shard_map(shards, mesh=mesh, in_specs=in_specs, out_specs=out_specs, check_vma=False)
```

```python
import functools

import jax
import jax.numpy as jnp
from jax import lax
from jax.experimental import pallas as pl
from jax.experimental.pallas import tpu as pltpu
from jax.sharding import PartitionSpec as P

F32 = jnp.float32
BF16 = jnp.bfloat16
NOWHERE = -4000
BAND_DEV = 3
PAD_ROWS = 8
TABLE_ROWS = 8
SMEM = pl.BlockSpec(memory_space=pltpu.SMEM)
VMEM = pl.BlockSpec(memory_space=pltpu.VMEM)
PARAMS = pltpu.CompilerParams(vmem_limit_bytes=24 * 1024 * 1024)


def move(value, target):
    count = lax.axis_size("tile")
    pairs = [(source, target(source)) for source in range(count) if 0 <= target(source) < count]
    return lax.ppermute(value, "tile", pairs)


def here():
    place = lax.axis_index("tile")
    return place // 2, place % 2, lax.axis_index("src")


def cores(value):
    return lax.ppermute(value, "src", [(0, 1), (1, 0)])


def dot(a, b):
    return jnp.dot(a, b, preferred_element_type=F32)


def dot_t(a, b):
    return lax.dot_general(a, b, (((1,), (1,)), ((), ())), preferred_element_type=F32)


def images_kernel(core_rows, slots, *refs):
    v_own, v_other, left = refs[2 * slots :]
    half = v_own.shape[1]
    core = lax.axis_index("src")
    at = pl.ds(pl.multiple_of(core * core_rows, core_rows), core_rows)
    sensors = []
    for own, other in zip(refs[: 2 * slots : 2], refs[1 : 2 * slots : 2]):
        own_real, own_imag, other_real, other_imag = own[0, at, :], own[1, at, :], other[0, at, :], other[1, at, :]
        sensors.append(jnp.concatenate([own_real, -own_imag, other_real, -other_imag], axis=1))
        sensors.append(jnp.concatenate([own_imag, own_real, other_imag, other_real], axis=1))
    sensors = jnp.concatenate(sensors, axis=0)
    for index, column in enumerate((core, 1 - core)):
        cols = pl.ds(pl.multiple_of(column * half, half), half)
        values = jnp.concatenate(
            [v_own[0, :, cols], v_own[1, :, cols], v_other[0, :, cols], v_other[1, :, cols]], axis=0
        )
        images = dot(sensors, values).astype(BF16)
        first = slice(2 * index * half, (2 * index + 1) * half)
        second = slice((2 * index + 1) * half, (2 * index + 2) * half)
        left[:, first] = images
        for slot in range(slots):
            real = slice(2 * slot * core_rows, (2 * slot + 1) * core_rows)
            imag = slice((2 * slot + 1) * core_rows, (2 * slot + 2) * core_rows)
            left[real, second] = images[imag]
            left[imag, second] = -images[real]


def images_call(core_rows, groups, direction, direction_other):
    half = direction.shape[1]
    args = [array for pair in groups for array in pair] + [direction, direction_other]
    return pl.pallas_call(
        functools.partial(images_kernel, core_rows, len(groups)),
        out_shape=jax.ShapeDtypeStruct((2 * len(groups) * core_rows, 4 * half), BF16),
        in_specs=[VMEM] * len(args),
        out_specs=VMEM,
        compiler_params=PARAMS,
        cost_estimate=pl.CostEstimate(
            flops=2 * len(groups) * 2 * core_rows * 8 * half * half, bytes_accessed=6 * 1024 * 1024, transcendentals=0
        ),
    )(*args)


def table_kernel(partners_ref, counts_ref, table_ref):
    row = lax.broadcasted_iota(jnp.int32, table_ref.shape, 0)
    col = lax.broadcasted_iota(jnp.int32, table_ref.shape, 1)
    tile_rows, kmax = partners_ref.shape
    table = jnp.zeros(table_ref.shape, F32)
    for r in range(tile_rows):
        for k in range(kmax + 1):
            value = partners_ref[r, k] if k < kmax else counts_ref[r]
            table = jnp.where((row == r) & (col == k), value.astype(F32), table)
    table_ref[...] = table


def stage_kernel(count, *refs):
    sources, targets, arrived = refs[:count], refs[count:-1], refs[-1]
    copies = [pltpu.make_async_copy(a, b, arrived.at[i]) for i, (a, b) in enumerate(zip(sources, targets))]
    for copy in copies:
        copy.start()
    for copy in copies:
        copy.wait()


def stage(*arrays):
    return pl.pallas_call(
        functools.partial(stage_kernel, len(arrays)),
        out_shape=tuple(jax.ShapeDtypeStruct(a.shape, a.dtype) for a in arrays),
        in_specs=[pl.BlockSpec(memory_space=pl.ANY)] * len(arrays),
        out_specs=(VMEM,) * len(arrays),
        scratch_shapes=[pltpu.SemaphoreType.DMA((len(arrays),))],
        compiler_params=PARAMS,
    )(*arrays)


def extend_kernel(block_ref, table_ref, out):
    rows = block_ref.shape[1]
    lanes = table_ref.shape[1]
    for part in range(2):
        out[part, :rows, :] = block_ref[part]
        out[part, rows:, :lanes] = table_ref[...].astype(BF16)
        out[part, rows:, lanes:] = jnp.zeros((TABLE_ROWS, out.shape[2] - lanes), BF16)


def sampled_kernel(kmax, row_tiles, slots, *refs):
    out = refs[-1]
    plane, side, core = here()
    lanes = out.shape[1]

    def table_of(ref):
        return ref[...] if len(ref.shape) == 2 else ref[0, ref.shape[1] - TABLE_ROWS :, :lanes].astype(F32)

    sublane = lax.broadcasted_iota(jnp.int32, (TABLE_ROWS, lanes), 0)
    lane = lax.broadcasted_iota(jnp.int32, (1, lanes), 1)
    out[...] = jnp.full(out.shape, NOWHERE, F32)
    for slot, mine_of in enumerate(slots):
        table = jnp.where(mine_of(plane, side), table_of(refs[2 * slot]), table_of(refs[2 * slot + 1]))
        for row_tile in range(row_tiles):
            wanted = core * row_tiles + row_tile
            row = jnp.sum(jnp.where(sublane == wanted, table, 0.0), axis=0, keepdims=True)
            count = jnp.sum(jnp.where(lane == kmax, row, 0.0), axis=1, keepdims=True)
            count = jnp.where((plane == 0) | (plane == 3), 0.0, count)
            at = slot * row_tiles + row_tile
            out[at : at + 1, :] = jnp.where(lane.astype(F32) < jnp.minimum(count, kmax), row, NOWHERE)


def sampled_call(shape, slots):
    tiles, kmax = shape
    args = [array for slot in slots for array in slot[1:]]
    return pl.pallas_call(
        functools.partial(sampled_kernel, kmax, tiles // 2, [slot[0] for slot in slots]),
        out_shape=jax.ShapeDtypeStruct((8, 128), F32),
        in_specs=[VMEM] * len(args),
        out_specs=VMEM,
        compiler_params=PARAMS,
    )(*args)


def window_kernel(blocks, slots, skip, shape, done, start, source_halves, apart, sampled, left, *refs):
    plane, side, core = here()
    tiles = shape[0]
    row_tiles = tiles // 2
    core_rows = left.shape[0] // (2 * (skip + slots)) if not skip else refs[1].shape[0] // 2
    rows = 2 * core_rows
    held = []
    for group_of, width in blocks:
        halves = []
        for _ in range(2):
            if width == 1:
                halves.append((refs[0][0, :rows, :], refs[0][1, :rows, :]))
            else:
                late = side == plane % 2
                whole, real, imag = refs[:3]
                halves.append(
                    (jnp.where(late, real[...], whole[0, :rows, :]), jnp.where(late, imag[...], whole[1, :rows, :]))
                )
            refs = refs[width:]
        held.append((group_of(plane, side), *halves))
    tile = core_rows // row_tiles
    count = len(source_halves) * slots
    sums, outs, couples = refs[: 0 if start else count], refs[-count - 1 : -1], refs[-1]
    left_rows = left[skip * rows : (skip + slots) * rows, :]
    wide = tiles * tile
    for block, (group, own, other) in enumerate(held):
        readers = slots - 1 if apart and block == len(held) - 1 else slots
        couple = dot_t(left_rows[: readers * rows], jnp.concatenate([*own, *other], axis=1))
        for index in range(readers * row_tiles):
            partners = sampled[skip * row_tiles + index : skip * row_tiles + index + 1, :]
            begin = index // row_tiles * rows + index % row_tiles * tile
            upper = slice(begin, begin + tile)
            lower = slice(begin + core_rows, begin + core_rows + tile)
            for c in range(tiles):
                wanted = (group * tiles + c).astype(F32)
                keep = jnp.max(jnp.where(partners == wanted, 1.0, 0.0), axis=1, keepdims=True)
                real = (couple[upper, c * tile : (c + 1) * tile] * keep).astype(BF16)
                imag = (couple[lower, c * tile : (c + 1) * tile] * keep).astype(BF16)
                at = 2 * block * wide + c * tile
                couples[upper, at : at + tile] = real
                couples[lower, at : at + tile] = imag
                couples[upper, at + wide : at + wide + tile] = -imag
                couples[lower, at + wide : at + wide + tile] = real
    for position, index in enumerate(source_halves):
        values = jnp.concatenate([part for block in held for part in block[1 + index]], axis=0)
        if apart:
            cut, depth = (slots - 1) * rows, couples.shape[1] - 2 * rows
            total = jnp.concatenate(
                [dot(couples[:cut, :], values), dot(couples[cut:, :depth], values[:depth])], axis=0
            )
        else:
            total = dot(couples[...], values)
        for slot in range(slots):
            part = total[slot * rows : (slot + 1) * rows]
            if not start:
                part = part + sums[len(source_halves) * slot + position][...]
            outs[len(source_halves) * slot + position][...] = part.astype(BF16) if slot in done else part


def window_call(sampled, shape, rows, left, skip, slots, blocks, sums, done, halves=(0, 1), apart=False):
    args = [sampled, left]
    for _, own, other in blocks:
        args.extend(own)
        args.extend(other)
    if sums is not None:
        args.extend(sums)
    half = left.shape[1] // 4
    outs = [jax.ShapeDtypeStruct((rows, half), BF16 if slot in done else F32) for slot in range(slots) for _ in halves]
    couples = (slots * rows, 2 * len(blocks) * rows)
    if len(halves) == 1:
        outs.append(jax.ShapeDtypeStruct(couples, BF16))
    return pl.pallas_call(
        functools.partial(
            window_kernel,
            [(group_of, len(own)) for group_of, own, _ in blocks],
            slots,
            skip,
            shape,
            done,
            sums is None,
            halves,
            apart,
        ),
        out_shape=tuple(outs),
        in_specs=[VMEM] * len(args),
        out_specs=(VMEM,) * len(outs),
        scratch_shapes=[pltpu.VMEM(couples, BF16)] if len(halves) == 2 else [],
        compiler_params=PARAMS,
        cost_estimate=pl.CostEstimate(
            flops=len(blocks) * slots * 2 * 2 * rows * 4 * half * rows,
            bytes_accessed=sum(a.size * a.dtype.itemsize for a in args),
            transcendentals=0,
        ),
    )(*args)


def finish_kernel(couples, whole, real, imag, held, out):
    plane, side, core = here()
    late = side == plane % 2
    rows = out.shape[0]
    values = [jnp.where(late, part[...], whole[index, :rows, :]) for index, part in enumerate((real, imag))]
    out[...] = (held[...] + dot(couples[...], jnp.concatenate(values, axis=0))).astype(BF16)


def pick_kernel(choices, *refs):
    place = here()
    outs = refs[len(refs) - len(choices) :]

    def put(out, value, part):
        out[...] = value[...] if part is None else value[part, : out.shape[0], :]

    for index, (flag_of, part) in enumerate(choices):
        flag = flag_of(*place)
        first, second, out = refs[2 * index], refs[2 * index + 1], outs[index]
        pl.when(flag)(functools.partial(put, out, first, part))
        pl.when(jnp.logical_not(flag))(functools.partial(put, out, second, part))


def pick(*choices, rows=None):
    args = [value for choice in choices for value in choice[1:3]]
    shapes = [
        a.shape if choice[3] is None else (rows, a.shape[2]) for a, choice in zip(args[::2], choices)
    ]
    return pl.pallas_call(
        functools.partial(pick_kernel, [(choice[0], choice[3]) for choice in choices]),
        out_shape=tuple(jax.ShapeDtypeStruct(shape, args[0].dtype) for shape in shapes),
        in_specs=[VMEM] * len(args),
        out_specs=(VMEM,) * len(choices),
        compiler_params=PARAMS,
    )(*args)


def columns_kernel(turns, block, core_rows, *refs):
    plane, side, core = here()
    slots = len(refs) // 3
    half = refs[0].shape[2]
    for index, turn in enumerate(turns):
        first = (2 * (plane ^ turn) + side) * block
        own = first // half == core
        cols = pl.ds(pl.multiple_of(lax.rem(first, half), block), block)
        for slot in range(slots):
            out = refs[2 * slots + slot]
            for position, reader in enumerate((core, 1 - core)):
                at = pl.ds(pl.multiple_of(reader * core_rows, core_rows), core_rows)
                for part in range(2):
                    value = jnp.where(own, refs[2 * slot][part, at, cols], refs[2 * slot + 1][part, at, cols])
                    start = (2 * position + part) * core_rows
                    out[index * block : (index + 1) * block, start : start + core_rows] = value.T


def columns_call(turns, block, core_rows, groups):
    args = [array for pair in groups for array in pair]
    out = jax.ShapeDtypeStruct((len(turns) * block, 4 * core_rows), BF16)
    return pl.pallas_call(
        functools.partial(columns_kernel, turns, block, core_rows),
        out_shape=(out,) * len(groups),
        in_specs=[VMEM] * len(args),
        out_specs=(VMEM,) * len(groups),
        compiler_params=PARAMS,
    )(*args)


def outer_kernel(first, block, pairs, base, *refs):
    half = refs[1].shape[1]
    straight, turned = [], []
    for index in range(pairs):
        for w in refs[3 * index + 1 : 3 * index + 3]:
            rows = w.shape[0] // 2
            straight.append(w[...])
            turned.extend([w[rows:, :], -w[:rows, :]])
    straight = jnp.concatenate(straight, axis=0)
    turned = jnp.concatenate(turned, axis=0)
    for index, out in enumerate(refs[3 * pairs + base :]):
        at = slice((first + index) * block, (first + index + 1) * block)
        a = jnp.concatenate([refs[3 * pair][at, :] for pair in range(pairs)], axis=1)
        real = dot(a, straight)
        imag = dot(a, turned)
        if base:
            begin = 2 * (first + index) * block
            real += refs[3 * pairs][begin : begin + block, :]
            imag += refs[3 * pairs][begin + block : begin + 2 * block, :]
        if out.shape[0] > 2 * block:
            top = jnp.maximum(jnp.max(jnp.abs(real)), jnp.max(jnp.abs(imag)))
            power = 14.0 - jnp.ceil(jnp.log2(jnp.full((PAD_ROWS, half), jnp.maximum(top, 1e-30), F32)))
            power = jnp.clip(power, -110.0, 110.0)
            scale = jnp.exp2(power)[:1]
            out[:block, :] = real * scale
            out[block : 2 * block, :] = imag * scale
            out[2 * block :, :] = power
        else:
            out[:block, :] = real
            out[block:, :] = imag


def base_kernel(block, pairs, *refs):
    out = refs[-1]
    straight, turned = [], []
    for index in range(pairs):
        for w in refs[3 * index + 1 : 3 * index + 3]:
            rows = w.shape[0] // 2
            straight.append(w[...])
            turned.extend([w[rows:, :], -w[:rows, :]])
    straight = jnp.concatenate(straight, axis=0)
    turned = jnp.concatenate(turned, axis=0)
    for index in range(out.shape[0] // (2 * block)):
        a = jnp.concatenate([ref[index * block : (index + 1) * block, :] for ref in refs[: 3 * pairs : 3]], axis=1)
        for part, w in enumerate((straight, turned)):
            at = slice((2 * index + part) * block, (2 * index + part + 1) * block)
            term = dot(a, w)
            out[at, :] = term if len(refs) == 3 * pairs + 1 else term + refs[-2][at, :]


def lay_kernel(total, *refs):
    got, out = refs[:-1], refs[-1]
    block = total.shape[0] // 2
    for part in range(2):
        at = slice(part * block, (part + 1) * block)
        value = total[at, :]
        for term in got:
            value += term[at, :] * jnp.exp2(-term[2 * block : 2 * block + 1, :])
        out[:, part, :] = value


def from_behind(value, axis, steps):
    count = lax.axis_size(axis)
    first, last = (max(0, -steps), min(count, count - steps))
    return lax.ppermute(value, axis, [(source, source + steps) for source in range(first, last)])


def any_shards(green, direction, partners, counts):
    tile_dev, kmax = partners.shape
    rows = green.shape[1]
    half = green.shape[2]
    tile = rows // tile_dev
    real_part = jnp.dot(green[0], direction[0], preferred_element_type=jnp.float32) - jnp.dot(
        green[1], direction[1], preferred_element_type=jnp.float32
    )
    imag_part = jnp.dot(green[0], direction[1], preferred_element_type=jnp.float32) + jnp.dot(
        green[1], direction[0], preferred_element_type=jnp.float32
    )
    images = lax.psum_scatter(
        jnp.stack([real_part, imag_part]), "src", scatter_dimension=2, tiled=True
    ).astype(jnp.bfloat16)
    tiles = green.reshape(2, tile_dev, tile, half)
    count_tile = lax.axis_size("tile")
    reach = min(BAND_DEV, count_tile - 1)
    empty = jnp.zeros_like(tiles)
    offsets = [offset for offset in range(-reach, reach + 1) if offset != 0]
    moved = [from_behind(tiles, "tile", -offset) for offset in offsets]
    nearby = dict(zip(offsets, moved))
    nearby[0] = tiles
    window = jnp.concatenate(
        [nearby.get(offset, empty) for offset in range(-BAND_DEV, BAND_DEV + 1)], axis=1
    )
    first_tile = (lax.axis_index("tile") - BAND_DEV) * tile_dev
    local_index = partners - first_tile
    live = (jnp.arange(kmax, dtype=jnp.int32)[None, :] < counts[:, None]).astype(jnp.float32)
    across = (((1,), (1,)), ((), ()))
    stacks = []
    pieces = []
    for row in range(tile_dev):
        stack = jnp.take(window, local_index[row], axis=1).reshape(2, kmax * tile, half)
        stacks.append(stack)
        image_row = images[:, row * tile : (row + 1) * tile]
        couple_real = lax.dot_general(
            image_row[0], stack[0], across, preferred_element_type=jnp.float32
        ) + lax.dot_general(image_row[1], stack[1], across, preferred_element_type=jnp.float32)
        couple_imag = lax.dot_general(
            image_row[1], stack[0], across, preferred_element_type=jnp.float32
        ) - lax.dot_general(image_row[0], stack[1], across, preferred_element_type=jnp.float32)
        blocks = jnp.stack([couple_real, couple_imag]).reshape(2, tile, kmax, tile)
        pieces.append(blocks * live[row][None, None, :, None])
    partial_blocks = jnp.stack(pieces, axis=1)
    coupling = lax.psum(partial_blocks, "src").astype(jnp.bfloat16)
    weight_rows = []
    for row in range(tile_dev):
        stack = stacks[row]
        flat = coupling[:, row].reshape(2, tile, kmax * tile)
        weight_real = jnp.dot(flat[0], stack[0], preferred_element_type=jnp.float32) - jnp.dot(
            flat[1], stack[1], preferred_element_type=jnp.float32
        )
        weight_imag = jnp.dot(flat[0], stack[1], preferred_element_type=jnp.float32) + jnp.dot(
            flat[1], stack[0], preferred_element_type=jnp.float32
        )
        weight_rows.append(jnp.stack([weight_real, weight_imag]))
    weighted = jnp.concatenate(weight_rows, axis=1).astype(jnp.bfloat16)
    full_rows = lax.all_gather(green, "src", axis=2, tiled=True)
    down = (((0,), (0,)), ((), ()))
    out_real = lax.dot_general(
        full_rows[0], weighted[0], down, preferred_element_type=jnp.float32
    ) + lax.dot_general(full_rows[1], weighted[1], down, preferred_element_type=jnp.float32)
    out_imag = lax.dot_general(
        full_rows[0], weighted[1], down, preferred_element_type=jnp.float32
    ) - lax.dot_general(full_rows[1], weighted[0], down, preferred_element_type=jnp.float32)
    return lax.psum_scatter(
        jnp.stack([out_real, out_imag], axis=1), "tile", scatter_dimension=0, tiled=True
    )


def four_shards(green, direction, partners, counts):
    shape = partners.shape
    rows, half = green.shape[1:]
    core_rows = rows // 2
    block = 2 * half // lax.axis_size("tile")
    turns = [2, 3, 1, 0]

    def other_side(index):
        return index ^ 1

    def even_pair(index):
        return index ^ 2

    def odd_pair(index):
        return index ^ 6 if inner(index) else -1

    def inner(index):
        return index // 2 in (1, 2)

    def early(index):
        return inner(index) and index // 2 % 2 != index % 2

    def second_mine(plane, side, core=None):
        return jnp.where(plane < 2, side, 1 - side) == 1

    def first_mine(plane, side, core=None):
        return jnp.where(plane < 2, side, 1 - side) == 0

    def always(plane, side, core=None):
        return plane >= 0

    def of_own(plane, side):
        return 2 * plane + side

    def of_mate(plane, side):
        return 2 * plane + 1 - side

    def of_pair(plane, side):
        return 2 * (plane ^ 1) + side

    def of_next(plane, side):
        return 2 * (3 - plane) + side

    def of_across(plane, side):
        return 2 * (plane ^ 1) + 1 - side

    def of_near(plane, side):
        return 2 * (3 - plane) + 1 - side

    def of_far(plane, side):
        return jnp.where(plane < 2, 6, 1)

    direction_other = cores(direction)
    green_other = cores(green)
    mate = move(green, other_side)
    pair = move(green, even_pair)
    beyond = move(green, odd_pair)
    late_partners, green_other = lax.optimization_barrier((partners, green_other))
    table = pl.pallas_call(
        table_kernel,
        out_shape=jax.ShapeDtypeStruct((TABLE_ROWS, 128), F32),
        in_specs=[SMEM, SMEM],
        out_specs=VMEM,
        compiler_params=PARAMS,
    )(late_partners, counts)
    table_mate = move(table, other_side)
    late_green, late_direction, table = lax.optimization_barrier((green, direction, table))
    green_here, direction_here = stage(late_green, late_direction)
    late_table, direction_other = lax.optimization_barrier((table, direction_other))
    table_pair = move(late_table, even_pair)
    mate, direction_other, green_other, table_mate, green, direction = lax.optimization_barrier(
        (mate, direction_other, green_other, table_mate, green_here, direction_here)
    )
    pair, beyond, table_pair = lax.optimization_barrier((pair, beyond, table_pair))

    mate_sent = pl.pallas_call(
        extend_kernel,
        out_shape=jax.ShapeDtypeStruct((2, rows + TABLE_ROWS, half), BF16),
        in_specs=[VMEM, VMEM],
        out_specs=VMEM,
        compiler_params=PARAMS,
    )(mate, table_mate)
    across = move(mate_sent, even_pair)
    ahead = move(pair, lambda i: odd_pair(i) if inner(i) and not early(i) else -1)
    near = move(beyond, other_side)
    mate_other = cores(mate)
    pair_other = cores(pair)
    beyond_other = cores(beyond)

    first_rows = pick(
        (first_mine, green, mate, None),
        (first_mine, green_other, mate_other, None),
        (second_mine, green, mate, None),
        (second_mine, green_other, mate_other, None),
    )
    row_groups = [first_rows[:2], first_rows[2:], (pair, pair_other)]
    left = images_call(core_rows, row_groups, direction, direction_other)
    columns = columns_call(turns, block, core_rows, row_groups)

    sampled = sampled_call(
        shape,
        [(first_mine, table, table_mate), (second_mine, table, table_mate), (always, table_pair, table_pair)],
    )
    first_blocks = [
        (of_own, [green], [green_other]),
        (of_mate, [mate], [mate_other]),
        (of_pair, [pair], [pair_other]),
        (of_next, [beyond], [beyond_other]),
    ]
    sums = window_call(sampled, shape, rows, left, 0, 3, first_blocks, None, (), apart=True)
    across, ahead, sums, columns = lax.optimization_barrier((across, ahead, sums, columns))

    far_real, far_imag = pick((always, across, across, 0), (always, ahead, ahead, 1), rows=rows)
    far_real = move(far_real, lambda i: odd_pair(i) if early(i) else -1)
    far_imag = move(far_imag, lambda i: other_side(i) if early(i) else -1)
    across_other = cores(across)
    last_row = (across, across_other)
    across_block = (of_across, [across], [across_other])
    sums = window_call(
        sampled, shape, rows, left, 0, 3, [across_block, (of_near, [near], [cores(near)])], sums, (0, 2)
    )
    last_left = images_call(core_rows, [last_row], direction, direction_other)
    last_sampled = sampled_call(shape, [(always, across, across)])
    last_sums = window_call(
        last_sampled, shape, rows, last_left, 0, 1, [*first_blocks, across_block], None, (0,)
    )
    (last_columns,) = columns_call(turns, block, core_rows, [last_row])
    def share(*operands):
        pairs = len(operands) // 3
        return pl.pallas_call(
            functools.partial(base_kernel, block, pairs),
            out_shape=jax.ShapeDtypeStruct((2 * len(turns) * block, half), F32),
            in_specs=[VMEM] * len(operands),
            out_specs=VMEM,
            compiler_params=PARAMS,
        )(*operands)

    base = share(columns[0], sums[0], cores(sums[1]), columns[2], sums[4], cores(sums[5]))
    ahead_other = cores(ahead)
    far_real, far_imag, sums, last_sums = lax.optimization_barrier((far_real, far_imag, sums, last_sums))
    sums, base = lax.optimization_barrier((sums, base))
    weighted_other, couples = window_call(
        sampled,
        shape,
        rows,
        left,
        1,
        1,
        [(of_far, [ahead, far_real, far_imag], [ahead_other, cores(far_real), cores(far_imag)])],
        sums[3:4],
        (0,),
        (1,),
    )
    weighted_other = cores(weighted_other)
    weighted = pl.pallas_call(
        finish_kernel,
        out_shape=jax.ShapeDtypeStruct((rows, half), BF16),
        in_specs=[VMEM] * 5,
        out_specs=VMEM,
        compiler_params=PARAMS,
    )(couples, ahead, far_real, far_imag, sums[2])
    last_base = share(last_columns, last_sums[0], cores(last_sums[1]), base)
    operands = [columns[1], weighted, weighted_other, last_base]

    def terms(first, turns):
        pads = [PAD_ROWS if turn else 0 for turn in turns]
        return pl.pallas_call(
            functools.partial(outer_kernel, first, block, 1, 1),
            out_shape=tuple(jax.ShapeDtypeStruct((2 * block + pad, half), F32) for pad in pads),
            in_specs=[VMEM] * len(operands),
            out_specs=(VMEM,) * len(turns),
            compiler_params=PARAMS,
        )(*operands)

    def send(term, turn):
        return move(term.astype(jnp.float16), lambda i: i ^ 2 * turn if inner(i) or turn == 1 else -1)

    (first,) = terms(0, turns[:1])
    operands[0], first = lax.optimization_barrier((operands[0], first))
    sent = [send(first, turns[0])]
    sent += [send(term, turn) for term, turn in zip(terms(1, turns[1:-1]), turns[1:-1])]
    (total,) = terms(len(turns) - 1, turns[-1:])
    args = [total] + [got.astype(F32) for got in sent]
    return pl.pallas_call(
        lay_kernel,
        out_shape=jax.ShapeDtypeStruct((block, 2, half), F32),
        in_specs=[VMEM] * len(args),
        out_specs=VMEM,
        compiler_params=PARAMS,
    )(*args)


def solution(mesh):
    in_specs = (
        P(None, ("freq", "tile"), "src"),
        P(None, ("freq", "src"), None),
        P(("freq", "tile"), None),
        P(("freq", "tile")),
    )
    out_specs = P(("freq", "tile"), None, "src")
    shards = four_shards if mesh.shape["tile"] == 8 else any_shards
    return jax.shard_map(shards, mesh=mesh, in_specs=in_specs, out_specs=out_specs, check_vma=False)
```

```python
import functools

import jax
import jax.numpy as jnp
from jax import lax
from jax.experimental import pallas as pl
from jax.experimental.pallas import tpu as pltpu
from jax.sharding import PartitionSpec as P

F32 = jnp.float32
BF16 = jnp.bfloat16
NOWHERE = -4000
BAND_DEV = 3
PAD_ROWS = 8
TABLE_ROWS = 8
SMEM = pl.BlockSpec(memory_space=pltpu.SMEM)
VMEM = pl.BlockSpec(memory_space=pltpu.VMEM)
PARAMS = pltpu.CompilerParams(vmem_limit_bytes=24 * 1024 * 1024)


def move(value, target):
    count = lax.axis_size("tile")
    pairs = [(source, target(source)) for source in range(count) if 0 <= target(source) < count]
    return lax.ppermute(value, "tile", pairs)


def here():
    place = lax.axis_index("tile")
    return place // 2, place % 2, lax.axis_index("src")


def cores(value):
    return lax.ppermute(value, "src", [(0, 1), (1, 0)])


def dot(a, b):
    return jnp.dot(a, b, preferred_element_type=F32)


def dot_t(a, b):
    return lax.dot_general(a, b, (((1,), (1,)), ((), ())), preferred_element_type=F32)


def images_kernel(core_rows, slots, *refs):
    v_own, v_other, left = refs[2 * slots :]
    half = v_own.shape[1]
    core = lax.axis_index("src")
    at = pl.ds(pl.multiple_of(core * core_rows, core_rows), core_rows)
    sensors = []
    for own, other in zip(refs[: 2 * slots : 2], refs[1 : 2 * slots : 2]):
        own_real, own_imag, other_real, other_imag = own[0, at, :], own[1, at, :], other[0, at, :], other[1, at, :]
        sensors.append(jnp.concatenate([own_real, -own_imag, other_real, -other_imag], axis=1))
        sensors.append(jnp.concatenate([own_imag, own_real, other_imag, other_real], axis=1))
    sensors = jnp.concatenate(sensors, axis=0)
    for index, column in enumerate((core, 1 - core)):
        cols = pl.ds(pl.multiple_of(column * half, half), half)
        values = jnp.concatenate(
            [v_own[0, :, cols], v_own[1, :, cols], v_other[0, :, cols], v_other[1, :, cols]], axis=0
        )
        images = dot(sensors, values).astype(BF16)
        first = slice(2 * index * half, (2 * index + 1) * half)
        second = slice((2 * index + 1) * half, (2 * index + 2) * half)
        left[:, first] = images
        for slot in range(slots):
            real = slice(2 * slot * core_rows, (2 * slot + 1) * core_rows)
            imag = slice((2 * slot + 1) * core_rows, (2 * slot + 2) * core_rows)
            left[real, second] = images[imag]
            left[imag, second] = -images[real]


def images_call(core_rows, groups, direction, direction_other):
    half = direction.shape[1]
    args = [array for pair in groups for array in pair] + [direction, direction_other]
    return pl.pallas_call(
        functools.partial(images_kernel, core_rows, len(groups)),
        out_shape=jax.ShapeDtypeStruct((2 * len(groups) * core_rows, 4 * half), BF16),
        in_specs=[VMEM] * len(args),
        out_specs=VMEM,
        compiler_params=PARAMS,
        cost_estimate=pl.CostEstimate(
            flops=2 * len(groups) * 2 * core_rows * 8 * half * half, bytes_accessed=6 * 1024 * 1024, transcendentals=0
        ),
    )(*args)


def table_kernel(partners_ref, counts_ref, table_ref):
    row = lax.broadcasted_iota(jnp.int32, table_ref.shape, 0)
    col = lax.broadcasted_iota(jnp.int32, table_ref.shape, 1)
    tile_rows, kmax = partners_ref.shape
    table = jnp.zeros(table_ref.shape, F32)
    for r in range(tile_rows):
        for k in range(kmax + 1):
            value = partners_ref[r, k] if k < kmax else counts_ref[r]
            table = jnp.where((row == r) & (col == k), value.astype(F32), table)
    table_ref[...] = table


def stage_kernel(count, *refs):
    sources, targets, arrived = refs[:count], refs[count:-1], refs[-1]
    copies = [pltpu.make_async_copy(a, b, arrived.at[i]) for i, (a, b) in enumerate(zip(sources, targets))]
    for copy in copies:
        copy.start()
    for copy in copies:
        copy.wait()


def stage(*arrays):
    return pl.pallas_call(
        functools.partial(stage_kernel, len(arrays)),
        out_shape=tuple(jax.ShapeDtypeStruct(a.shape, a.dtype) for a in arrays),
        in_specs=[pl.BlockSpec(memory_space=pl.ANY)] * len(arrays),
        out_specs=(VMEM,) * len(arrays),
        scratch_shapes=[pltpu.SemaphoreType.DMA((len(arrays),))],
        compiler_params=PARAMS,
    )(*arrays)


def extend_kernel(block_ref, table_ref, out):
    rows = block_ref.shape[1]
    lanes = table_ref.shape[1]
    for part in range(2):
        out[part, :rows, :] = block_ref[part]
        out[part, rows:, :lanes] = table_ref[...].astype(BF16)
        out[part, rows:, lanes:] = jnp.zeros((TABLE_ROWS, out.shape[2] - lanes), BF16)


def sampled_kernel(kmax, row_tiles, slots, *refs):
    out = refs[-1]
    plane, side, core = here()
    lanes = out.shape[1]

    def table_of(ref):
        return ref[...] if len(ref.shape) == 2 else ref[0, ref.shape[1] - TABLE_ROWS :, :lanes].astype(F32)

    sublane = lax.broadcasted_iota(jnp.int32, (TABLE_ROWS, lanes), 0)
    lane = lax.broadcasted_iota(jnp.int32, (1, lanes), 1)
    out[...] = jnp.full(out.shape, NOWHERE, F32)
    for slot, mine_of in enumerate(slots):
        table = jnp.where(mine_of(plane, side), table_of(refs[2 * slot]), table_of(refs[2 * slot + 1]))
        for row_tile in range(row_tiles):
            wanted = core * row_tiles + row_tile
            row = jnp.sum(jnp.where(sublane == wanted, table, 0.0), axis=0, keepdims=True)
            count = jnp.sum(jnp.where(lane == kmax, row, 0.0), axis=1, keepdims=True)
            count = jnp.where((plane == 0) | (plane == 3), 0.0, count)
            at = slot * row_tiles + row_tile
            out[at : at + 1, :] = jnp.where(lane.astype(F32) < jnp.minimum(count, kmax), row, NOWHERE)


def sampled_call(shape, slots):
    tiles, kmax = shape
    args = [array for slot in slots for array in slot[1:]]
    return pl.pallas_call(
        functools.partial(sampled_kernel, kmax, tiles // 2, [slot[0] for slot in slots]),
        out_shape=jax.ShapeDtypeStruct((8, 128), F32),
        in_specs=[VMEM] * len(args),
        out_specs=VMEM,
        compiler_params=PARAMS,
    )(*args)


def window_kernel(blocks, slots, skip, shape, done, start, source_halves, apart, sampled, left, *refs):
    plane, side, core = here()
    tiles = shape[0]
    row_tiles = tiles // 2
    core_rows = left.shape[0] // (2 * (skip + slots)) if not skip else refs[1].shape[0] // 2
    rows = 2 * core_rows
    held = []
    for group_of, width in blocks:
        halves = []
        for _ in range(2):
            if width == 1:
                halves.append((refs[0][0, :rows, :], refs[0][1, :rows, :]))
            else:
                late = side == plane % 2
                whole, real, imag = refs[:3]
                halves.append(
                    (jnp.where(late, real[...], whole[0, :rows, :]), jnp.where(late, imag[...], whole[1, :rows, :]))
                )
            refs = refs[width:]
        held.append((group_of(plane, side), *halves))
    tile = core_rows // row_tiles
    count = len(source_halves) * slots
    sums, outs, couples = refs[: 0 if start else count], refs[-count - 1 : -1], refs[-1]
    left_rows = left[skip * rows : (skip + slots) * rows, :]
    wide = tiles * tile
    for block, (group, own, other) in enumerate(held):
        readers = slots - 1 if apart and block == len(held) - 1 else slots
        couple = dot_t(left_rows[: readers * rows], jnp.concatenate([*own, *other], axis=1))
        for index in range(readers * row_tiles):
            partners = sampled[skip * row_tiles + index : skip * row_tiles + index + 1, :]
            begin = index // row_tiles * rows + index % row_tiles * tile
            upper = slice(begin, begin + tile)
            lower = slice(begin + core_rows, begin + core_rows + tile)
            for c in range(tiles):
                wanted = (group * tiles + c).astype(F32)
                keep = jnp.max(jnp.where(partners == wanted, 1.0, 0.0), axis=1, keepdims=True)
                real = (couple[upper, c * tile : (c + 1) * tile] * keep).astype(BF16)
                imag = (couple[lower, c * tile : (c + 1) * tile] * keep).astype(BF16)
                at = 2 * block * wide + c * tile
                couples[upper, at : at + tile] = real
                couples[lower, at : at + tile] = imag
                couples[upper, at + wide : at + wide + tile] = -imag
                couples[lower, at + wide : at + wide + tile] = real
    for position, index in enumerate(source_halves):
        values = jnp.concatenate([part for block in held for part in block[1 + index]], axis=0)
        if apart:
            cut, depth = (slots - 1) * rows, couples.shape[1] - 2 * rows
            total = jnp.concatenate(
                [dot(couples[:cut, :], values), dot(couples[cut:, :depth], values[:depth])], axis=0
            )
        else:
            total = dot(couples[...], values)
        for slot in range(slots):
            part = total[slot * rows : (slot + 1) * rows]
            if not start:
                part = part + sums[len(source_halves) * slot + position][...]
            outs[len(source_halves) * slot + position][...] = part.astype(BF16) if slot in done else part


def window_call(sampled, shape, rows, left, skip, slots, blocks, sums, done, halves=(0, 1), apart=False):
    args = [sampled, left]
    for _, own, other in blocks:
        args.extend(own)
        args.extend(other)
    if sums is not None:
        args.extend(sums)
    half = left.shape[1] // 4
    outs = [jax.ShapeDtypeStruct((rows, half), BF16 if slot in done else F32) for slot in range(slots) for _ in halves]
    couples = (slots * rows, 2 * len(blocks) * rows)
    if len(halves) == 1:
        outs.append(jax.ShapeDtypeStruct(couples, BF16))
    return pl.pallas_call(
        functools.partial(
            window_kernel,
            [(group_of, len(own)) for group_of, own, _ in blocks],
            slots,
            skip,
            shape,
            done,
            sums is None,
            halves,
            apart,
        ),
        out_shape=tuple(outs),
        in_specs=[VMEM] * len(args),
        out_specs=(VMEM,) * len(outs),
        scratch_shapes=[pltpu.VMEM(couples, BF16)] if len(halves) == 2 else [],
        compiler_params=PARAMS,
        cost_estimate=pl.CostEstimate(
            flops=len(blocks) * slots * 2 * 2 * rows * 4 * half * rows,
            bytes_accessed=sum(a.size * a.dtype.itemsize for a in args),
            transcendentals=0,
        ),
    )(*args)


def finish_kernel(couples, whole, real, imag, held, out):
    plane, side, core = here()
    late = side == plane % 2
    rows = out.shape[0]
    values = [jnp.where(late, part[...], whole[index, :rows, :]) for index, part in enumerate((real, imag))]
    out[...] = (held[...] + dot(couples[...], jnp.concatenate(values, axis=0))).astype(BF16)


def pick_kernel(choices, *refs):
    place = here()
    outs = refs[len(refs) - len(choices) :]

    def put(out, value, part):
        out[...] = value[...] if part is None else value[part, : out.shape[0], :]

    for index, (flag_of, part) in enumerate(choices):
        flag = flag_of(*place)
        first, second, out = refs[2 * index], refs[2 * index + 1], outs[index]
        pl.when(flag)(functools.partial(put, out, first, part))
        pl.when(jnp.logical_not(flag))(functools.partial(put, out, second, part))


def pick(*choices, rows=None):
    args = [value for choice in choices for value in choice[1:3]]
    shapes = [
        a.shape if choice[3] is None else (rows, a.shape[2]) for a, choice in zip(args[::2], choices)
    ]
    return pl.pallas_call(
        functools.partial(pick_kernel, [(choice[0], choice[3]) for choice in choices]),
        out_shape=tuple(jax.ShapeDtypeStruct(shape, args[0].dtype) for shape in shapes),
        in_specs=[VMEM] * len(args),
        out_specs=(VMEM,) * len(choices),
        compiler_params=PARAMS,
    )(*args)


def columns_kernel(turns, block, core_rows, *refs):
    plane, side, core = here()
    slots = len(refs) // 3
    half = refs[0].shape[2]
    for index, turn in enumerate(turns):
        first = (2 * (plane ^ turn) + side) * block
        own = first // half == core
        cols = pl.ds(pl.multiple_of(lax.rem(first, half), block), block)
        for slot in range(slots):
            out = refs[2 * slots + slot]
            for position, reader in enumerate((core, 1 - core)):
                at = pl.ds(pl.multiple_of(reader * core_rows, core_rows), core_rows)
                for part in range(2):
                    value = jnp.where(own, refs[2 * slot][part, at, cols], refs[2 * slot + 1][part, at, cols])
                    start = (2 * position + part) * core_rows
                    out[index * block : (index + 1) * block, start : start + core_rows] = value.T


def columns_call(turns, block, core_rows, groups):
    args = [array for pair in groups for array in pair]
    out = jax.ShapeDtypeStruct((len(turns) * block, 4 * core_rows), BF16)
    return pl.pallas_call(
        functools.partial(columns_kernel, turns, block, core_rows),
        out_shape=(out,) * len(groups),
        in_specs=[VMEM] * len(args),
        out_specs=(VMEM,) * len(groups),
        compiler_params=PARAMS,
    )(*args)


def outer_kernel(first, block, pairs, base, *refs):
    half = refs[1].shape[1]
    straight, turned = [], []
    for index in range(pairs):
        for w in refs[3 * index + 1 : 3 * index + 3]:
            rows = w.shape[0] // 2
            straight.append(w[...])
            turned.extend([w[rows:, :], -w[:rows, :]])
    straight = jnp.concatenate(straight, axis=0)
    turned = jnp.concatenate(turned, axis=0)
    for index, out in enumerate(refs[3 * pairs + base :]):
        at = slice((first + index) * block, (first + index + 1) * block)
        a = jnp.concatenate([refs[3 * pair][at, :] for pair in range(pairs)], axis=1)
        real = dot(a, straight)
        imag = dot(a, turned)
        if base:
            begin = 2 * (first + index) * block
            real += refs[3 * pairs][begin : begin + block, :]
            imag += refs[3 * pairs][begin + block : begin + 2 * block, :]
        if out.shape[0] > 2 * block:
            top = jnp.maximum(jnp.max(jnp.abs(real)), jnp.max(jnp.abs(imag)))
            power = 14.0 - jnp.ceil(jnp.log2(jnp.full((PAD_ROWS, half), jnp.maximum(top, 1e-30), F32)))
            power = jnp.clip(power, -110.0, 110.0)
            scale = jnp.exp2(power)[:1]
            out[:block, :] = real * scale
            out[block : 2 * block, :] = imag * scale
            out[2 * block :, :] = power
        else:
            out[:block, :] = real
            out[block:, :] = imag


def base_kernel(block, pairs, *refs):
    out = refs[-1]
    straight, turned = [], []
    for index in range(pairs):
        for w in refs[3 * index + 1 : 3 * index + 3]:
            rows = w.shape[0] // 2
            straight.append(w[...])
            turned.extend([w[rows:, :], -w[:rows, :]])
    straight = jnp.concatenate(straight, axis=0)
    turned = jnp.concatenate(turned, axis=0)
    for index in range(out.shape[0] // (2 * block)):
        a = jnp.concatenate([ref[index * block : (index + 1) * block, :] for ref in refs[: 3 * pairs : 3]], axis=1)
        for part, w in enumerate((straight, turned)):
            at = slice((2 * index + part) * block, (2 * index + part + 1) * block)
            term = dot(a, w)
            out[at, :] = term if len(refs) == 3 * pairs + 1 else term + refs[-2][at, :]


def lay_kernel(total, *refs):
    got, out = refs[:-1], refs[-1]
    block = total.shape[0] // 2
    for part in range(2):
        at = slice(part * block, (part + 1) * block)
        value = total[at, :]
        for term in got:
            value += term[at, :] * jnp.exp2(-term[2 * block : 2 * block + 1, :])
        out[:, part, :] = value


def from_behind(value, axis, steps):
    count = lax.axis_size(axis)
    first, last = (max(0, -steps), min(count, count - steps))
    return lax.ppermute(value, axis, [(source, source + steps) for source in range(first, last)])


def any_shards(green, direction, partners, counts):
    tile_dev, kmax = partners.shape
    rows = green.shape[1]
    half = green.shape[2]
    tile = rows // tile_dev
    real_part = jnp.dot(green[0], direction[0], preferred_element_type=jnp.float32) - jnp.dot(
        green[1], direction[1], preferred_element_type=jnp.float32
    )
    imag_part = jnp.dot(green[0], direction[1], preferred_element_type=jnp.float32) + jnp.dot(
        green[1], direction[0], preferred_element_type=jnp.float32
    )
    images = lax.psum_scatter(
        jnp.stack([real_part, imag_part]), "src", scatter_dimension=2, tiled=True
    ).astype(jnp.bfloat16)
    tiles = green.reshape(2, tile_dev, tile, half)
    count_tile = lax.axis_size("tile")
    reach = min(BAND_DEV, count_tile - 1)
    empty = jnp.zeros_like(tiles)
    offsets = [offset for offset in range(-reach, reach + 1) if offset != 0]
    moved = [from_behind(tiles, "tile", -offset) for offset in offsets]
    nearby = dict(zip(offsets, moved))
    nearby[0] = tiles
    window = jnp.concatenate(
        [nearby.get(offset, empty) for offset in range(-BAND_DEV, BAND_DEV + 1)], axis=1
    )
    first_tile = (lax.axis_index("tile") - BAND_DEV) * tile_dev
    local_index = partners - first_tile
    live = (jnp.arange(kmax, dtype=jnp.int32)[None, :] < counts[:, None]).astype(jnp.float32)
    across = (((1,), (1,)), ((), ()))
    stacks = []
    pieces = []
    for row in range(tile_dev):
        stack = jnp.take(window, local_index[row], axis=1).reshape(2, kmax * tile, half)
        stacks.append(stack)
        image_row = images[:, row * tile : (row + 1) * tile]
        couple_real = lax.dot_general(
            image_row[0], stack[0], across, preferred_element_type=jnp.float32
        ) + lax.dot_general(image_row[1], stack[1], across, preferred_element_type=jnp.float32)
        couple_imag = lax.dot_general(
            image_row[1], stack[0], across, preferred_element_type=jnp.float32
        ) - lax.dot_general(image_row[0], stack[1], across, preferred_element_type=jnp.float32)
        blocks = jnp.stack([couple_real, couple_imag]).reshape(2, tile, kmax, tile)
        pieces.append(blocks * live[row][None, None, :, None])
    partial_blocks = jnp.stack(pieces, axis=1)
    coupling = lax.psum(partial_blocks, "src").astype(jnp.bfloat16)
    weight_rows = []
    for row in range(tile_dev):
        stack = stacks[row]
        flat = coupling[:, row].reshape(2, tile, kmax * tile)
        weight_real = jnp.dot(flat[0], stack[0], preferred_element_type=jnp.float32) - jnp.dot(
            flat[1], stack[1], preferred_element_type=jnp.float32
        )
        weight_imag = jnp.dot(flat[0], stack[1], preferred_element_type=jnp.float32) + jnp.dot(
            flat[1], stack[0], preferred_element_type=jnp.float32
        )
        weight_rows.append(jnp.stack([weight_real, weight_imag]))
    weighted = jnp.concatenate(weight_rows, axis=1).astype(jnp.bfloat16)
    full_rows = lax.all_gather(green, "src", axis=2, tiled=True)
    down = (((0,), (0,)), ((), ()))
    out_real = lax.dot_general(
        full_rows[0], weighted[0], down, preferred_element_type=jnp.float32
    ) + lax.dot_general(full_rows[1], weighted[1], down, preferred_element_type=jnp.float32)
    out_imag = lax.dot_general(
        full_rows[0], weighted[1], down, preferred_element_type=jnp.float32
    ) - lax.dot_general(full_rows[1], weighted[0], down, preferred_element_type=jnp.float32)
    return lax.psum_scatter(
        jnp.stack([out_real, out_imag], axis=1), "tile", scatter_dimension=0, tiled=True
    )


def four_shards(green, direction, partners, counts):
    shape = partners.shape
    rows, half = green.shape[1:]
    core_rows = rows // 2
    block = 2 * half // lax.axis_size("tile")
    turns = [2, 3, 1, 0]

    def other_side(index):
        return index ^ 1

    def even_pair(index):
        return index ^ 2

    def odd_pair(index):
        return index ^ 6 if inner(index) else -1

    def inner(index):
        return index // 2 in (1, 2)

    def early(index):
        return inner(index) and index // 2 % 2 != index % 2

    def second_mine(plane, side, core=None):
        return jnp.where(plane < 2, side, 1 - side) == 1

    def first_mine(plane, side, core=None):
        return jnp.where(plane < 2, side, 1 - side) == 0

    def always(plane, side, core=None):
        return plane >= 0

    def of_own(plane, side):
        return 2 * plane + side

    def of_mate(plane, side):
        return 2 * plane + 1 - side

    def of_pair(plane, side):
        return 2 * (plane ^ 1) + side

    def of_next(plane, side):
        return 2 * (3 - plane) + side

    def of_across(plane, side):
        return 2 * (plane ^ 1) + 1 - side

    def of_near(plane, side):
        return 2 * (3 - plane) + 1 - side

    def of_far(plane, side):
        return jnp.where(plane < 2, 6, 1)

    direction_other = cores(direction)
    green_other = cores(green)
    mate = move(green, other_side)
    pair = move(green, even_pair)
    beyond = move(green, odd_pair)
    late_partners, green_other = lax.optimization_barrier((partners, green_other))
    table = pl.pallas_call(
        table_kernel,
        out_shape=jax.ShapeDtypeStruct((TABLE_ROWS, 128), F32),
        in_specs=[SMEM, SMEM],
        out_specs=VMEM,
        compiler_params=PARAMS,
    )(late_partners, counts)
    table_mate = move(table, other_side)
    late_green, late_direction, table = lax.optimization_barrier((green, direction, table))
    green_here, direction_here = stage(late_green, late_direction)
    late_table, direction_other = lax.optimization_barrier((table, direction_other))
    table_pair = move(late_table, even_pair)
    mate, direction_other, green_other, table_mate, green, direction = lax.optimization_barrier(
        (mate, direction_other, green_other, table_mate, green_here, direction_here)
    )
    pair, beyond, table_pair = lax.optimization_barrier((pair, beyond, table_pair))

    mate_sent = pl.pallas_call(
        extend_kernel,
        out_shape=jax.ShapeDtypeStruct((2, rows + TABLE_ROWS, half), BF16),
        in_specs=[VMEM, VMEM],
        out_specs=VMEM,
        compiler_params=PARAMS,
    )(mate, table_mate)
    across = move(mate_sent, even_pair)
    ahead = move(pair, lambda i: odd_pair(i) if inner(i) and not early(i) else -1)
    near = move(beyond, other_side)
    mate_other = cores(mate)
    pair_other = cores(pair)
    beyond_other = cores(beyond)

    first_rows = pick(
        (first_mine, green, mate, None),
        (first_mine, green_other, mate_other, None),
        (second_mine, green, mate, None),
        (second_mine, green_other, mate_other, None),
    )
    row_groups = [first_rows[:2], first_rows[2:], (pair, pair_other)]
    left = images_call(core_rows, row_groups, direction, direction_other)
    columns = columns_call(turns, block, core_rows, row_groups)

    sampled = sampled_call(
        shape,
        [(first_mine, table, table_mate), (second_mine, table, table_mate), (always, table_pair, table_pair)],
    )
    first_blocks = [
        (of_own, [green], [green_other]),
        (of_mate, [mate], [mate_other]),
        (of_pair, [pair], [pair_other]),
        (of_next, [beyond], [beyond_other]),
    ]
    sums = window_call(sampled, shape, rows, left, 0, 3, first_blocks, None, (), apart=True)
    across, ahead, sums, columns = lax.optimization_barrier((across, ahead, sums, columns))

    far_real, far_imag = pick((always, across, across, 0), (always, ahead, ahead, 1), rows=rows)
    far_real = move(far_real, lambda i: odd_pair(i) if early(i) else -1)
    far_imag = move(far_imag, lambda i: other_side(i) if early(i) else -1)
    across_other = cores(across)
    last_row = (across, across_other)
    across_block = (of_across, [across], [across_other])
    sums = window_call(
        sampled, shape, rows, left, 0, 3, [across_block, (of_near, [near], [cores(near)])], sums, (0, 2)
    )
    last_left = images_call(core_rows, [last_row], direction, direction_other)
    last_sampled = sampled_call(shape, [(always, across, across)])
    last_sums = window_call(
        last_sampled, shape, rows, last_left, 0, 1, [*first_blocks, across_block], None, (0,)
    )
    (last_columns,) = columns_call(turns, block, core_rows, [last_row])
    def share(*operands):
        pairs = len(operands) // 3
        return pl.pallas_call(
            functools.partial(base_kernel, block, pairs),
            out_shape=jax.ShapeDtypeStruct((2 * len(turns) * block, half), F32),
            in_specs=[VMEM] * len(operands),
            out_specs=VMEM,
            compiler_params=PARAMS,
        )(*operands)

    base = share(columns[0], sums[0], cores(sums[1]), columns[2], sums[4], cores(sums[5]))
    ahead_other = cores(ahead)
    far_real, far_imag, sums, last_sums = lax.optimization_barrier((far_real, far_imag, sums, last_sums))
    sums, base = lax.optimization_barrier((sums, base))
    weighted_other, couples = window_call(
        sampled,
        shape,
        rows,
        left,
        1,
        1,
        [(of_far, [ahead, far_real, far_imag], [ahead_other, cores(far_real), cores(far_imag)])],
        sums[3:4],
        (0,),
        (1,),
    )
    weighted_other = cores(weighted_other)
    weighted = pl.pallas_call(
        finish_kernel,
        out_shape=jax.ShapeDtypeStruct((rows, half), BF16),
        in_specs=[VMEM] * 5,
        out_specs=VMEM,
        compiler_params=PARAMS,
    )(couples, ahead, far_real, far_imag, sums[2])
    last_base = share(last_columns, last_sums[0], cores(last_sums[1]), base)
    operands = [columns[1], weighted, weighted_other, last_base]

    def terms(first, turns):
        pads = [PAD_ROWS if turn else 0 for turn in turns]
        return pl.pallas_call(
            functools.partial(outer_kernel, first, block, 1, 1),
            out_shape=tuple(jax.ShapeDtypeStruct((2 * block + pad, half), F32) for pad in pads),
            in_specs=[VMEM] * len(operands),
            out_specs=(VMEM,) * len(turns),
            compiler_params=PARAMS,
        )(*operands)

    def send(term, turn):
        return move(term.astype(jnp.float16), lambda i: i ^ 2 * turn if inner(i) or turn == 1 else -1)

    (first,) = terms(0, turns[:1])
    operands[0], first = lax.optimization_barrier((operands[0], first))
    sent = [send(first, turns[0])]
    sent += [send(term, turn) for term, turn in zip(terms(1, turns[1:-1]), turns[1:-1])]
    (total,) = terms(len(turns) - 1, turns[-1:])
    for got in (sent[0], sent[2]):
        got = got.astype(F32)
        total = total + got[: 2 * block] * jnp.exp2(-got[2 * block : 2 * block + 1])
    args = [total, sent[1].astype(F32)]
    return pl.pallas_call(
        lay_kernel,
        out_shape=jax.ShapeDtypeStruct((block, 2, half), F32),
        in_specs=[VMEM] * len(args),
        out_specs=VMEM,
        compiler_params=PARAMS,
    )(*args)


def solution(mesh):
    in_specs = (
        P(None, ("freq", "tile"), "src"),
        P(None, ("freq", "src"), None),
        P(("freq", "tile"), None),
        P(("freq", "tile")),
    )
    out_specs = P(("freq", "tile"), None, "src")
    shards = four_shards if mesh.shape["tile"] == 8 else any_shards
    return jax.shard_map(shards, mesh=mesh, in_specs=in_specs, out_specs=out_specs, check_vma=False)
```
